32 devices in a mesh: gx: 4 (over z), gy: 4 (over y, x), comp: 2 (over core).
Axes of the slice: x: 2, y: 2, z: 4, core: 2. Of those that a mesh axis runs over, the one named last changes fastest.
Arguments:
- spectrum: bfloat16 [64, 512, 1024], P('gx', 'gy', 'comp'), may hold values from -6 to 6
- sea_mask: int32 [64, 512], P('gx', 'gy'), may hold values 0 or 1
- courant: float32 [2, 1024], P(None, 'comp'), may hold values from -0.45 to 0.45
- interaction: bfloat16 [1024, 1024], replicated, may hold values from -0.1875 to 0.1875
- stokes_proj: bfloat16 [2, 1024, 64], replicated, may hold values from -0.1875 to 0.1875
- currents: float32 [2, 64, 64, 512], P(None, 'comp', 'gx', 'gy'), may hold values from -6 to 6
- level_drag: float32 [64], P('comp'), may hold values from 0.05 to 0.5
Outputs:
- wave_out: bfloat16 [64, 512, 1024], P('gx', 'gy', 'comp')
- currents_out: float32 [2, 64, 64, 512], P(None, 'comp', 'gx', 'gy')
The draws below stay inside these ranges and needn't reach their ends.
All inputs are finite; a program needn't handle non-finite values. No bound on the sum of `sea_mask` on one device may be relied on, other than what follows from the above.
Results may differ from the reference program's by a relative error of at most 0.0049.
Values may be sent and summed in bfloat16 or wider, within the bound.
No kernel may reach another device: no remote copies, remote signals or barrier semaphores. Data moves between devices by JAX's collectives and lax.ppermute only.
A program may use at most 64 MiB of HBM per device.

```python
import math
import jax
import jax.numpy as jnp
from jax import lax

K = 1024
LEV = 64
SUBSTEPS = 3
NX = 64
NY = 512


def plant(drawn, rng, low, top_value):
    longest = drawn.shape.index(max(drawn.shape))
    spots = []
    for shift in (0, 1):
        where = [jax.random.randint(jax.random.fold_in(rng, axis), (), 0, length) for axis, length in enumerate(drawn.shape)]
        where[longest] = (where[longest] + shift) % drawn.shape[longest]
        spots.append(tuple(where))
    return drawn.at[spots[0]].set(low).at[spots[1]].set(top_value)


def steps_of(stream_key, shape, pieces, least, high):
    loudness = 1.0
    for position, shards_of in pieces:
        heights = jax.random.uniform(jax.random.fold_in(jax.random.fold_in(stream_key, 6), position), (shards_of,), jnp.float32, least / len(pieces), high / len(pieces))
        loudness = loudness * jnp.repeat(jnp.exp(heights), shape[position] // shards_of).reshape((-1,) + (1,) * (len(shape) - 1 - position))
    return loudness


def noise(own_key, shape, deviation, most, pieces=(), kind=jnp.bfloat16):
    level = steps_of(own_key, shape, pieces, -0.22, 0.18) if pieces else 1.0
    result = jax.random.normal(own_key, shape, jnp.float32) * deviation * level
    return jnp.minimum(jnp.maximum(result, -most), most).astype(kind)


def setup_inputs(seed: int = 0) -> dict:
    key_of = jax.random.split(jax.random.key(seed), 8)
    return {
        "spectrum": noise(key_of[0], (NX, NY, K), 1.0, 6.0, ((0, 4), (1, 4), (2, 2))),
        "sea_mask": plant((jax.random.randint(key_of[1], (NX, NY), 0, 4) < 3).astype(jnp.int32), jax.random.fold_in(key_of[1], 1), 0, 1),
        "courant": jnp.clip(jax.random.uniform(key_of[2], (2, K), jnp.float32, -0.45, 0.45) * steps_of(key_of[2], (2, K), ((1, 2),), -0.4, 0.0), -0.45, 0.45),
        "interaction": noise(key_of[3], (K, K), K ** -0.5, 0.1875),
        "stokes_proj": noise(key_of[4], (2, K, LEV), K ** -0.5, 0.1875),
        "currents": noise(key_of[5], (2, LEV, NX, NY), 1.0, 6.0, ((1, 2), (2, 4), (3, 4)), jnp.float32),
        "level_drag": jnp.clip(jnp.exp(math.log(0.5) - 2.3025851 * jax.random.uniform(key_of[6], (LEV,), jnp.float32) ** steps_of(key_of[6], (LEV,), ((0, 2),), -0.2, 0.2)), 0.05, 0.5),
    }


time_step = 0.5
viscosity = 0.4


def upwind(centre, west_cell, east_cell, south_cell, north_cell, courant):
    cour_x = courant[0]
    cour_y = courant[1]
    return (centre - jnp.maximum(cour_x, 0.0) * (centre - west_cell)
            - jnp.minimum(cour_x, 0.0) * (east_cell - centre)
            - jnp.maximum(cour_y, 0.0) * (centre - south_cell)
            - jnp.minimum(cour_y, 0.0) * (north_cell - centre))


def substep(u_pad, v_pad, stokes_u, stokes_v, coriolis, sea_cells, level_drag):
    u_mid = u_pad[:, 1:-1, 1:-1]
    v_mid = v_pad[:, 1:-1, 1:-1]
    vorticity = 0.5 * (v_pad[:, 2:, 1:-1] - v_pad[:, :-2, 1:-1]) - 0.5 * (u_pad[:, 1:-1, 2:] - u_pad[:, 1:-1, :-2])
    lap_u = u_pad[:, 2:, 1:-1] + u_pad[:, :-2, 1:-1] + u_pad[:, 1:-1, 2:] + u_pad[:, 1:-1, :-2] - 4.0 * u_mid
    lap_v = v_pad[:, 2:, 1:-1] + v_pad[:, :-2, 1:-1] + v_pad[:, 1:-1, 2:] + v_pad[:, 1:-1, :-2] - 4.0 * v_mid
    abs_vort = coriolis + vorticity
    drag_col = level_drag[:, None, None]
    u_next = u_mid + time_step * (abs_vort * (v_mid + stokes_v) - drag_col * u_mid + viscosity * lap_u)
    v_next = v_mid + time_step * (-abs_vort * (u_mid + stokes_u) - drag_col * v_mid + viscosity * lap_v)
    return u_next * sea_cells, v_next * sea_cells


def pad_field(field):
    wrapped = jnp.concatenate([field[:, -1:], field, field[:, :1]], axis=1)
    return jnp.pad(wrapped, ((0, 0), (0, 0), (1, 1)))


def reference(spectrum, sea_mask, courant, interaction, stokes_proj, currents, level_drag):
    sea_cells = sea_mask.astype(jnp.float32)
    proj_wide = stokes_proj.astype(jnp.float32)

    def row_work(row_index):
        row_index = row_index.astype(jnp.int32)
        centre = lax.dynamic_index_in_dim(spectrum, row_index, 0, keepdims=False).astype(jnp.float32)
        west_cell = lax.dynamic_index_in_dim(spectrum, (row_index - 1) % NX, 0, keepdims=False).astype(jnp.float32)
        east_cell = lax.dynamic_index_in_dim(spectrum, (row_index + 1) % NX, 0, keepdims=False).astype(jnp.float32)
        south_cell = jnp.pad(centre, ((1, 0), (0, 0)))[:-1]
        north_cell = jnp.pad(centre, ((0, 1), (0, 0)))[1:]
        sea_col = lax.dynamic_index_in_dim(sea_cells, row_index, 0, keepdims=False)[:, None]
        advected = (upwind(centre, west_cell, east_cell, south_cell, north_cell, courant) * sea_col).astype(jnp.bfloat16)
        gain = jnp.dot(advected, interaction, preferred_element_type=jnp.float32)
        wave_row = ((advected.astype(jnp.float32) + gain) * sea_col).astype(jnp.bfloat16)
        stokes_row = jnp.einsum("yk,ckl->cly", advected.astype(jnp.float32), proj_wide)
        return wave_row, stokes_row

    wave_out, stokes_rows = lax.map(row_work, jnp.arange(NX, dtype=jnp.int32))
    stokes = jnp.transpose(stokes_rows, (1, 2, 0, 3))
    lat_index = jnp.arange(NY).astype(jnp.float32)
    coriolis = jnp.sin(jnp.pi * ((lat_index + 0.5) / NY - 0.5))[None, :]
    u_field = currents[0]
    v_field = currents[1]
    for sub_index in range(SUBSTEPS):
        u_field, v_field = substep(pad_field(u_field), pad_field(v_field), stokes[0], stokes[1], coriolis, sea_cells, level_drag)
    return wave_out, jnp.stack([u_field, v_field])
```

```python
import jax
import jax.numpy as jnp
from jax import lax
from jax.sharding import PartitionSpec as P

SUBSTEPS = 3


time_step = 0.5
viscosity = 0.4


def padded_2(block, sides, width, periodic):
    for axis, dim in sides:
        count = lax.axis_size(axis)
        forward = [(i, i + 1) for i in range(count - 1)]
        if periodic:
            forward.append((count - 1, 0))
        backward = [(target, source) for source, target in forward]
        low = lax.ppermute(
            lax.slice_in_dim(block, block.shape[dim] - width, None, axis=dim), axis, forward
        )
        high = lax.ppermute(lax.slice_in_dim(block, 0, width, axis=dim), axis, backward)
        block = jnp.concatenate([low, block, high], axis=dim)
    return block


def upwind(centre, west_cell, east_cell, south_cell, north_cell, courant):
    cour_x = courant[0]
    cour_y = courant[1]
    return (
        centre
        - jnp.maximum(cour_x, 0.0) * (centre - west_cell)
        - jnp.minimum(cour_x, 0.0) * (east_cell - centre)
        - jnp.maximum(cour_y, 0.0) * (centre - south_cell)
        - jnp.minimum(cour_y, 0.0) * (north_cell - centre)
    )


def substep(u_pad, v_pad, stokes_u, stokes_v, coriolis, sea_cells, level_drag):
    u_mid = u_pad[:, 1:-1, 1:-1]
    v_mid = v_pad[:, 1:-1, 1:-1]
    vorticity = 0.5 * (v_pad[:, 2:, 1:-1] - v_pad[:, :-2, 1:-1]) - 0.5 * (
        u_pad[:, 1:-1, 2:] - u_pad[:, 1:-1, :-2]
    )
    lap_u = (
        u_pad[:, 2:, 1:-1]
        + u_pad[:, :-2, 1:-1]
        + u_pad[:, 1:-1, 2:]
        + u_pad[:, 1:-1, :-2]
        - 4.0 * u_mid
    )
    lap_v = (
        v_pad[:, 2:, 1:-1]
        + v_pad[:, :-2, 1:-1]
        + v_pad[:, 1:-1, 2:]
        + v_pad[:, 1:-1, :-2]
        - 4.0 * v_mid
    )
    abs_vort = coriolis + vorticity
    drag_col = level_drag[:, None, None]
    u_next = u_mid + time_step * (
        abs_vort * (v_mid + stokes_v) - drag_col * u_mid + viscosity * lap_u
    )
    v_next = v_mid + time_step * (
        -abs_vort * (u_mid + stokes_u) - drag_col * v_mid + viscosity * lap_v
    )
    return (u_next * sea_cells, v_next * sea_cells)


def crop_cells(field, margin):
    return field[..., margin : field.shape[-2] - margin, margin : field.shape[-1] - margin]


def lat_coriolis(cells_y, margin):
    ny_total = lax.axis_size("gy") * cells_y
    lat_index = lax.axis_index("gy") * cells_y + jnp.arange(-margin, cells_y + margin)
    return jnp.sin(jnp.pi * ((lat_index.astype(jnp.float32) + 0.5) / ny_total - 0.5))[None, :]


def local(spectrum, sea_mask, courant, interaction, stokes_proj, currents, level_drag):
    sea_cells = sea_mask.astype(jnp.float32)
    lon_padded = padded_2(spectrum, (("gx", 0),), 1, True)
    padded = padded_2(lon_padded, (("gy", 1),), 1, False)
    centre = padded[1:-1, 1:-1].astype(jnp.float32)
    west_cell = padded[:-2, 1:-1].astype(jnp.float32)
    east_cell = padded[2:, 1:-1].astype(jnp.float32)
    south_cell = padded[1:-1, :-2].astype(jnp.float32)
    north_cell = padded[1:-1, 2:].astype(jnp.float32)
    advected = (
        upwind(centre, west_cell, east_cell, south_cell, north_cell, courant)
        * sea_cells[:, :, None]
    ).astype(jnp.bfloat16)
    cells_x, cells_y, bins_own = advected.shape
    lev_own = currents.shape[1]
    core_index = lax.axis_index("comp")
    w_cols = lax.dynamic_slice_in_dim(interaction, core_index * bins_own, bins_own, 1)
    proj_own = lax.dynamic_slice_in_dim(stokes_proj, core_index * lev_own, lev_own, 2)
    cores = lax.axis_size("comp")
    gain_sum = 0.0
    stokes_sum = 0.0
    block = advected
    for hop in range(cores):
        owner = lax.rem(core_index + cores - hop, cores) * bins_own
        rows = lax.dynamic_slice_in_dim(w_cols, owner, bins_own, 0)
        proj_rows = lax.dynamic_slice_in_dim(proj_own, owner, bins_own, 1)
        following = block
        if hop + 1 < cores:
            following = lax.ppermute(block, "comp", [(i, (i + 1) % cores) for i in range(cores)])
        gain_sum = gain_sum + jnp.dot(
            block.reshape(-1, bins_own), rows, preferred_element_type=jnp.float32
        )
        stokes_sum = stokes_sum + jnp.einsum(
            "xyk,ckl->clxy", block, proj_rows, preferred_element_type=jnp.float32
        )
        block = following
    wave_out = (
        (advected.astype(jnp.float32) + gain_sum.reshape(cells_x, cells_y, bins_own))
        * sea_cells[:, :, None]
    ).astype(jnp.bfloat16)
    stacked = jnp.concatenate(
        [
            currents.reshape(2 * lev_own, cells_x, cells_y),
            stokes_sum.reshape(2 * lev_own, cells_x, cells_y),
            sea_cells[None],
        ],
        0,
    )
    lon_state = padded_2(stacked, (("gx", 1),), SUBSTEPS, True)
    state_ext = padded_2(lon_state, (("gy", 2),), SUBSTEPS, False)
    flow = state_ext[: 2 * lev_own]
    stokes_ext = state_ext[2 * lev_own : 4 * lev_own]
    mask_ext = state_ext[4 * lev_own]
    coriolis_ext = lat_coriolis(cells_y, SUBSTEPS)
    for sub_index in range(SUBSTEPS):
        inner = sub_index + 1
        cor_now = coriolis_ext[:, inner : coriolis_ext.shape[1] - inner]
        u_next, v_next = substep(
            flow[:lev_own],
            flow[lev_own:],
            crop_cells(stokes_ext[:lev_own], inner),
            crop_cells(stokes_ext[lev_own:], inner),
            cor_now,
            crop_cells(mask_ext, inner),
            level_drag,
        )
        flow = jnp.concatenate([u_next, v_next], 0)
    currents_out = flow.reshape(2, lev_own, cells_x, cells_y)
    return (wave_out, currents_out)


def solution(mesh):
    in_specs = (
        P("gx", "gy", "comp"),
        P("gx", "gy"),
        P(None, "comp"),
        P(),
        P(),
        P(None, "comp", "gx", "gy"),
        P("comp"),
    )
    out_specs = (P("gx", "gy", "comp"), P(None, "comp", "gx", "gy"))
    return jax.shard_map(local, mesh=mesh, in_specs=in_specs, out_specs=out_specs, check_vma=False)
```

```python
import functools

import jax
import jax.numpy as jnp
from jax import lax
from jax.experimental import pallas as pl
from jax.experimental.pallas import tpu as pltpu
from jax.sharding import PartitionSpec as P

SUBSTEPS = 3

time_step = 0.5
viscosity = 0.4

F32 = jnp.float32
BF16 = jnp.bfloat16
MIB = 1 << 20
EDGE = 3
PARTS = 5


def shifts(axis, periodic):
    count = lax.axis_size(axis)
    forward = [(i, i + 1) for i in range(count - 1)]
    if periodic:
        forward.append((count - 1, 0))
    return forward, [(target, source) for source, target in forward]


def diagonal(step_x, step_y):
    size_x, size_y = lax.axis_size("gx"), lax.axis_size("gy")
    return [
        (x * size_y + y, (x + step_x) % size_x * size_y + y + step_y)
        for x in range(size_x)
        for y in range(size_y)
        if 0 <= y + step_y < size_y
    ]


def lane_of(rows, width):
    return lax.broadcasted_iota(jnp.int32, (rows, width), 1)


def between(lane, low, high):
    return (lane >= low) & (lane < high)


def project_kernel(
    f_own, f_oth, wt_own, wt_oth, cur,
    s_main, s_aux, msg_e, msg_w, msg_n, msg_s, msg_ne, msg_nw, msg_se, msg_sw,
    proj,
):
    cells_x, fields, width = cur.shape
    chans = s_main.shape[1]
    stride = width // (cells_x + 2)
    half = width // 2
    contract = (((1,), (1,)), ((), ()))
    for pair in range(cells_x // 2):
        cells = pl.ds(pair * 2 * width, 2 * width)
        both = lax.dot_general(wt_own[...], f_own[cells, :], contract, preferred_element_type=F32)
        both += lax.dot_general(wt_oth[...], f_oth[cells, :], contract, preferred_element_type=F32)
        proj[2 * pair] = both[:, :width]
        proj[2 * pair + 1] = both[:, width:]

    lane = lane_of(chans, width)
    lane_f = lane_of(fields, width)

    def part(x, which):
        return proj[x, which * chans : (which + 1) * chans, :]

    pack_n = pack_s = jnp.zeros((chans, width), F32)
    cur_n = cur_s = jnp.zeros((fields, width), F32)
    for x in range(-1, cells_x + 1):
        start = stride * (x + 1)
        main = jnp.zeros((chans, width), F32)
        aux = jnp.zeros((chans, width), F32)
        if 0 <= x < cells_x:
            south = pltpu.roll(part(x, 3), 1, 1)
            north = pltpu.roll(part(x, 4), width - 1, 1)
            main = part(x, 0) + jnp.where(lane > 0, south, 0.0) + jnp.where(lane < width - 1, north, 0.0)
            aux = jnp.where(lane == 0, south, jnp.where(lane == width - 1, north, 0.0))
            s_aux[x] = aux
        if x >= 1:
            main += part(x - 1, 1)
        if x <= cells_x - 2:
            main += part(x + 1, 2)
        s_main[x + 1] = main
        window = between(lane, start, start + 4)
        ring_n = pltpu.roll(jnp.where(lane == 0, aux, main), (3 + start) % width, 1)
        ring_s = pltpu.roll(jnp.where(lane == width - 1, aux, main), (1 + start) % width, 1)
        pack_n = jnp.where(window, ring_n, pack_n)
        pack_s = jnp.where(window, ring_s, pack_s)
        if 0 <= x < cells_x:
            row = cur[x]
            cur_n = jnp.where(
                between(lane_f, start, start + 3), pltpu.roll(row, (3 + start) % width, 1), cur_n
            )
            cur_s = jnp.where(
                between(lane_f, start + 1, start + 4), pltpu.roll(row, (1 + start) % width, 1), cur_s
            )
    for msg, pack, cur_pack in ((msg_n, pack_n, cur_n), (msg_s, pack_s, cur_s)):
        msg[:chans] = pack.astype(BF16)
        msg[chans:] = cur_pack.astype(BF16)
    corners = (
        (msg_ne, pack_n, cur_n, cells_x - 1, cells_x - 2),
        (msg_nw, pack_n, cur_n, 0, 1),
        (msg_se, pack_s, cur_s, cells_x - 1, cells_x - 2),
        (msg_sw, pack_s, cur_s, 0, 1),
    )
    for msg, pack, cur_pack, first, first_cur in corners:
        kept = jnp.where(lane < EDGE * stride, pltpu.roll(pack, (-stride * first) % width, 1), 0.0)
        cur_kept = jnp.where(
            between(lane_f, half, half + EDGE * stride),
            pltpu.roll(cur_pack, (half - stride * first_cur) % width, 1),
            0.0,
        )
        msg[:chans] = (kept + cur_kept[:chans]).astype(BF16)
        msg[chans:] = cur_kept[chans:].astype(BF16)
    sides = ((msg_e, cells_x - 1, cells_x - 1, cells_x - EDGE), (msg_w, 0, 0, 0))
    for msg, first, aux_row, first_cur in sides:
        for i in range(EDGE):
            msg[i * chans : (i + 1) * chans] = s_main[first + i].astype(BF16)
            base = (EDGE + 1) * chans + i * fields
            msg[base : base + fields] = cur[first_cur + i].astype(BF16)
        msg[EDGE * chans : (EDGE + 1) * chans] = s_aux[aux_row].astype(BF16)


def momentum_kernel(
    s_main, s_aux, cur, from_w, from_e, from_s, from_n, from_sw, from_se, from_nw, from_ne, drag, cor,
    out,
    flow_a, flow_b, stokes, result, sem,
):
    cells_x, fields, width = cur.shape
    chans = s_main.shape[1]
    levels = chans // 2
    stride = width // (cells_x + 2)
    half = width // 2
    lane = lane_of(chans, width)
    lane_f = lane_of(fields, width)

    def southern(tile, start):
        return pltpu.roll(tile, (-start - 3) % width, 1)

    def northern(tile, start):
        return pltpu.roll(tile, (-start - 1) % width, 1)

    cur_base = (EDGE + 1) * chans
    cur_s, cur_n = from_s[chans:].astype(F32), from_n[chans:].astype(F32)
    for x in range(-SUBSTEPS, cells_x + SUBSTEPS):
        if x < 0:
            at = x + SUBSTEPS
            main = from_w[cur_base + at * fields : cur_base + (at + 1) * fields].astype(F32)
            low = southern(from_sw[...].astype(F32), half + stride * at)
            high = northern(from_nw[...].astype(F32), half + stride * at)
        elif x < cells_x:
            main = cur[x]
            low = southern(cur_s, stride * (x + 1))
            high = northern(cur_n, stride * (x + 1))
        else:
            at = x - cells_x
            main = from_e[cur_base + at * fields : cur_base + (at + 1) * fields].astype(F32)
            low = southern(from_se[...].astype(F32), half + stride * at)
            high = northern(from_ne[...].astype(F32), half + stride * at)
        flow_a[x + SUBSTEPS, :, :width] = main
        flow_a[x + SUBSTEPS, :, width:] = jnp.where(
            lane_f >= width - 3, low, jnp.where(lane_f < 3, high, 0.0)
        )

    pack_s, pack_n = from_s[:chans].astype(F32), from_n[:chans].astype(F32)
    margin = SUBSTEPS - 1
    for x in range(-margin, cells_x + margin):
        main = aux = low = high = jnp.zeros((chans, width), F32)
        if -1 <= x <= cells_x:
            main += s_main[x + 1]
            low += southern(pack_s, stride * (x + 1))
            high += northern(pack_n, stride * (x + 1))
        if 0 <= x < cells_x:
            aux += s_aux[x]
        for message, message_s, message_n, first, spill in (
            (from_w, from_sw, from_nw, -2, -1),
            (from_e, from_se, from_ne, cells_x - 1, cells_x),
        ):
            at = x - first
            if 0 <= at < EDGE:
                main += message[at * chans : (at + 1) * chans].astype(F32)
                low += southern(message_s[:chans].astype(F32), stride * at)
                high += northern(message_n[:chans].astype(F32), stride * at)
            if x == spill:
                aux += message[EDGE * chans : (EDGE + 1) * chans].astype(F32)
        main += jnp.where(lane == 0, low, 0.0) + jnp.where(lane == width - 1, high, 0.0)
        aux += jnp.where(lane >= width - 3, low, jnp.where(lane < 3, high, 0.0))
        sea = flow_a[x + SUBSTEPS, chans : chans + 1, :]
        stokes[x + margin, :, :width] = main * sea[:, :width]
        stokes[x + margin, :, width:] = aux * sea[:, width:]

    half_cor = time_step * cor[...]
    keep = 1.0 - 4.0 * time_step * viscosity - time_step * drag[...]
    ring = 2 * width
    source, target = flow_a, flow_b
    for step in range(SUBSTEPS):
        margin = SUBSTEPS - 1 - step
        last = step == SUBSTEPS - 1
        for x in range(-margin, cells_x + margin):
            at = x + SUBSTEPS
            u, v = source[at, :levels], source[at, levels:chans]
            u_w, v_w = source[at - 1, :levels], source[at - 1, levels:chans]
            u_e, v_e = source[at + 1, :levels], source[at + 1, levels:chans]
            u_s, v_s = pltpu.roll(u, 1, 1), pltpu.roll(v, 1, 1)
            u_n, v_n = pltpu.roll(u, ring - 1, 1), pltpu.roll(v, ring - 1, 1)
            drift = stokes[x + SUBSTEPS - 1]
            spin = half_cor + 0.5 * time_step * ((v_e - v_w) - (u_n - u_s))
            sea = flow_a[at, chans : chans + 1, :]
            u_new = keep * u + spin * (v + drift[levels:])
            v_new = keep * v - spin * (u + drift[:levels])
            u_new = sea * (u_new + time_step * viscosity * ((u_e + u_w) + (u_n + u_s)))
            v_new = sea * (v_new + time_step * viscosity * ((v_e + v_w) + (v_n + v_s)))
            if last:
                result[x, :levels] = u_new[:, :width]
                result[x, levels:] = v_new[:, :width]
                for c in range(2):
                    pltpu.make_async_copy(
                        result.at[x, pl.ds(c * levels, levels), :], out.at[c, :, x, :], sem.at[c, x]
                    ).start()
            else:
                target[at, :levels] = u_new
                target[at, levels:chans] = v_new
        source, target = target, source
    for x in range(cells_x):
        for c in range(2):
            pltpu.make_async_copy(
                result.at[x, pl.ds(c * levels, levels), :], out.at[c, :, x, :], sem.at[c, x]
            ).wait()


def advect(centre, west, east, south, north, coef, sea, adv, row, col):
    width, bins = centre.shape
    chunk = 128
    at_y = lax.broadcasted_iota(jnp.int32, (width, chunk), 0)
    for j in range(bins // chunk):
        cols = slice(j * chunk, (j + 1) * chunk)
        mid = centre[:, cols].astype(F32)
        low = jnp.where(at_y == 0, south[:, cols].astype(F32), pltpu.roll(mid, 1, 0))
        high = jnp.where(at_y == width - 1, north[:, cols].astype(F32), pltpu.roll(mid, width - 1, 0))
        beside = jnp.where(coef[3:4, cols] > 0, west[:, cols].astype(F32), east[:, cols].astype(F32))
        along = jnp.where(coef[4:5, cols] > 0, low, high)
        value = coef[0:1, cols] * mid + coef[1:2, cols] * beside + coef[2:3, cols] * along
        adv[row : row + width, col + j * chunk : col + (j + 1) * chunk] = (value * sea).astype(BF16)


def sea_column(mask, x, width):
    return jnp.transpose(jnp.broadcast_to(mask[pl.ds(x, 1), :], (128, width)))


def finish(adv, inter_own, inter_oth, seas, out_slot):
    bins = inter_own.shape[1]
    width = seas[0].shape[0]
    gain = jnp.dot(adv[:, :bins], inter_own[...], preferred_element_type=F32)
    gain += jnp.dot(adv[:, bins:], inter_oth[...], preferred_element_type=F32)
    for i, sea in enumerate(seas):
        rows = slice(i * width, (i + 1) * width)
        for j in range(bins // 128):
            cols = slice(j * 128, (j + 1) * 128)
            total = adv[rows, cols].astype(F32) + gain[rows, cols]
            out_slot[i, :, cols] = (total * sea).astype(BF16)


def interior_kernel(
    f_own, f_oth, south_own, south_oth, north_own, north_oth, mask, coef_own, coef_oth, inter_own, inter_oth,
    out,
    adv, slots, out_sem,
):
    cells_x, width, bins = f_own.shape
    pairs = cells_x // 2 - 1

    def copy_out(pair):
        slot = lax.rem(pair, 2)
        return pltpu.make_async_copy(
            slots.at[slot], out.at[pl.ds(1 + 2 * pair, 2)], out_sem.at[slot]
        )

    def body(pair, carry):
        seas = []
        for i in range(2):
            x = 1 + 2 * pair + i
            sea = sea_column(mask, x, width)
            seas.append(sea)
            for f, south, north, coef, col in (
                (f_own, south_own, north_own, coef_own, 0),
                (f_oth, south_oth, north_oth, coef_oth, bins),
            ):
                advect(
                    f.at[x], f.at[x - 1], f.at[x + 1], south.at[x], north.at[x],
                    coef, sea, adv, i * width, col,
                )

        @pl.when(pair >= 2)
        def _():
            copy_out(pair - 2).wait()

        finish(adv, inter_own, inter_oth, seas, slots.at[lax.rem(pair, 2)])
        copy_out(pair).start()
        return carry

    lax.fori_loop(0, pairs, body, 0)
    for pair in range(max(pairs - 2, 0), pairs):
        copy_out(pair).wait()


def edge_kernel(
    f_own, f_oth, west_own, west_oth, east_own, east_oth, south_own, south_oth, north_own, north_oth,
    mask, coef_own, coef_oth, inter_own, inter_oth, wave,
    out,
    rows_own, rows_oth, adv, slots, in_sem, out_sem,
):
    del wave
    cells_x, width, bins = f_own.shape
    picked = ((0, 0), (cells_x - 2, 2))
    copies = [
        pltpu.make_async_copy(f.at[pl.ds(first, 2)], rows.at[pl.ds(at, 2)], in_sem.at[n, i])
        for n, (f, rows) in enumerate(((f_own, rows_own), (f_oth, rows_oth)))
        for i, (first, at) in enumerate(picked)
    ]
    for copy in copies:
        copy.start()
    for copy in copies:
        copy.wait()
    seas = []
    for i, x in enumerate((0, cells_x - 1)):
        sea = sea_column(mask, x, width)
        seas.append(sea)
        for rows, west, east, south, north, coef, col in (
            (rows_own, west_own, east_own, south_own, north_own, coef_own, 0),
            (rows_oth, west_oth, east_oth, south_oth, north_oth, coef_oth, bins),
        ):
            if i == 0:
                centre, west_row, east_row = rows.at[0], west.at[0], rows.at[1]
            else:
                centre, west_row, east_row = rows.at[3], rows.at[2], east.at[0]
            advect(
                centre, west_row, east_row, south.at[x], north.at[x], coef, sea, adv, i * width, col
            )
    finish(adv, inter_own, inter_oth, seas, slots)
    writes = [
        pltpu.make_async_copy(slots.at[i], out.at[x], out_sem.at[i])
        for i, x in enumerate((0, cells_x - 1))
    ]
    for copy in writes:
        copy.start()
    for copy in writes:
        copy.wait()


def lat_coriolis(cells_y):
    ny_total = lax.axis_size("gy") * cells_y
    lane = jnp.arange(2 * cells_y)
    lane = jnp.where(lane >= cells_y + cells_y // 2, lane - 2 * cells_y, lane)
    lat_index = lax.axis_index("gy") * cells_y + lane
    return jnp.sin(jnp.pi * ((lat_index.astype(F32) + 0.5) / ny_total - 0.5))[None, :]


def coefficients(courant):
    cour_x, cour_y = courant[0], courant[1]
    rows = [
        1.0 - jnp.abs(cour_x) - jnp.abs(cour_y),
        jnp.abs(cour_x),
        jnp.abs(cour_y),
        cour_x,
        cour_y,
    ]
    return jnp.stack(rows + [jnp.zeros_like(cour_x)] * 3)


def projections(proj_rows, courant):
    cour_x, cour_y = courant[0], courant[1]
    weights = jnp.stack(
        [
            1.0 - jnp.abs(cour_x) - jnp.abs(cour_y),
            jnp.maximum(cour_x, 0.0),
            -jnp.minimum(cour_x, 0.0),
            jnp.maximum(cour_y, 0.0),
            -jnp.minimum(cour_y, 0.0),
        ]
    )
    scaled = weights[:, None, :] * proj_rows.astype(F32)[None]
    return scaled.reshape(-1, proj_rows.shape[1]).astype(BF16)


VMEM = pl.BlockSpec(memory_space=pltpu.VMEM)
ANY = pl.BlockSpec(memory_space=pl.ANY)


def params(limit):
    return pltpu.CompilerParams(vmem_limit_bytes=limit * MIB)


def local(spectrum, sea_mask, courant, interaction, stokes_proj, currents, level_drag):
    cells_x, cells_y, bins = spectrum.shape
    levels = currents.shape[1]
    chans = 2 * levels
    fields = chans + 16
    core = lax.axis_index("comp")
    swap = [(0, 1), (1, 0)]
    east, west = shifts("gx", True)
    north, south = shifts("gy", False)

    f_oth = lax.ppermute(spectrum, "comp", swap)
    courant_oth = lax.ppermute(courant, "comp", swap)
    south_own = lax.ppermute(spectrum[:, -1:], "gy", north)
    north_own = lax.ppermute(spectrum[:, :1], "gy", south)
    west_own = lax.ppermute(spectrum[-1:], "gx", east)
    east_own = lax.ppermute(spectrum[:1], "gx", west)
    south_oth = lax.ppermute(south_own, "comp", swap)
    north_oth = lax.ppermute(north_own, "comp", swap)
    west_oth = lax.ppermute(west_own, "comp", swap)
    east_oth = lax.ppermute(east_own, "comp", swap)

    sea = sea_mask.astype(F32)
    coef_own, coef_oth = coefficients(courant), coefficients(courant_oth)
    own_at, oth_at = core * bins, (1 - core) * bins
    inter_own = lax.dynamic_slice(interaction, (own_at, own_at), (bins, bins))
    inter_oth = lax.dynamic_slice(interaction, (oth_at, own_at), (bins, bins))
    proj_t = lax.dynamic_slice_in_dim(stokes_proj, core * levels, levels, 2)
    proj_t = jnp.transpose(proj_t, (0, 2, 1)).reshape(chans, -1)
    wt_own = projections(lax.dynamic_slice_in_dim(proj_t, own_at, bins, 1), courant)
    wt_oth = projections(lax.dynamic_slice_in_dim(proj_t, oth_at, bins, 1), courant_oth)
    cur = jnp.concatenate(
        [
            jnp.transpose(currents, (2, 0, 1, 3)).reshape(cells_x, chans, cells_y),
            jnp.broadcast_to(sea[:, None, :], (cells_x, 16, cells_y)),
        ],
        1,
    )

    side_rows = (EDGE + 1) * chans + EDGE * fields
    message = lambda rows: jax.ShapeDtypeStruct((rows, cells_y), BF16)
    s_main, s_aux, to_e, to_w, to_n, to_s, to_ne, to_nw, to_se, to_sw = pl.pallas_call(
        project_kernel,
        out_shape=(
            jax.ShapeDtypeStruct((cells_x + 2, chans, cells_y), F32),
            jax.ShapeDtypeStruct((cells_x, chans, cells_y), F32),
            message(side_rows),
            message(side_rows),
            message(chans + fields),
            message(chans + fields),
            *[message(fields)] * 4,
        ),
        in_specs=[VMEM] * 5,
        out_specs=(VMEM,) * 10,
        scratch_shapes=[pltpu.VMEM((cells_x, PARTS * chans, cells_y), F32)],
        compiler_params=params(20),
        cost_estimate=pl.CostEstimate(flops=3 * 10**9, bytes_accessed=8 * MIB, transcendentals=0),
        name="project",
    )(
        spectrum.reshape(-1, bins), f_oth.reshape(-1, bins), wt_own, wt_oth, cur
    )
    from_w = lax.ppermute(to_e, "gx", east)
    from_e = lax.ppermute(to_w, "gx", west)
    from_s = lax.ppermute(to_n, "gy", north)
    from_n = lax.ppermute(to_s, "gy", south)
    from_sw = lax.ppermute(to_ne, ("gx", "gy"), diagonal(1, 1))
    from_se = lax.ppermute(to_nw, ("gx", "gy"), diagonal(-1, 1))
    from_nw = lax.ppermute(to_se, ("gx", "gy"), diagonal(1, -1))
    from_ne = lax.ppermute(to_sw, ("gx", "gy"), diagonal(-1, -1))

    wave_type = jax.ShapeDtypeStruct(spectrum.shape, BF16)
    wave = pl.pallas_call(
        interior_kernel,
        out_shape=wave_type,
        in_specs=[VMEM] * 11,
        out_specs=ANY,
        scratch_shapes=[
            pltpu.VMEM((2 * cells_y, 2 * bins), BF16),
            pltpu.VMEM((2, 2, cells_y, bins), BF16),
            pltpu.SemaphoreType.DMA((2,)),
        ],
        compiler_params=params(20),
        cost_estimate=pl.CostEstimate(flops=4 * 10**9, bytes_accessed=10 * MIB, transcendentals=0),
        name="interior",
    )(
        spectrum, f_oth, south_own, south_oth, north_own, north_oth,
        sea, coef_own, coef_oth, inter_own, inter_oth,
    )
    out_type = jax.ShapeDtypeStruct(currents.shape, F32)
    currents_out = pl.pallas_call(
        momentum_kernel,
        out_shape=out_type,
        in_specs=[VMEM] * 13,
        out_specs=ANY,
        scratch_shapes=[
            pltpu.VMEM((cells_x + 2 * SUBSTEPS, fields, 2 * cells_y), F32),
            pltpu.VMEM((cells_x + 2 * SUBSTEPS, chans, 2 * cells_y), F32),
            pltpu.VMEM((cells_x + 2 * SUBSTEPS - 2, chans, 2 * cells_y), F32),
            pltpu.VMEM((cells_x, chans, cells_y), F32),
            pltpu.SemaphoreType.DMA((2, cells_x)),
        ],
        compiler_params=params(20),
        cost_estimate=pl.CostEstimate(flops=10**8, bytes_accessed=4 * MIB, transcendentals=0),
        name="momentum",
    )(
        s_main, s_aux, cur, from_w, from_e, from_s, from_n, from_sw, from_se, from_nw, from_ne,
        level_drag[:, None], lat_coriolis(cells_y),
    )
    wave_out = pl.pallas_call(
        edge_kernel,
        out_shape=wave_type,
        in_specs=[ANY] * 2 + [VMEM] * 13 + [ANY],
        out_specs=ANY,
        input_output_aliases={15: 0},
        scratch_shapes=[
            pltpu.VMEM((4, cells_y, bins), BF16),
            pltpu.VMEM((4, cells_y, bins), BF16),
            pltpu.VMEM((2 * cells_y, 2 * bins), BF16),
            pltpu.VMEM((2, cells_y, bins), BF16),
            pltpu.SemaphoreType.DMA((2, 2)),
            pltpu.SemaphoreType.DMA((2,)),
        ],
        compiler_params=params(20),
        cost_estimate=pl.CostEstimate(flops=10**9, bytes_accessed=3 * MIB, transcendentals=0),
        name="edge",
    )(
        spectrum, f_oth, west_own, west_oth, east_own, east_oth, south_own, south_oth, north_own, north_oth,
        sea, coef_own, coef_oth, inter_own, inter_oth, wave,
    )
    return (wave_out, currents_out)


def solution(mesh):
    in_specs = (
        P("gx", "gy", "comp"),
        P("gx", "gy"),
        P(None, "comp"),
        P(),
        P(),
        P(None, "comp", "gx", "gy"),
        P("comp"),
    )
    out_specs = (P("gx", "gy", "comp"), P(None, "comp", "gx", "gy"))
    return jax.shard_map(local, mesh=mesh, in_specs=in_specs, out_specs=out_specs, check_vma=False)
```

```python
import functools

import jax
import jax.numpy as jnp
from jax import lax
from jax.experimental import pallas as pl
from jax.experimental.pallas import tpu as pltpu
from jax.sharding import PartitionSpec as P

SUBSTEPS = 3

time_step = 0.5
viscosity = 0.4

F32 = jnp.float32
BF16 = jnp.bfloat16
MIB = 1 << 20
EDGE = 3
MASK_ROWS = 16
SLOT = 8
CHUNK = 128
PARTS = 5


def ring(axis):
    count = lax.axis_size(axis)
    forward = [(i, (i + 1) % count) for i in range(count)]
    return forward, [(target, source) for source, target in forward]


def pairing(axis, first):
    swaps = [(i, i + 1) for i in range(first, lax.axis_size(axis) - 1, 2)]
    return swaps + [(target, source) for source, target in swaps]


def lane_of(rows, width):
    return lax.broadcasted_iota(jnp.int32, (rows, width), 1)


def between(lane, low, high):
    return (lane >= low) & (lane < high)


def chunks_of(bins):
    return [slice(j * CHUNK, (j + 1) * CHUNK) for j in range(bins // CHUNK)]


def load_currents(currents, rows, cur, sem):
    levels = currents.shape[1]
    return [
        pltpu.make_async_copy(
            currents.at[c, :, x, :], cur.at[i, pl.ds(c * levels, levels), :], sem.at[i, c]
        )
        for i, x in enumerate(rows)
        for c in range(2)
    ]


def sea_row(mask, x, rows):
    return jnp.broadcast_to(mask[x : x + 1, :].astype(F32), (rows, mask.shape[1]))


def outgoing_kernel(spectrum, currents, mask, msg_e, msg_w, cur, sem, row_sem):
    cells_x, width, bins = spectrum.shape
    chans = cur.shape[1]
    fields = chans + MASK_ROWS
    rows = list(range(EDGE)) + list(range(cells_x - EDGE, cells_x))
    copies = load_currents(currents, rows, cur, sem)
    for side, (msg, x) in enumerate(((msg_e, cells_x - 1), (msg_w, 0))):
        for j, cols in enumerate(chunks_of(bins)):
            copies.append(
                pltpu.make_async_copy(
                    spectrum.at[x, :, cols], msg.at[pl.ds(j * width, width), :], row_sem.at[side, j]
                )
            )
    for copy in copies:
        copy.start()
    for copy in copies:
        copy.wait()
    base = bins // CHUNK * width
    for i, x in enumerate(rows):
        msg = msg_w if i < EDGE else msg_e
        at = base + i % EDGE * fields
        msg[at : at + chans] = cur[i].astype(BF16)
        msg[at + chans : at + fields] = sea_row(mask, x, MASK_ROWS).astype(BF16)


def stokes_weights(proj, courant, core, owner, weights):
    levels = proj.shape[1] // 2
    bins = courant.shape[1]
    bins_at = pl.ds(pl.multiple_of(owner * bins, bins), bins)
    cour_x, cour_y = courant[0:1, :], courant[1:2, :]
    terms = (
        1.0 - jnp.abs(cour_x) - jnp.abs(cour_y),
        jnp.maximum(cour_x, 0.0),
        -jnp.minimum(cour_x, 0.0),
        jnp.maximum(cour_y, 0.0),
        -jnp.minimum(cour_y, 0.0),
    )
    for c in range(2):
        mine = proj[c, pl.ds(pl.multiple_of(core * levels, levels), levels), bins_at].astype(F32)
        for k, term in enumerate(terms):
            row = (2 * k + c) * levels
            weights[row : row + levels] = (mine * term).astype(BF16)


def project_kernel(
    f_own, f_oth, courant_own, courant_oth, stokes_proj, currents, mask,
    s_main, s_aux, s_edge, msg_a, msg_b,
    proj, wt_own, wt_oth, cur, sem,
):
    cells_x, width, bins = f_own.shape
    chans = s_main.shape[1]
    fields = chans + MASK_ROWS
    stride = width // (cells_x + 2)
    core = lax.axis_index("comp")
    copies = load_currents(currents, range(cells_x), cur, sem)
    for copy in copies:
        copy.start()
    stokes_weights(stokes_proj, courant_own, core, core, wt_own)
    stokes_weights(stokes_proj, courant_oth, core, 1 - core, wt_oth)
    contract = (((1,), (1,)), ((), ()))
    for pair in range(cells_x // 2):
        both = 0.0
        for wt, f in ((wt_own, f_own), (wt_oth, f_oth)):
            cells = f[2 * pair : 2 * pair + 2].reshape(2 * width, bins)
            both += lax.dot_general(wt[...], cells, contract, preferred_element_type=F32)
        proj[2 * pair] = both[:, :width]
        proj[2 * pair + 1] = both[:, width:]
    for copy in copies:
        copy.wait()

    lane = lane_of(chans, width)
    lane_f = lane_of(fields, width)

    def part(x, which):
        return proj[x, which * chans : (which + 1) * chans, :]

    pack_n = pack_s = jnp.zeros((chans, width), F32)
    cur_n = cur_s = jnp.zeros((fields, width), F32)
    for x in range(-1, cells_x + 1):
        start = stride * (x + 1)
        main = jnp.zeros((chans, width), F32)
        aux = jnp.zeros((chans, width), F32)
        if 0 <= x < cells_x:
            south = pltpu.roll(part(x, 3), 1, 1)
            north = pltpu.roll(part(x, 4), width - 1, 1)
            main = part(x, 0) + jnp.where(lane > 0, south, 0.0) + jnp.where(lane < width - 1, north, 0.0)
            aux = jnp.where(lane == 0, south, jnp.where(lane == width - 1, north, 0.0))
            s_aux[x] = aux
        if x >= 1:
            main += part(x - 1, 1)
        if x <= cells_x - 2:
            main += part(x + 1, 2)
        s_main[x + 1] = main
        if x < EDGE - 1 or x > cells_x - EDGE:
            at = x + 1 if x < EDGE - 1 else x - (cells_x - 2) + EDGE
            s_edge[at, :, :width] = main
            s_edge[at, :, width:] = aux
        window = between(lane, start, start + 4)
        ring_n = pltpu.roll(jnp.where(lane == 0, aux, main), (3 + start) % width, 1)
        ring_s = pltpu.roll(jnp.where(lane == width - 1, aux, main), (1 + start) % width, 1)
        pack_n = jnp.where(window, ring_n, pack_n)
        pack_s = jnp.where(window, ring_s, pack_s)
        if 0 <= x < cells_x:
            row = jnp.concatenate([cur[x], sea_row(mask, x, MASK_ROWS)], 0)
            cur_n = jnp.where(
                between(lane_f, start, start + 3), pltpu.roll(row, (3 + start) % width, 1), cur_n
            )
            cur_s = jnp.where(
                between(lane_f, start + 1, start + 4), pltpu.roll(row, (1 + start) % width, 1), cur_s
            )
    even = is_even("gy")
    for msg, north_first in ((msg_a, even), (msg_b, ~even)):
        msg[:chans] = jnp.where(north_first, pack_n, pack_s).astype(BF16)
        msg[chans : chans + fields] = jnp.where(north_first, cur_n, cur_s).astype(BF16)
    base = chans + fields
    for f in (f_own, f_oth):
        for cols in chunks_of(bins):
            high = [f[x, width - 16 :, cols].astype(F32)[15:] for x in range(cells_x)]
            low = [f[x, :16, cols].astype(F32)[:1] for x in range(cells_x)]
            high, low = jnp.concatenate(high, 0), jnp.concatenate(low, 0)
            msg_a[base : base + cells_x] = jnp.where(even, high, low).astype(BF16)
            msg_b[base : base + cells_x] = jnp.where(even, low, high).astype(BF16)
            base += cells_x


def is_even(axis):
    return lax.rem(lax.axis_index(axis), 2) == 0


def from_sides(from_a, from_b, rows):
    even = is_even("gy")
    a, b = from_a[rows].astype(F32), from_b[rows].astype(F32)
    return jnp.where(even, b, a), jnp.where(even, a, b)


def southern(tile, start, width):
    return pltpu.roll(tile, (-start - 3) % width, 1)


def northern(tile, start, width):
    return pltpu.roll(tile, (-start - 1) % width, 1)


def halo_lanes(lane, low, high, width):
    return jnp.where(lane >= width - 3, low, jnp.where(lane < 3, high, 0.0))


def stokes_row(main, aux, pack_s, pack_n, start, lane, width):
    low = southern(pack_s, start, width)
    high = northern(pack_n, start, width)
    main = main + jnp.where(lane == 0, low, 0.0) + jnp.where(lane == width - 1, high, 0.0)
    return main, aux + halo_lanes(lane, low, high, width)


def relay_kernel(cells_x, s_edge, from_a, from_b, side_w, side_e, msg_e, msg_w, spectra):
    rows = spectra.shape[0] // 2
    spectra[:rows] = side_w[:rows]
    spectra[rows:] = side_e[:rows]
    chans, width = s_edge.shape[1], s_edge.shape[2] // 2
    fields = chans + MASK_ROWS
    stride = width // (cells_x + 2)
    half = width // 2
    lane = lane_of(chans, width)
    lane_f = lane_of(fields, width)
    pack_s, pack_n = from_sides(from_a, from_b, slice(0, chans))
    cur_s, cur_n = from_sides(from_a, from_b, slice(chans, chans + fields))
    for msg, first, first_cur, first_edge in (
        (msg_e, cells_x - 2, cells_x - EDGE, EDGE),
        (msg_w, -1, 0, 0),
    ):
        tile = jnp.zeros((chans, width), F32)
        cur_tile = jnp.zeros((fields, width), F32)
        for i in range(EDGE):
            edge = s_edge[first_edge + i]
            start = stride * (first + i + 1)
            main, aux = stokes_row(
                edge[:, :width], edge[:, width:], pack_s, pack_n, start, lane, width
            )
            msg[i * chans : (i + 1) * chans] = main.astype(BF16)
            at = SLOT * i
            tile = jnp.where(between(lane, at, at + 6), pltpu.roll(aux, at + 3, 1), tile)
            x = first_cur + i
            ring = halo_lanes(
                lane_f,
                southern(cur_s, stride * (x + 1), width),
                northern(cur_n, stride * (x + 1), width),
                width,
            )
            at += half
            cur_tile = jnp.where(between(lane_f, at, at + 6), pltpu.roll(ring, at + 3, 1), cur_tile)
        base = EDGE * chans
        msg[base : base + chans] = (tile + cur_tile[:chans]).astype(BF16)
        msg[base + chans : base + fields] = cur_tile[chans:].astype(BF16)


def momentum_kernel(
    s_main, s_aux, currents, mask, side_w, side_e, from_a, from_b, from_w, from_e, token, drag, cor,
    out,
    cur, flow_a, flow_b, stokes, result, in_sem, sem,
):
    del token
    cells_x, chans, width = s_aux.shape
    fields = chans + MASK_ROWS
    levels = chans // 2
    stride = width // (cells_x + 2)
    half = width // 2
    lane = lane_of(chans, width)
    lane_f = lane_of(fields, width)
    copies = load_currents(currents, range(cells_x), cur, in_sem)
    for copy in copies:
        copy.start()

    side_base = side_w.shape[0] - EDGE * fields
    corner_w, corner_e = from_w[EDGE * chans :].astype(F32), from_e[EDGE * chans :].astype(F32)
    pack_s, pack_n = from_sides(from_a, from_b, slice(0, chans))
    cur_s, cur_n = from_sides(from_a, from_b, slice(chans, chans + fields))

    def corner(tile, at, lanes):
        ring = pltpu.roll(tile, (-at - 3) % width, 1)
        return halo_lanes(lanes, ring, ring, width)

    for x in range(-SUBSTEPS, cells_x + SUBSTEPS):
        if 0 <= x < cells_x:
            flow_a[x + SUBSTEPS, chans:, :width] = sea_row(mask, x, MASK_ROWS)
            aux = halo_lanes(
                lane_f,
                southern(cur_s, stride * (x + 1), width),
                northern(cur_n, stride * (x + 1), width),
                width,
            )
        else:
            side, tile, i = (side_w, corner_w, x + SUBSTEPS) if x < 0 else (side_e, corner_e, x - cells_x)
            at = side_base + i * fields
            flow_a[x + SUBSTEPS, :, :width] = side[at : at + fields].astype(F32)
            aux = corner(tile, half + SLOT * i, lane_f)
        flow_a[x + SUBSTEPS, :, width:] = aux

    margin = SUBSTEPS - 1
    for x in range(-margin, cells_x + margin):
        main = aux = 0.0
        if -1 <= x <= cells_x:
            own_aux = s_aux[x] if 0 <= x < cells_x else 0.0
            main, aux = stokes_row(
                s_main[x + 1], own_aux, pack_s, pack_n, stride * (x + 1), lane, width
            )
        for message, tile, first in ((from_w, corner_w, -2), (from_e, corner_e, cells_x - 1)):
            i = x - first
            if 0 <= i < EDGE:
                main += message[i * chans : (i + 1) * chans].astype(F32)
                aux += corner(tile[:chans], SLOT * i, lane)
        sea = flow_a[x + SUBSTEPS, chans : chans + 1, :]
        stokes[x + margin, :, :width] = main * sea[:, :width]
        stokes[x + margin, :, width:] = aux * sea[:, width:]

    for copy in copies:
        copy.wait()
    for x in range(cells_x):
        flow_a[x + SUBSTEPS, :chans, :width] = cur[x]
    at_level = lax.broadcasted_iota(jnp.int32, (levels, 1), 0)
    drag_col = jnp.zeros((levels, 1), F32)
    for level in range(levels):
        drag_col = jnp.where(at_level == level, drag[level], drag_col)
    half_cor = time_step * cor[...]
    keep = 1.0 - 4.0 * time_step * viscosity - time_step * drag_col
    ring = 2 * width
    source, target = flow_a, flow_b
    for step in range(SUBSTEPS):
        margin = SUBSTEPS - 1 - step
        last = step == SUBSTEPS - 1
        for x in range(-margin, cells_x + margin):
            at = x + SUBSTEPS
            u, v = source[at, :levels], source[at, levels:chans]
            u_w, v_w = source[at - 1, :levels], source[at - 1, levels:chans]
            u_e, v_e = source[at + 1, :levels], source[at + 1, levels:chans]
            u_s, v_s = pltpu.roll(u, 1, 1), pltpu.roll(v, 1, 1)
            u_n, v_n = pltpu.roll(u, ring - 1, 1), pltpu.roll(v, ring - 1, 1)
            drift = stokes[x + SUBSTEPS - 1]
            if last:
                u, v, u_w, v_w, u_e, v_e, u_s, v_s, u_n, v_n, drift = (
                    field[:, :width] for field in (u, v, u_w, v_w, u_e, v_e, u_s, v_s, u_n, v_n, drift)
                )
            lanes = u.shape[1]
            spin = half_cor[:, :lanes] + 0.5 * time_step * ((v_e - v_w) - (u_n - u_s))
            sea = flow_a[at, chans : chans + 1, :lanes]
            u_new = keep * u + spin * (v + drift[levels:])
            v_new = keep * v - spin * (u + drift[:levels])
            u_new = sea * (u_new + time_step * viscosity * ((u_e + u_w) + (u_n + u_s)))
            v_new = sea * (v_new + time_step * viscosity * ((v_e + v_w) + (v_n + v_s)))
            if last:
                result[x, :levels] = u_new
                result[x, levels:] = v_new
                for c in range(2):
                    pltpu.make_async_copy(
                        result.at[x, pl.ds(c * levels, levels), :], out.at[c, :, x, :], sem.at[c, x]
                    ).start()
            else:
                target[at, :levels] = u_new
                target[at, levels:chans] = v_new
        source, target = target, source
    for x in range(cells_x):
        for c in range(2):
            pltpu.make_async_copy(
                result.at[x, pl.ds(c * levels, levels), :], out.at[c, :, x, :], sem.at[c, x]
            ).wait()


def wave_kernel(
    f_own, f_oth, courant_own, courant_oth, mask, interaction,
    sides_own, sides_oth, from_a, from_b,
    out, token,
    adv, shifted, slots, out_sem,
):
    cells_x, width, bins = f_own.shape
    pairs = cells_x // 2
    core = lax.axis_index("comp")
    own_at, oth_at = pl.multiple_of(core * bins, bins), pl.multiple_of((1 - core) * bins, bins)
    base = from_a.shape[0] - 2 * bins // CHUNK * cells_x
    halves = []
    for rows, sides, courant in (
        (f_own, sides_own, courant_own),
        (f_oth, sides_oth, courant_oth),
    ):
        for j, cols in enumerate(chunks_of(bins)):
            cour_x, cour_y = courant[0:1, cols], courant[1:2, cols]
            size_x, size_y = jnp.abs(cour_x), jnp.abs(cour_y)
            halves.append(
                (
                    rows, sides, j, cols,
                    *from_sides(from_a, from_b, slice(base, base + cells_x)),
                    1.0 - size_x - size_y, size_x, size_y, cour_x > 0.0, cour_y > 0.0,
                )
            )
            base += cells_x

    token[...] = jnp.zeros_like(token)

    def sea_column(x):
        return jnp.transpose(sea_row(mask, x, CHUNK))

    def advect(pair):
        for i in range(2):
            x = 2 * pair + i
            sea = sea_column(x)
            for n, (rows, sides, j, cols, south, north, c_mid, c_x, c_y, up_x, up_y) in enumerate(halves):
                west = slice(j * width, (j + 1) * width)
                east = slice(bins // CHUNK * width + j * width, bins // CHUNK * width + (j + 1) * width)
                mid = rows[x, :, cols].astype(F32)
                west_cell = rows[x - 1, :, cols] if x else sides[west]
                east_cell = rows[x + 1, :, cols] if x < cells_x - 1 else sides[east]
                shifted[n, 8 : 8 + width] = mid
                shifted[n, 7:8] = south[x : x + 1]
                shifted[n, 8 + width : 9 + width] = north[x : x + 1]
                beside = jnp.where(up_x, west_cell.astype(F32), east_cell.astype(F32))
                along = jnp.where(up_y, shifted[n, 7 : 7 + width], shifted[n, 9 : 9 + width])
                value = c_mid * mid + c_x * beside + c_y * along
                adv[pair % 2, i * width : (i + 1) * width, n * CHUNK : (n + 1) * CHUNK] = (
                    value * sea
                ).astype(BF16)

    def copy_out(pair):
        return pltpu.make_async_copy(
            slots.at[pair % 2], out.at[pl.ds(2 * pair, 2)], out_sem.at[pair % 2]
        )

    def finish(pair):
        at = pair % 2
        gain = 0.0
        for half, owner_at in ((adv[at, :, :bins], own_at), (adv[at, :, bins:], oth_at)):
            block = interaction[pl.ds(owner_at, bins), pl.ds(own_at, bins)]
            gain += jnp.dot(half, block, preferred_element_type=F32)
        if pair >= 2:
            copy_out(pair - 2).wait()
        for i in range(2):
            sea = sea_column(2 * pair + i)
            rows = slice(i * width, (i + 1) * width)
            for cols in chunks_of(bins):
                total = adv[at, rows, cols].astype(F32) + gain[rows, cols]
                slots[at, i, :, cols] = (total * sea).astype(BF16)
        copy_out(pair).start()

    advect(0)
    for pair in range(1, pairs):
        advect(pair)
        finish(pair - 1)
    finish(pairs - 1)
    for pair in range(max(pairs - 2, 0), pairs):
        copy_out(pair).wait()


def lat_coriolis(cells_y):
    ny_total = lax.axis_size("gy") * cells_y
    lane = jnp.arange(2 * cells_y)
    lane = jnp.where(lane >= cells_y + cells_y // 2, lane - 2 * cells_y, lane)
    lat_index = lax.axis_index("gy") * cells_y + lane
    return jnp.sin(jnp.pi * ((lat_index.astype(F32) + 0.5) / ny_total - 0.5))[None, :]


VMEM = pl.BlockSpec(memory_space=pltpu.VMEM)
SMEM = pl.BlockSpec(memory_space=pltpu.SMEM)
HBM = pl.BlockSpec(memory_space=pltpu.HBM)
DMA = pltpu.SemaphoreType.DMA


def call(kernel, name, out_shape, in_specs, out_specs, scratch, flops, traffic, limit):
    return pl.pallas_call(
        kernel,
        out_shape=out_shape,
        in_specs=in_specs,
        out_specs=out_specs,
        scratch_shapes=scratch,
        compiler_params=pltpu.CompilerParams(vmem_limit_bytes=limit * MIB),
        cost_estimate=pl.CostEstimate(flops=flops, bytes_accessed=traffic, transcendentals=0),
        name=name,
    )


def local(spectrum, sea_mask, courant, interaction, stokes_proj, currents, level_drag):
    cells_x, cells_y, bins = spectrum.shape
    levels = currents.shape[1]
    chans = 2 * levels
    fields = chans + MASK_ROWS
    swap = [(0, 1), (1, 0)]
    east, west = ring("gx")

    def message(rows):
        return jax.ShapeDtypeStruct((rows, cells_y), BF16)

    f_oth = lax.ppermute(spectrum, "comp", swap)
    courant_oth = lax.ppermute(courant, "comp", swap)
    side_rows = bins // CHUNK * cells_y + EDGE * fields
    to_e, to_w = call(
        outgoing_kernel,
        "outgoing",
        (message(side_rows),) * 2,
        [HBM, HBM, VMEM],
        (VMEM,) * 2,
        [
            pltpu.VMEM((2 * EDGE, chans, cells_y), F32),
            DMA((2 * EDGE, 2)),
            DMA((2, bins // CHUNK)),
        ],
        10**6,
        MIB,
        52,
    )(spectrum, currents, sea_mask)
    west_own = lax.ppermute(to_e, "gx", east)
    east_own = lax.ppermute(to_w, "gx", west)

    edge_rows = chans + fields + 2 * bins // CHUNK * cells_x
    s_main, s_aux, s_edge, to_a, to_b = call(
        project_kernel,
        "project",
        (
            jax.ShapeDtypeStruct((cells_x + 2, chans, cells_y), F32),
            jax.ShapeDtypeStruct((cells_x, chans, cells_y), F32),
            jax.ShapeDtypeStruct((2 * EDGE, chans, 2 * cells_y), F32),
            message(edge_rows),
            message(edge_rows),
        ),
        [VMEM] * 5 + [HBM, VMEM],
        (VMEM,) * 5,
        [
            pltpu.VMEM((cells_x, PARTS * chans, cells_y), F32),
            pltpu.VMEM((PARTS * chans, bins), BF16),
            pltpu.VMEM((PARTS * chans, bins), BF16),
            pltpu.VMEM((cells_x, chans, cells_y), F32),
            DMA((cells_x, 2)),
        ],
        3 * 10**9,
        8 * MIB,
        10,
    )(
        spectrum, f_oth, courant, courant_oth, jnp.transpose(stokes_proj, (0, 2, 1)), currents, sea_mask
    )
    from_a = lax.ppermute(to_a, "gy", pairing("gy", 0))
    from_b = lax.ppermute(to_b, "gy", pairing("gy", 1))

    to_e, to_w, sides_own = call(
        functools.partial(relay_kernel, cells_x),
        "relay",
        (message(EDGE * chans + fields),) * 2 + (message(2 * bins // CHUNK * cells_y),),
        [VMEM] * 5,
        (VMEM,) * 3,
        [],
        10**6,
        MIB,
        4,
    )(s_edge, from_a, from_b, west_own, east_own)
    sides_oth = lax.ppermute(sides_own, "comp", swap)
    from_w = lax.ppermute(to_e, "gx", east)
    from_e = lax.ppermute(to_w, "gx", west)

    wave_out, token = call(
        wave_kernel,
        "wave",
        (jax.ShapeDtypeStruct(spectrum.shape, BF16), jax.ShapeDtypeStruct((8, CHUNK), F32)),
        [VMEM] * 10,
        (HBM, VMEM),
        [
            pltpu.VMEM((2, 2 * cells_y, 2 * bins), BF16),
            pltpu.VMEM((2 * bins // CHUNK, cells_y + 16, CHUNK), F32),
            pltpu.VMEM((2, 2, cells_y, bins), BF16),
            DMA((2,)),
        ],
        4 * 10**9,
        10 * MIB,
        8,
    )(
        spectrum, f_oth, courant, courant_oth, sea_mask, interaction,
        sides_own, sides_oth, from_a, from_b,
    )
    currents_out = call(
        momentum_kernel,
        "momentum",
        jax.ShapeDtypeStruct(currents.shape, F32),
        [VMEM] * 2 + [HBM] + [VMEM] * 8 + [SMEM, VMEM],
        HBM,
        [
            pltpu.VMEM((cells_x, chans, cells_y), F32),
            pltpu.VMEM((cells_x + 2 * SUBSTEPS, fields, 2 * cells_y), F32),
            pltpu.VMEM((cells_x + 2 * SUBSTEPS, chans, 2 * cells_y), F32),
            pltpu.VMEM((cells_x + 2 * SUBSTEPS - 2, chans, 2 * cells_y), F32),
            pltpu.VMEM((cells_x, chans, cells_y), F32),
            DMA((cells_x, 2)),
            DMA((2, cells_x)),
        ],
        10**8,
        4 * MIB,
        10,
    )(
        s_main, s_aux, currents, sea_mask, west_own, east_own, from_a, from_b, from_w, from_e, token,
        level_drag, lat_coriolis(cells_y),
    )
    return (wave_out, currents_out)


def solution(mesh):
    in_specs = (
        P("gx", "gy", "comp"),
        P("gx", "gy"),
        P(None, "comp"),
        P(),
        P(),
        P(None, "comp", "gx", "gy"),
        P("comp"),
    )
    out_specs = (P("gx", "gy", "comp"), P(None, "comp", "gx", "gy"))
    return jax.shard_map(local, mesh=mesh, in_specs=in_specs, out_specs=out_specs, check_vma=False)
```

```python
import functools

import jax
import jax.numpy as jnp
from jax import lax
from jax.experimental import pallas as pl
from jax.experimental.pallas import tpu as pltpu
from jax.sharding import PartitionSpec as P

SUBSTEPS = 3

time_step = 0.5
viscosity = 0.4

F32 = jnp.float32
BF16 = jnp.bfloat16
MIB = 1 << 20
EDGE = 3
MASK_ROWS = 16
SLOT = 8
CHUNK = 128
PARTS = 5


def ring(axis):
    count = lax.axis_size(axis)
    forward = [(i, (i + 1) % count) for i in range(count)]
    return forward, [(target, source) for source, target in forward]


def pairing(axis, first):
    swaps = [(i, i + 1) for i in range(first, lax.axis_size(axis) - 1, 2)]
    return swaps + [(target, source) for source, target in swaps]


def lane_of(rows, width):
    return lax.broadcasted_iota(jnp.int32, (rows, width), 1)


def between(lane, low, high):
    return (lane >= low) & (lane < high)


def chunks_of(bins):
    return [slice(j * CHUNK, (j + 1) * CHUNK) for j in range(bins // CHUNK)]


def load_currents(currents, rows, cur, sem):
    levels = currents.shape[1]
    return [
        pltpu.make_async_copy(
            currents.at[c, :, x, :], cur.at[i, pl.ds(c * levels, levels), :], sem.at[i, c]
        )
        for i, x in enumerate(rows)
        for c in range(2)
    ]


def sea_row(mask, x, rows):
    return jnp.broadcast_to(mask[x : x + 1, :].astype(F32), (rows, mask.shape[1]))


def outgoing_kernel(
    spectrum, currents, mask_in, proj_in,
    msg_e, msg_w, proj,
    cur, mask, sem, row_sem,
):
    cells_x, width, bins = spectrum.shape
    levels = cur.shape[1]
    chans = 2 * levels
    fields = chans + MASK_ROWS
    copies = [
        pltpu.make_async_copy(currents, cur, sem.at[0]),
        pltpu.make_async_copy(mask_in, mask, sem.at[1]),
    ]
    proj_copy = pltpu.make_async_copy(proj_in, proj, sem.at[2])
    for side, (msg, x) in enumerate(((msg_e, cells_x - 1), (msg_w, 0))):
        for j, cols in enumerate(chunks_of(bins)):
            copies.append(
                pltpu.make_async_copy(
                    spectrum.at[x, :, cols], msg.at[pl.ds(j * width, width), :], row_sem.at[side, j]
                )
            )
    for copy in (*copies, proj_copy):
        copy.start()
    copies[0].wait()
    copies[1].wait()
    base = bins // CHUNK * width
    for msg, first in ((msg_e, cells_x - EDGE), (msg_w, 0)):
        for i in range(EDGE):
            x = first + i
            at = base + i * fields
            for c in range(2):
                msg[at + c * levels : at + (c + 1) * levels] = cur[c, :, x, :].astype(BF16)
            msg[at + chans : at + fields] = sea_row(mask, x, MASK_ROWS).astype(BF16)
    for copy in (*copies[2:], proj_copy):
        copy.wait()


def stokes_weights(proj, courant, core, owner, weights):
    levels = proj.shape[1] // 2
    bins = courant.shape[1]
    bins_at = pl.ds(pl.multiple_of(owner * bins, bins), bins)
    cour_x, cour_y = courant[0:1, :], courant[1:2, :]
    terms = (
        1.0 - jnp.abs(cour_x) - jnp.abs(cour_y),
        jnp.maximum(cour_x, 0.0),
        -jnp.minimum(cour_x, 0.0),
        jnp.maximum(cour_y, 0.0),
        -jnp.minimum(cour_y, 0.0),
    )
    for c in range(2):
        mine = proj[c, pl.ds(pl.multiple_of(core * levels, levels), levels), bins_at].astype(F32)
        for k, term in enumerate(terms):
            row = (2 * k + c) * levels
            weights[row : row + levels] = (mine * term).astype(BF16)


def project_kernel(
    f_own, f_oth, courant_own, courant_oth, stokes_proj, currents, mask,
    s_main, s_aux, s_edge, msg_a, msg_b,
    proj, wt_own, wt_oth, cur, sem,
):
    cells_x, width, bins = f_own.shape
    chans = s_main.shape[1]
    fields = chans + MASK_ROWS
    core = lax.axis_index("comp")
    copies = load_currents(currents, range(cells_x), cur, sem)
    for copy in copies:
        copy.start()
    stokes_weights(stokes_proj, courant_own, core, core, wt_own)
    stokes_weights(stokes_proj, courant_oth, core, 1 - core, wt_oth)
    contract = (((1,), (1,)), ((), ()))
    for pair in range(cells_x // 2):
        both = 0.0
        for wt, f in ((wt_own, f_own), (wt_oth, f_oth)):
            cells = f[2 * pair : 2 * pair + 2].reshape(2 * width, bins)
            both += lax.dot_general(wt[...], cells, contract, preferred_element_type=F32)
        proj[2 * pair] = both[:, :width]
        proj[2 * pair + 1] = both[:, width:]
    for copy in copies:
        copy.wait()

    lane = lane_of(chans, width)
    lane_f = lane_of(fields, width)

    def part(x, which):
        return proj[x, which * chans : (which + 1) * chans, :]

    pack_n = pack_s = jnp.zeros((chans, width), F32)
    cur_n = cur_s = jnp.zeros((fields, width), F32)
    for x in range(-1, cells_x + 1):
        start = stokes_lane(x)
        main = jnp.zeros((chans, width), F32)
        aux = jnp.zeros((chans, width), F32)
        if 0 <= x < cells_x:
            south = pltpu.roll(part(x, 3), 1, 1)
            north = pltpu.roll(part(x, 4), width - 1, 1)
            main = part(x, 0) + jnp.where(lane > 0, south, 0.0) + jnp.where(lane < width - 1, north, 0.0)
            aux = jnp.where(lane == 0, south, jnp.where(lane == width - 1, north, 0.0))
            s_aux[x] = aux
        if x >= 1:
            main += part(x - 1, 1)
        if x <= cells_x - 2:
            main += part(x + 1, 2)
        s_main[x + 1] = main
        if x < EDGE - 1 or x > cells_x - EDGE:
            at = x + 1 if x < EDGE - 1 else x - (cells_x - 2) + EDGE
            s_edge[at, :, :width] = main
            s_edge[at, :, width:] = aux
        window = between(lane, start, start + 4)
        ring_n = pltpu.roll(jnp.where(lane == 0, aux, main), (3 + start) % width, 1)
        ring_s = pltpu.roll(jnp.where(lane == width - 1, aux, main), (1 + start) % width, 1)
        pack_n = jnp.where(window, ring_n, pack_n)
        pack_s = jnp.where(window, ring_s, pack_s)
        if 0 <= x < cells_x:
            row = jnp.concatenate([cur[x], sea_row(mask, x, MASK_ROWS)], 0)
            start = current_lane(x, cells_x)
            window = between(lane_f, start, start + 3)
            cur_n = jnp.where(window, pltpu.roll(row, (3 + start) % width, 1), cur_n)
            cur_s = jnp.where(window, pltpu.roll(row, start, 1), cur_s)
    even = is_even("gy")
    for msg, north_first in ((msg_a, even), (msg_b, ~even)):
        pack, cur_pack = jnp.where(north_first, pack_n, pack_s), jnp.where(north_first, cur_n, cur_s)
        msg[:chans] = (pack + cur_pack[:chans]).astype(BF16)
        msg[chans:fields] = cur_pack[chans:].astype(BF16)
    for j, cols in enumerate(chunks_of(bins)):
        high = [f_own[x, width - 16 :, cols].astype(F32)[15:] for x in range(cells_x)]
        low = [f_own[x, :16, cols].astype(F32)[:1] for x in range(cells_x)]
        high, low = jnp.concatenate(high, 0), jnp.concatenate(low, 0)
        base = fields + j * cells_x
        msg_a[base : base + cells_x] = jnp.where(even, high, low).astype(BF16)
        msg_b[base : base + cells_x] = jnp.where(even, low, high).astype(BF16)


def is_even(axis):
    return lax.rem(lax.axis_index(axis), 2) == 0


def from_sides(from_a, from_b, rows):
    even = is_even("gy")
    a, b = from_a[rows].astype(F32), from_b[rows].astype(F32)
    return jnp.where(even, b, a), jnp.where(even, a, b)


def stokes_lane(x):
    return 4 * (x + 1)


def current_lane(x, cells_x):
    return 4 * (cells_x + 2) + 3 * x


def current_halo(tile_s, tile_n, x, cells_x, lane, width):
    start = current_lane(x, cells_x)
    low = pltpu.roll(tile_s, (-start - 3) % width, 1)
    return halo_lanes(lane, low, pltpu.roll(tile_n, (-start) % width, 1), width)


def southern(tile, start, width):
    return pltpu.roll(tile, (-start - 3) % width, 1)


def northern(tile, start, width):
    return pltpu.roll(tile, (-start - 1) % width, 1)


def halo_lanes(lane, low, high, width):
    return jnp.where(lane >= width - 3, low, jnp.where(lane < 3, high, 0.0))


def stokes_row(main, aux, pack_s, pack_n, start, lane, width):
    low = southern(pack_s, start, width)
    high = northern(pack_n, start, width)
    main = main + jnp.where(lane == 0, low, 0.0) + jnp.where(lane == width - 1, high, 0.0)
    return main, aux + halo_lanes(lane, low, high, width)


def relay_kernel(cells_x, s_edge, from_a, from_b, side_w, side_e, msg_e, msg_w, spectra):
    chans, width = s_edge.shape[1], s_edge.shape[2] // 2
    fields = chans + MASK_ROWS
    rows, edges = side_w.shape[0] - EDGE * fields, from_a.shape[0] - fields
    spectra[:rows] = side_w[:rows]
    spectra[rows : 2 * rows] = side_e[:rows]
    spectra[2 * rows : 2 * rows + edges] = from_a[fields:]
    spectra[2 * rows + edges :] = from_b[fields:]
    half = width // 2
    lane = lane_of(chans, width)
    lane_f = lane_of(fields, width)
    tile_s, tile_n = from_sides(from_a, from_b, slice(0, fields))
    for msg, first, first_cur, first_edge in (
        (msg_e, cells_x - 2, cells_x - EDGE, EDGE),
        (msg_w, -1, 0, 0),
    ):
        tile = jnp.zeros((chans, width), F32)
        cur_tile = jnp.zeros((fields, width), F32)
        for i in range(EDGE):
            edge = s_edge[first_edge + i]
            start = stokes_lane(first + i)
            main, aux = stokes_row(
                edge[:, :width], edge[:, width:], tile_s[:chans], tile_n[:chans], start, lane, width
            )
            msg[i * chans : (i + 1) * chans] = main.astype(BF16)
            at = SLOT * i
            tile = jnp.where(between(lane, at, at + 6), pltpu.roll(aux, at + 3, 1), tile)
            ring = current_halo(tile_s, tile_n, first_cur + i, cells_x, lane_f, width)
            at += half
            cur_tile = jnp.where(between(lane_f, at, at + 6), pltpu.roll(ring, at + 3, 1), cur_tile)
        base = EDGE * chans
        msg[base : base + chans] = (tile + cur_tile[:chans]).astype(BF16)
        msg[base + chans : base + fields] = cur_tile[chans:].astype(BF16)


def lat_coriolis(cells_y):
    ny_total = lax.axis_size("gy") * cells_y
    lane = lane_of(1, 2 * cells_y)
    lane = jnp.where(lane >= cells_y + cells_y // 2, lane - 2 * cells_y, lane)
    lat_index = lax.axis_index("gy") * cells_y + lane
    return jnp.sin(jnp.pi * ((lat_index.astype(F32) + 0.5) / ny_total - 0.5))


def momentum_kernel(
    s_main, s_aux, currents, mask_in, side_w, side_e, from_a, from_b, from_w, from_e, token, drag,
    out,
    cur, mask, flow_a, flow_b, stokes, result, mask_sem, in_sem, sem,
):
    del token
    cells_x, chans, width = s_aux.shape
    fields = chans + MASK_ROWS
    levels = chans // 2
    half = width // 2
    lane = lane_of(chans, width)
    lane_f = lane_of(fields, width)
    copies = load_currents(currents, range(cells_x), cur, in_sem)
    mask_copy = pltpu.make_async_copy(mask_in, mask, mask_sem)
    for copy in (mask_copy, *copies):
        copy.start()

    side_base = side_w.shape[0] - EDGE * fields
    corner_w, corner_e = from_w[EDGE * chans :].astype(F32), from_e[EDGE * chans :].astype(F32)
    tile_s, tile_n = from_sides(from_a, from_b, slice(0, fields))

    def corner(tile, at, lanes):
        ring = pltpu.roll(tile, (-at - 3) % width, 1)
        return halo_lanes(lanes, ring, ring, width)

    mask_copy.wait()
    for x in range(-SUBSTEPS, cells_x + SUBSTEPS):
        if 0 <= x < cells_x:
            flow_a[x + SUBSTEPS, chans:, :width] = sea_row(mask, x, MASK_ROWS)
            aux = current_halo(tile_s, tile_n, x, cells_x, lane_f, width)
        else:
            side, tile, i = (side_w, corner_w, x + SUBSTEPS) if x < 0 else (side_e, corner_e, x - cells_x)
            at = side_base + i * fields
            flow_a[x + SUBSTEPS, :, :width] = side[at : at + fields].astype(F32)
            aux = corner(tile, half + SLOT * i, lane_f)
        flow_a[x + SUBSTEPS, :, width:] = aux

    margin = SUBSTEPS - 1
    for x in range(-margin, cells_x + margin):
        main = aux = 0.0
        if -1 <= x <= cells_x:
            own_aux = s_aux[x] if 0 <= x < cells_x else 0.0
            main, aux = stokes_row(
                s_main[x + 1], own_aux, tile_s[:chans], tile_n[:chans], stokes_lane(x), lane, width
            )
        for message, tile, first in ((from_w, corner_w, -2), (from_e, corner_e, cells_x - 1)):
            i = x - first
            if 0 <= i < EDGE:
                main += message[i * chans : (i + 1) * chans].astype(F32)
                aux += corner(tile[:chans], SLOT * i, lane)
        sea = flow_a[x + SUBSTEPS, chans : chans + 1, :]
        stokes[x + margin, :, :width] = main * sea[:, :width]
        stokes[x + margin, :, width:] = aux * sea[:, width:]

    for copy in copies:
        copy.wait()
    for x in range(cells_x):
        flow_a[x + SUBSTEPS, :chans, :width] = cur[x]
    at_level = lax.broadcasted_iota(jnp.int32, (levels, 1), 0)
    drag_col = jnp.zeros((levels, 1), F32)
    for level in range(levels):
        drag_col = jnp.where(at_level == level, drag[level], drag_col)
    half_cor = time_step * lat_coriolis(width)
    keep = 1.0 - 4.0 * time_step * viscosity - time_step * drag_col
    ring = 2 * width
    source, target = flow_a, flow_b
    for step in range(SUBSTEPS):
        margin = SUBSTEPS - 1 - step
        last = step == SUBSTEPS - 1
        for x in range(-margin, cells_x + margin):
            at = x + SUBSTEPS
            u, v = source[at, :levels], source[at, levels:chans]
            u_w, v_w = source[at - 1, :levels], source[at - 1, levels:chans]
            u_e, v_e = source[at + 1, :levels], source[at + 1, levels:chans]
            u_s, v_s = pltpu.roll(u, 1, 1), pltpu.roll(v, 1, 1)
            u_n, v_n = pltpu.roll(u, ring - 1, 1), pltpu.roll(v, ring - 1, 1)
            drift = stokes[x + SUBSTEPS - 1]
            if last:
                u, v, u_w, v_w, u_e, v_e, u_s, v_s, u_n, v_n, drift = (
                    field[:, :width] for field in (u, v, u_w, v_w, u_e, v_e, u_s, v_s, u_n, v_n, drift)
                )
            lanes = u.shape[1]
            spin = half_cor[:, :lanes] + 0.5 * time_step * ((v_e - v_w) - (u_n - u_s))
            sea = flow_a[at, chans : chans + 1, :lanes]
            u_new = keep * u + spin * (v + drift[levels:])
            v_new = keep * v - spin * (u + drift[:levels])
            u_new = sea * (u_new + time_step * viscosity * ((u_e + u_w) + (u_n + u_s)))
            v_new = sea * (v_new + time_step * viscosity * ((v_e + v_w) + (v_n + v_s)))
            if last:
                result[x, :levels] = u_new
                result[x, levels:] = v_new
                for c in range(2):
                    pltpu.make_async_copy(
                        result.at[x, pl.ds(c * levels, levels), :], out.at[c, :, x, :], sem.at[c, x]
                    ).start()
            else:
                target[at, :levels] = u_new
                target[at, levels:chans] = v_new
        source, target = target, source
    for x in range(cells_x):
        for c in range(2):
            pltpu.make_async_copy(
                result.at[x, pl.ds(c * levels, levels), :], out.at[c, :, x, :], sem.at[c, x]
            ).wait()


def wave_kernel(
    rows_own, rows_oth, courant_own, courant_oth, mask, interaction,
    sides_own, sides_oth,
    out, token,
    inter, adv_a, adv_b, shifted, slots, inter_sem, out_sem,
):
    cells_x, width, bins = rows_own.shape
    pairs = cells_x // 2
    core = lax.axis_index("comp")
    own_at, oth_at = pl.multiple_of(core * bins, bins), pl.multiple_of((1 - core) * bins, bins)
    inter_copies = [
        pltpu.make_async_copy(
            interaction.at[pl.ds(at, bins), pl.ds(own_at, bins)],
            inter.at[pl.ds(n * bins, bins)],
            inter_sem.at[n],
        )
        for n, at in enumerate((own_at, oth_at))
    ]
    for copy in inter_copies:
        copy.start()

    even = is_even("gy")
    halves = []
    for rows, sides, courant in (
        (rows_own, sides_own, courant_own),
        (rows_oth, sides_oth, courant_oth),
    ):
        for j, cols in enumerate(chunks_of(bins)):
            cour_x, cour_y = courant[0:1, cols], courant[1:2, cols]
            size_x, size_y = jnp.abs(cour_x), jnp.abs(cour_y)
            base = bins // CHUNK * 2 * width + j * cells_x
            edge_a = sides[base : base + cells_x].astype(F32)
            base += bins // CHUNK * cells_x
            edge_b = sides[base : base + cells_x].astype(F32)
            halves.append(
                (
                    rows, sides, j, cols, jnp.where(even, edge_b, edge_a), jnp.where(even, edge_a, edge_b),
                    1.0 - size_x - size_y, size_x, size_y, cour_x > 0.0, cour_y > 0.0,
                )
            )

    token[...] = jnp.zeros_like(token)

    def sea_column(x):
        return jnp.transpose(sea_row(mask, x, CHUNK))

    adv = (adv_a, adv_b)

    def advect(pair, n):
        rows, sides, j, cols, south, north, c_mid, c_x, c_y, up_x, up_y = halves[n]
        first = 2 * pair
        cells = []
        for x in range(first - 1, first + 3):
            if x < 0:
                cells.append(sides[j * width : (j + 1) * width].astype(F32))
            elif x == cells_x:
                base = bins // CHUNK * width
                cells.append(sides[base + j * width : base + (j + 1) * width].astype(F32))
            else:
                cells.append(rows[x, :, cols].astype(F32))
        for i in range(2):
            x = first + i
            mid = cells[i + 1]
            moved = shifted.at[2 * n + i]
            moved[8 : 8 + width] = mid
            moved[7:8] = south[x : x + 1]
            moved[8 + width : 9 + width] = north[x : x + 1]
            low, high = moved[7 : 7 + width], moved[9 : 9 + width]
            beside = jnp.where(up_x, cells[i], cells[i + 2])
            value = c_mid * mid + c_x * beside + c_y * jnp.where(up_y, low, high)
            adv[pair % 2][i * width : (i + 1) * width, n * CHUNK : (n + 1) * CHUNK] = value.astype(BF16)

    def copy_out(pair):
        return pltpu.make_async_copy(
            slots.at[pl.ds(2 * pair, 2)], out.at[pl.ds(2 * pair, 2)], out_sem.at[pair]
        )

    def finish(pair, seas, piece):
        done = adv[pair % 2]
        i, block = piece // blocks, piece % blocks
        rows = slice(i * width, (i + 1) * width)
        cols = slice(block * bins // blocks, (block + 1) * bins // blocks)
        gain = jnp.dot(done[rows, :], inter[:, cols], preferred_element_type=F32)
        for c in chunks_of(bins // blocks):
            own = slice(cols.start + c.start, cols.start + c.stop)
            total = done[rows, own].astype(F32) + gain[:, c]
            slots[2 * pair + i, :, own] = (total * seas[i]).astype(BF16)

    def both_seas(pair):
        return [sea_column(2 * pair + i) for i in range(2)]

    blocks = 2
    pieces = 2 * blocks
    parts = len(halves)
    for n in range(parts):
        advect(0, n)
    for copy in inter_copies:
        copy.wait()
    for pair in range(1, pairs + 1):
        seas = both_seas(pair - 1)
        for piece in range(pieces):
            if pair < pairs:
                for n in range(piece * parts // pieces, (piece + 1) * parts // pieces):
                    advect(pair, n)
            finish(pair - 1, seas, piece)
        copy_out(pair - 1).start()
    for pair in range(pairs):
        copy_out(pair).wait()


VMEM = pl.BlockSpec(memory_space=pltpu.VMEM)
SMEM = pl.BlockSpec(memory_space=pltpu.SMEM)
HBM = pl.BlockSpec(memory_space=pltpu.HBM)
DMA = pltpu.SemaphoreType.DMA


def in_hbm(array):
    return pltpu.with_memory_space_constraint(array, pltpu.HBM)


def call(kernel, name, out_shape, in_specs, out_specs, scratch, flops, traffic, limit):
    return pl.pallas_call(
        kernel,
        out_shape=out_shape,
        in_specs=in_specs,
        out_specs=out_specs,
        scratch_shapes=scratch,
        compiler_params=pltpu.CompilerParams(vmem_limit_bytes=limit * MIB),
        cost_estimate=pl.CostEstimate(flops=flops, bytes_accessed=traffic, transcendentals=0),
        name=name,
    )


def local(spectrum, sea_mask, courant, interaction, stokes_proj, currents, level_drag):
    cells_x, cells_y, bins = spectrum.shape
    levels = currents.shape[1]
    chans = 2 * levels
    fields = chans + MASK_ROWS
    swap = [(0, 1), (1, 0)]
    east, west = ring("gx")

    def message(rows):
        return jax.ShapeDtypeStruct((rows, cells_y), BF16)

    f_oth = lax.ppermute(spectrum, "comp", swap)
    courant_oth = lax.ppermute(courant, "comp", swap)
    stokes_proj = jnp.transpose(stokes_proj, (0, 2, 1))
    side_rows = bins // CHUNK * cells_y + EDGE * fields
    to_e, to_w, stokes_proj = call(
        outgoing_kernel,
        "outgoing",
        (message(side_rows),) * 2 + (jax.ShapeDtypeStruct(stokes_proj.shape, BF16),),
        [HBM] * 4,
        (VMEM,) * 3,
        [
            pltpu.VMEM(currents.shape, F32),
            pltpu.VMEM(sea_mask.shape, jnp.int32),
            DMA((3,)),
            DMA((2, bins // CHUNK)),
        ],
        10**6,
        MIB,
        4,
    )(in_hbm(spectrum), in_hbm(currents), in_hbm(sea_mask), in_hbm(stokes_proj))
    west_own = lax.ppermute(to_e, "gx", east)
    east_own = lax.ppermute(to_w, "gx", west)

    edge_rows = fields + bins // CHUNK * cells_x
    s_main, s_aux, s_edge, to_a, to_b = call(
        project_kernel,
        "project",
        (
            jax.ShapeDtypeStruct((cells_x + 2, chans, cells_y), F32),
            jax.ShapeDtypeStruct((cells_x, chans, cells_y), F32),
            jax.ShapeDtypeStruct((2 * EDGE, chans, 2 * cells_y), F32),
            message(edge_rows),
            message(edge_rows),
        ),
        [VMEM] * 7,
        (VMEM,) * 5,
        [
            pltpu.VMEM((cells_x, PARTS * chans, cells_y), F32),
            pltpu.VMEM((PARTS * chans, bins), BF16),
            pltpu.VMEM((PARTS * chans, bins), BF16),
            pltpu.VMEM((cells_x, chans, cells_y), F32),
            DMA((cells_x, 2)),
        ],
        3 * 10**9,
        8 * MIB,
        8,
    )(
        spectrum, f_oth, courant, courant_oth, stokes_proj, currents, sea_mask
    )
    from_a = lax.ppermute(to_a, "gy", pairing("gy", 0))
    from_b = lax.ppermute(to_b, "gy", pairing("gy", 1))

    to_e, to_w, sides_own = call(
        functools.partial(relay_kernel, cells_x),
        "relay",
        (message(EDGE * chans + fields),) * 2
        + (message(2 * bins // CHUNK * (cells_y + cells_x)),),
        [VMEM] * 5,
        (VMEM,) * 3,
        [],
        10**6,
        MIB,
        4,
    )(s_edge, from_a, from_b, west_own, east_own)
    sides_oth = lax.ppermute(sides_own, "comp", swap)
    from_w = lax.ppermute(to_e, "gx", east)
    from_e = lax.ppermute(to_w, "gx", west)

    wave_out, token = call(
        wave_kernel,
        "wave",
        (jax.ShapeDtypeStruct(spectrum.shape, BF16), jax.ShapeDtypeStruct((8, CHUNK), F32)),
        [VMEM] * 5 + [HBM] + [VMEM] * 2,
        (HBM, VMEM),
        [
            pltpu.VMEM((2 * bins, bins), BF16),
            pltpu.VMEM((2 * cells_y, 2 * bins), BF16),
            pltpu.VMEM((2 * cells_y, 2 * bins), BF16),
            pltpu.VMEM((4 * bins // CHUNK, cells_y + 16, CHUNK), F32),
            pltpu.VMEM(spectrum.shape, BF16),
            DMA((2,)),
            DMA((cells_x // 2,)),
        ],
        4 * 10**9,
        10 * MIB,
        20,
    )(
        spectrum, f_oth, courant, courant_oth, sea_mask, in_hbm(interaction),
        sides_own, sides_oth,
    )
    currents_out = call(
        momentum_kernel,
        "momentum",
        jax.ShapeDtypeStruct(currents.shape, F32),
        [VMEM] * 2 + [HBM] * 2 + [VMEM] * 7 + [SMEM],
        HBM,
        [
            pltpu.VMEM((cells_x, chans, cells_y), F32),
            pltpu.VMEM(sea_mask.shape, jnp.int32),
            pltpu.VMEM((cells_x + 2 * SUBSTEPS, fields, 2 * cells_y), F32),
            pltpu.VMEM((cells_x + 2 * SUBSTEPS, chans, 2 * cells_y), F32),
            pltpu.VMEM((cells_x + 2 * SUBSTEPS - 2, chans, 2 * cells_y), F32),
            pltpu.VMEM((cells_x, chans, cells_y), F32),
            DMA,
            DMA((cells_x, 2)),
            DMA((2, cells_x)),
        ],
        10**8,
        4 * MIB,
        10,
    )(
        s_main, s_aux, in_hbm(currents), in_hbm(sea_mask), west_own, east_own, from_a, from_b, from_w, from_e, token,
        level_drag,
    )
    return (wave_out, currents_out)


def solution(mesh):
    in_specs = (
        P("gx", "gy", "comp"),
        P("gx", "gy"),
        P(None, "comp"),
        P(),
        P(),
        P(None, "comp", "gx", "gy"),
        P("comp"),
    )
    out_specs = (P("gx", "gy", "comp"), P(None, "comp", "gx", "gy"))
    return jax.shard_map(local, mesh=mesh, in_specs=in_specs, out_specs=out_specs, check_vma=False)
```

```python
import functools

import jax
import jax.numpy as jnp
from jax import lax
from jax.experimental import pallas as pl
from jax.experimental.pallas import tpu as pltpu
from jax.sharding import PartitionSpec as P

SUBSTEPS = 3

time_step = 0.5
viscosity = 0.4

F32 = jnp.float32
BF16 = jnp.bfloat16
MIB = 1 << 20
EDGE = 3
MASK_ROWS = 16
SLOT = 8
CHUNK = 128
TILE_ROWS = 16
EARLY_PAIRS = 4
TILE = 8
PARTS = 5


def ring(axis):
    count = lax.axis_size(axis)
    forward = [(i, (i + 1) % count) for i in range(count)]
    return forward, [(target, source) for source, target in forward]


def pairing(axis, first):
    swaps = [(i, i + 1) for i in range(first, lax.axis_size(axis) - 1, 2)]
    return swaps + [(target, source) for source, target in swaps]


def lane_of(rows, width):
    return lax.broadcasted_iota(jnp.int32, (rows, width), 1)


def between(lane, low, high):
    return (lane >= low) & (lane < high)


def chunks_of(bins):
    return [slice(j * CHUNK, (j + 1) * CHUNK) for j in range(bins // CHUNK)]


def sea_row(mask, x, rows):
    return jnp.broadcast_to(mask[x : x + 1, :].astype(F32), (rows, mask.shape[1]))


def outgoing_kernel(
    spectrum, currents, mask_in, proj_in,
    msg_e, msg_w, proj,
    cur, mask, sem, row_sem,
):
    cells_x, width, bins = spectrum.shape
    levels = cur.shape[1]
    chans = 2 * levels
    fields = chans + MASK_ROWS
    copies = [
        pltpu.make_async_copy(currents, cur, sem.at[0]),
        pltpu.make_async_copy(mask_in, mask, sem.at[1]),
    ]
    proj_copy = pltpu.make_async_copy(proj_in, proj, sem.at[2])
    for side, (msg, x) in enumerate(((msg_e, cells_x - 1), (msg_w, 0))):
        for j, cols in enumerate(chunks_of(bins)):
            copies.append(
                pltpu.make_async_copy(
                    spectrum.at[x, :, cols], msg.at[pl.ds(j * width, width), :], row_sem.at[side, j]
                )
            )
    for copy in (*copies, proj_copy):
        copy.start()
    copies[0].wait()
    copies[1].wait()
    base = bins // CHUNK * width
    for msg, first in ((msg_e, cells_x - EDGE), (msg_w, 0)):
        for i in range(EDGE):
            x = first + i
            at = base + i * fields
            for c in range(2):
                msg[at + c * levels : at + (c + 1) * levels] = cur[c, :, x, :].astype(BF16)
            msg[at + chans : at + fields] = sea_row(mask, x, MASK_ROWS).astype(BF16)
    for copy in (*copies[2:], proj_copy):
        copy.wait()


def stokes_weights(proj, courant, core, owner, weights):
    levels = proj.shape[1] // 2
    bins = courant.shape[1]
    bins_at = pl.ds(pl.multiple_of(owner * bins, bins), bins)
    cour_x, cour_y = courant[0:1, :], courant[1:2, :]
    terms = (
        1.0 - jnp.abs(cour_x) - jnp.abs(cour_y),
        jnp.maximum(cour_x, 0.0),
        -jnp.minimum(cour_x, 0.0),
        jnp.maximum(cour_y, 0.0),
        -jnp.minimum(cour_y, 0.0),
    )
    for c in range(2):
        mine = proj[c, pl.ds(pl.multiple_of(core * levels, levels), levels), bins_at].astype(F32)
        for k, term in enumerate(terms):
            row = (2 * k + c) * levels
            weights[row : row + levels] = (mine * term).astype(BF16)


def project_kernel(
    f_own, f_oth, courant_own, courant_oth, stokes_proj, currents, mask,
    s_main, s_aux, s_edge, state, msg_a, msg_b, token,
    proj, wt_own, wt_oth,
):
    cells_x, width, bins = f_own.shape
    chans = s_main.shape[1]
    fields = chans + MASK_ROWS
    core = lax.axis_index("comp")
    token[...] = jnp.zeros_like(token)
    stokes_weights(stokes_proj, courant_own, core, core, wt_own)
    stokes_weights(stokes_proj, courant_oth, core, 1 - core, wt_oth)
    contract = (((1,), (1,)), ((), ()))
    for pair in range(cells_x // 2):
        both = 0.0
        for wt, f in ((wt_own, f_own), (wt_oth, f_oth)):
            cells = f[2 * pair : 2 * pair + 2].reshape(2 * width, bins)
            both += lax.dot_general(wt[...], cells, contract, preferred_element_type=F32)
        proj[2 * pair] = both[:, :width]
        proj[2 * pair + 1] = both[:, width:]
    lane = lane_of(chans, width)
    lane_f = lane_of(fields, width)

    def part(x, which):
        return proj[x, which * chans : (which + 1) * chans, :]

    pack_n = pack_s = jnp.zeros((chans, width), F32)
    cur_n = cur_s = jnp.zeros((fields, width), F32)
    for x in range(-1, cells_x + 1):
        start = stokes_lane(x)
        main = jnp.zeros((chans, width), F32)
        aux = jnp.zeros((chans, width), F32)
        if 0 <= x < cells_x:
            south = pltpu.roll(part(x, 3), 1, 1)
            north = pltpu.roll(part(x, 4), width - 1, 1)
            main = part(x, 0) + jnp.where(lane > 0, south, 0.0) + jnp.where(lane < width - 1, north, 0.0)
            aux = jnp.where(lane == 0, south, jnp.where(lane == width - 1, north, 0.0))
            s_aux[x] = aux
        if x >= 1:
            main += part(x - 1, 1)
        if x <= cells_x - 2:
            main += part(x + 1, 2)
        s_main[x + 1] = main
        if x < EDGE - 1 or x > cells_x - EDGE:
            at = x + 1 if x < EDGE - 1 else x - (cells_x - 2) + EDGE
            s_edge[at, :, :width] = main
            s_edge[at, :, width:] = aux
        window = between(lane, start, start + 4)
        ring_n = pltpu.roll(jnp.where(lane == 0, aux, main), (3 + start) % width, 1)
        ring_s = pltpu.roll(jnp.where(lane == width - 1, aux, main), (1 + start) % width, 1)
        pack_n = jnp.where(window, ring_n, pack_n)
        pack_s = jnp.where(window, ring_s, pack_s)
        if 0 <= x < cells_x:
            row = jnp.concatenate(
                [currents[0, :, x, :], currents[1, :, x, :], sea_row(mask, x, MASK_ROWS)], 0
            )
            state[x] = row
            start = current_lane(x, cells_x)
            window = between(lane_f, start, start + 3)
            cur_n = jnp.where(window, pltpu.roll(row, (3 + start) % width, 1), cur_n)
            cur_s = jnp.where(window, pltpu.roll(row, start, 1), cur_s)
    even = is_even("gy")
    for msg, north_first in ((msg_a, even), (msg_b, ~even)):
        pack, cur_pack = jnp.where(north_first, pack_n, pack_s), jnp.where(north_first, cur_n, cur_s)
        msg[:chans] = (pack + cur_pack[:chans]).astype(BF16)
        msg[chans:fields] = cur_pack[chans:].astype(BF16)
    for j, cols in enumerate(chunks_of(bins)):
        high = [f_own[x, width - 16 :, cols].astype(F32)[15:] for x in range(cells_x)]
        low = [f_own[x, :16, cols].astype(F32)[:1] for x in range(cells_x)]
        high, low = jnp.concatenate(high, 0), jnp.concatenate(low, 0)
        base = fields + j * cells_x
        msg_a[base : base + cells_x] = jnp.where(even, high, low).astype(BF16)
        msg_b[base : base + cells_x] = jnp.where(even, low, high).astype(BF16)


def is_even(axis):
    return lax.rem(lax.axis_index(axis), 2) == 0


def from_sides(from_a, from_b, rows):
    even = is_even("gy")
    a, b = from_a[rows].astype(F32), from_b[rows].astype(F32)
    return jnp.where(even, b, a), jnp.where(even, a, b)


def stokes_lane(x):
    return 4 * (x + 1)


def current_lane(x, cells_x):
    return 4 * (cells_x + 2) + 3 * x


def current_halo(tile_s, tile_n, x, cells_x, lane, width):
    start = current_lane(x, cells_x)
    low = pltpu.roll(tile_s, (-start - 3) % width, 1)
    return halo_lanes(lane, low, pltpu.roll(tile_n, (-start) % width, 1), width)


def southern(tile, start, width):
    return pltpu.roll(tile, (-start - 3) % width, 1)


def northern(tile, start, width):
    return pltpu.roll(tile, (-start - 1) % width, 1)


def halo_lanes(lane, low, high, width):
    return jnp.where(lane >= width - 3, low, jnp.where(lane < 3, high, 0.0))


def stokes_row(main, aux, pack_s, pack_n, start, lane, width):
    low = southern(pack_s, start, width)
    high = northern(pack_n, start, width)
    main = main + jnp.where(lane == 0, low, 0.0) + jnp.where(lane == width - 1, high, 0.0)
    return main, aux + halo_lanes(lane, low, high, width)


def relay_kernel(cells_x, s_edge, from_a, from_b, side_w, side_e, token, msg_e, msg_w, spectra):
    del token
    chans, width = s_edge.shape[1], s_edge.shape[2] // 2
    fields = chans + MASK_ROWS
    rows, edges = side_w.shape[0] - EDGE * fields, from_a.shape[0] - fields
    spectra[:rows] = side_w[:rows]
    spectra[rows : 2 * rows] = side_e[:rows]
    spectra[2 * rows : 2 * rows + edges] = from_a[fields:]
    spectra[2 * rows + edges :] = from_b[fields:]
    half = width // 2
    lane = lane_of(chans, width)
    lane_f = lane_of(fields, width)
    tile_s, tile_n = from_sides(from_a, from_b, slice(0, fields))
    for msg, first, first_cur, first_edge in (
        (msg_e, cells_x - 2, cells_x - EDGE, EDGE),
        (msg_w, -1, 0, 0),
    ):
        tile = jnp.zeros((chans, width), F32)
        cur_tile = jnp.zeros((fields, width), F32)
        for i in range(EDGE):
            edge = s_edge[first_edge + i]
            start = stokes_lane(first + i)
            main, aux = stokes_row(
                edge[:, :width], edge[:, width:], tile_s[:chans], tile_n[:chans], start, lane, width
            )
            msg[i * chans : (i + 1) * chans] = main.astype(BF16)
            at = SLOT * i
            tile = jnp.where(between(lane, at, at + 6), pltpu.roll(aux, at + 3, 1), tile)
            ring = current_halo(tile_s, tile_n, first_cur + i, cells_x, lane_f, width)
            at += half
            cur_tile = jnp.where(between(lane_f, at, at + 6), pltpu.roll(ring, at + 3, 1), cur_tile)
        base = EDGE * chans
        msg[base : base + chans] = (tile + cur_tile[:chans]).astype(BF16)
        msg[base + chans : base + fields] = cur_tile[chans:].astype(BF16)


def lat_coriolis(cells_y):
    ny_total = lax.axis_size("gy") * cells_y
    lane = lane_of(1, 2 * cells_y)
    lane = jnp.where(lane >= cells_y + cells_y // 2, lane - 2 * cells_y, lane)
    lat_index = lax.axis_index("gy") * cells_y + lane
    return jnp.sin(jnp.pi * ((lat_index.astype(F32) + 0.5) / ny_total - 0.5))


def momentum_kernel(
    s_main, s_aux, state, side_w, side_e, from_a, from_b, from_w, from_e, token, drag,
    out,
    flow_a, flow_b, stokes, result, sem,
):
    del token
    cells_x, chans, width = s_aux.shape
    fields = chans + MASK_ROWS
    levels = chans // 2
    half = width // 2
    lane = lane_of(chans, width)
    lane_f = lane_of(fields, width)
    side_base = side_w.shape[0] - EDGE * fields
    corner_w, corner_e = from_w[EDGE * chans :].astype(F32), from_e[EDGE * chans :].astype(F32)
    tile_s, tile_n = from_sides(from_a, from_b, slice(0, fields))

    def corner(tile, at, lanes):
        ring = pltpu.roll(tile, (-at - 3) % width, 1)
        return halo_lanes(lanes, ring, ring, width)

    for x in range(-SUBSTEPS, cells_x + SUBSTEPS):
        if 0 <= x < cells_x:
            flow_a[x + SUBSTEPS, :, :width] = state[x]
            aux = current_halo(tile_s, tile_n, x, cells_x, lane_f, width)
        else:
            side, tile, i = (side_w, corner_w, x + SUBSTEPS) if x < 0 else (side_e, corner_e, x - cells_x)
            at = side_base + i * fields
            flow_a[x + SUBSTEPS, :, :width] = side[at : at + fields].astype(F32)
            aux = corner(tile, half + SLOT * i, lane_f)
        flow_a[x + SUBSTEPS, :, width:] = aux

    margin = SUBSTEPS - 1
    for x in range(-margin, cells_x + margin):
        main = aux = 0.0
        if -1 <= x <= cells_x:
            own_aux = s_aux[x] if 0 <= x < cells_x else 0.0
            main, aux = stokes_row(
                s_main[x + 1], own_aux, tile_s[:chans], tile_n[:chans], stokes_lane(x), lane, width
            )
        for message, tile, first in ((from_w, corner_w, -2), (from_e, corner_e, cells_x - 1)):
            i = x - first
            if 0 <= i < EDGE:
                main += message[i * chans : (i + 1) * chans].astype(F32)
                aux += corner(tile[:chans], SLOT * i, lane)
        sea = flow_a[x + SUBSTEPS, chans : chans + 1, :]
        stokes[x + margin, :, :width] = main * sea[:, :width]
        stokes[x + margin, :, width:] = aux * sea[:, width:]

    at_level = lax.broadcasted_iota(jnp.int32, (levels, 1), 0)
    drag_col = jnp.zeros((levels, 1), F32)
    for level in range(levels):
        drag_col = jnp.where(at_level == level, drag[level], drag_col)
    def copy_out(block):
        rows = pl.ds(block * TILE, TILE)
        return pltpu.make_async_copy(
            result.at[:, :, rows, :], out.at[:, :, rows, :], sem.at[block]
        )

    half_cor = time_step * lat_coriolis(width)
    keep = 1.0 - 4.0 * time_step * viscosity - time_step * drag_col
    ring = 2 * width
    source, target = flow_a, flow_b
    for step in range(SUBSTEPS):
        margin = SUBSTEPS - 1 - step
        last = step == SUBSTEPS - 1
        for x in range(-margin, cells_x + margin):
            at = x + SUBSTEPS
            u, v = source[at, :levels], source[at, levels:chans]
            u_w, v_w = source[at - 1, :levels], source[at - 1, levels:chans]
            u_e, v_e = source[at + 1, :levels], source[at + 1, levels:chans]
            u_s, v_s = pltpu.roll(u, 1, 1), pltpu.roll(v, 1, 1)
            u_n, v_n = pltpu.roll(u, ring - 1, 1), pltpu.roll(v, ring - 1, 1)
            drift = stokes[x + SUBSTEPS - 1]
            if last:
                u, v, u_w, v_w, u_e, v_e, u_s, v_s, u_n, v_n, drift = (
                    field[:, :width] for field in (u, v, u_w, v_w, u_e, v_e, u_s, v_s, u_n, v_n, drift)
                )
            lanes = u.shape[1]
            spin = half_cor[:, :lanes] + 0.5 * time_step * ((v_e - v_w) - (u_n - u_s))
            sea = flow_a[at, chans : chans + 1, :lanes]
            u_new = keep * u + spin * (v + drift[levels:])
            v_new = keep * v - spin * (u + drift[:levels])
            u_new = sea * (u_new + time_step * viscosity * ((u_e + u_w) + (u_n + u_s)))
            v_new = sea * (v_new + time_step * viscosity * ((v_e + v_w) + (v_n + v_s)))
            if last:
                result[0, :, x, :] = u_new
                result[1, :, x, :] = v_new
                if x % TILE == TILE - 1:
                    copy_out(x // TILE).start()
            else:
                target[at, :levels] = u_new
                target[at, levels:chans] = v_new
        source, target = target, source
    for block in range(cells_x // TILE):
        copy_out(block).wait()


def wave_groups(cells_x, width, early_pairs):
    inner = [[(x, TILE_ROWS, width - TILE_ROWS) for x in (1 + 2 * p, 2 + 2 * p)] for p in range(early_pairs)]
    outer = [[(0, 0, width), (cells_x - 1, 0, width)]]
    for x in range(1 + 2 * early_pairs, cells_x - 1, 2):
        outer.append([(i, 0, width) for i in range(x, min(x + 2, cells_x - 1))])
    seams = [
        block
        for x in range(1, 1 + 2 * early_pairs)
        for block in ((x, 0, TILE_ROWS), (x, width - TILE_ROWS, width))
    ]
    step = 2 * width // TILE_ROWS
    outer += [seams[i : i + step] for i in range(0, len(seams), step)]
    return inner, outer


def rows_of(group):
    return sum(last - first for _, first, last in group)


def wave_body(
    groups, sides,
    f_own, f_oth, courant_own, courant_oth, mask, interaction,
    slots, send,
    inter, adv, sea, moved, inter_sem,
):
    cells_x, width, bins = f_own.shape
    core = lax.axis_index("comp")
    own_at, oth_at = pl.multiple_of(core * bins, bins), pl.multiple_of((1 - core) * bins, bins)
    inter_copies = [
        pltpu.make_async_copy(
            interaction.at[pl.ds(at, bins), pl.ds(own_at, bins)],
            inter.at[pl.ds(n * bins, bins)],
            inter_sem.at[n],
        )
        for n, at in enumerate((own_at, oth_at))
    ]
    for copy in inter_copies:
        copy.start()

    even = is_even("gy")
    per_core = bins // CHUNK
    halves = []
    for rows, side, courant in zip((f_own, f_oth), sides, (courant_own, courant_oth), strict=True):
        for j, cols in enumerate(chunks_of(bins)):
            cour_x, cour_y = courant[0:1, cols], courant[1:2, cols]
            size_x, size_y = jnp.abs(cour_x), jnp.abs(cour_y)
            south = north = None
            if side is not None:
                base = 2 * per_core * width + j * cells_x
                edge_a = side[base : base + cells_x].astype(F32)
                base += per_core * cells_x
                edge_b = side[base : base + cells_x].astype(F32)
                south, north = jnp.where(even, edge_b, edge_a), jnp.where(even, edge_a, edge_b)
            halves.append(
                (
                    rows, side, j, cols, south, north,
                    1.0 - size_x - size_y, size_x, size_y, cour_x > 0.0, cour_y > 0.0,
                )
            )

    def cell(rows, side, j, cols, x, first, last):
        if 0 <= x < cells_x:
            return rows[x, first:last, cols].astype(F32)
        base = (0 if x < 0 else per_core * width) + j * width
        return side[base + first : base + last].astype(F32)

    def advect(at, n):
        rows, side, j, cols, south, north, c_mid, c_x, c_y, up_x, up_y = halves[n]
        row = 0
        for i, (x, first, last) in enumerate(groups[at]):
            low_end, high_end = max(first - TILE_ROWS, 0), min(last + TILE_ROWS, width)
            wide = cell(rows, side, j, cols, x, low_end, high_end)
            mid = wide[first - low_end : last - low_end]
            shifted = moved.at[(len(groups[at]) * n + i) % moved.shape[0]]
            shifted[8 + low_end : 8 + high_end] = wide
            if first == 0:
                shifted[7:8] = south[x : x + 1]
            if last == width:
                shifted[8 + width : 9 + width] = north[x : x + 1]
            low, high = shifted[7 + first : 7 + last], shifted[9 + first : 9 + last]
            west = cell(rows, side, j, cols, x - 1, first, last)
            east = cell(rows, side, j, cols, x + 1, first, last)
            value = c_mid * mid + c_x * jnp.where(up_x, west, east) + c_y * jnp.where(up_y, low, high)
            height = last - first
            adv[at % 2][row : row + height, n * CHUNK : (n + 1) * CHUNK] = value.astype(BF16)
            row += height

    def put_sea(at):
        row = 0
        for x, first, last in groups[at]:
            column = jnp.transpose(sea_row(mask, x, CHUNK))
            sea[at % 2][row : row + last - first] = column[first:last]
            row += last - first

    def finish(at, piece):
        done, mine = adv[at % 2], sea[at % 2]
        half, block = piece // blocks, piece % blocks
        middle = rows_of(groups[at]) // 2 // TILE_ROWS * TILE_ROWS
        low, high = (0, middle) if half == 0 else (middle, rows_of(groups[at]))
        cols = slice(block * bins // blocks, (block + 1) * bins // blocks)
        gain = jnp.dot(done[low:high, :], inter[:, cols], preferred_element_type=F32)
        row = 0
        for x, first, last in groups[at]:
            begin, end = max(low, row), min(high, row + last - first)
            if begin < end:
                lats = slice(first + begin - row, first + end - row)
                for c in chunks_of(bins // blocks):
                    own = slice(cols.start + c.start, cols.start + c.stop)
                    total = done[begin:end, own].astype(F32) + gain[begin - low : end - low, c]
                    slots[x, lats, own] = (total * mine[begin:end]).astype(BF16)
            row += last - first

    blocks = 2
    pieces = 2 * blocks
    parts = len(halves)
    for n in range(parts):
        advect(0, n)
    for copy in inter_copies:
        copy.wait()
    for at in range(1, len(groups) + 1):
        put_sea(at - 1)
        for piece in range(pieces):
            if at < len(groups):
                for n in range(piece * parts // pieces, (piece + 1) * parts // pieces):
                    advect(at, n)
            finish(at - 1, piece)
        send(at - 1)


def inner_kernel(
    groups,
    f_own, f_oth, courant_own, courant_oth, mask, interaction, token_in,
    wave, token,
    inter, adv_a, adv_b, sea_a, sea_b, moved, inter_sem,
):
    token[...] = token_in[...]
    wave_body(
        groups, (None, None),
        f_own, f_oth, courant_own, courant_oth, mask, interaction,
        wave, lambda n: None,
        inter, (adv_a, adv_b), (sea_a, sea_b), moved, inter_sem,
    )


def outer_kernel(
    groups, groups_before,
    f_own, f_oth, courant_own, courant_oth, mask, interaction, sides_own, sides_oth, wave,
    out, token,
    slots, inter, adv_a, adv_b, sea_a, sea_b, moved, inter_sem, out_sem,
):
    token[...] = jnp.zeros_like(token)
    copies = []

    def send(source, blocks):
        for x, first, last in blocks:
            lats = pl.ds(first, last - first)
            copies.append(
                pltpu.make_async_copy(source.at[x, lats], out.at[x, lats], out_sem.at[len(copies)])
            )
            copies[-1].start()

    for group in groups_before:
        send(wave, group)
    wave_body(
        groups, (sides_own, sides_oth),
        f_own, f_oth, courant_own, courant_oth, mask, interaction,
        slots, lambda n: send(slots, groups[n]),
        inter, (adv_a, adv_b), (sea_a, sea_b), moved, inter_sem,
    )
    for copy in copies:
        copy.wait()


VMEM = pl.BlockSpec(memory_space=pltpu.VMEM)
SMEM = pl.BlockSpec(memory_space=pltpu.SMEM)
HBM = pl.BlockSpec(memory_space=pltpu.HBM)
DMA = pltpu.SemaphoreType.DMA


def in_hbm(array):
    return pltpu.with_memory_space_constraint(array, pltpu.HBM)


def call(kernel, name, out_shape, in_specs, out_specs, scratch, flops, traffic, limit):
    return pl.pallas_call(
        kernel,
        out_shape=out_shape,
        in_specs=in_specs,
        out_specs=out_specs,
        scratch_shapes=scratch,
        compiler_params=pltpu.CompilerParams(vmem_limit_bytes=limit * MIB),
        cost_estimate=pl.CostEstimate(flops=flops, bytes_accessed=traffic, transcendentals=0),
        name=name,
    )


def local(spectrum, sea_mask, courant, interaction, stokes_proj, currents, level_drag):
    cells_x, cells_y, bins = spectrum.shape
    levels = currents.shape[1]
    chans = 2 * levels
    fields = chans + MASK_ROWS
    swap = [(0, 1), (1, 0)]
    east, west = ring("gx")

    def message(rows):
        return jax.ShapeDtypeStruct((rows, cells_y), BF16)

    f_oth = lax.ppermute(spectrum, "comp", swap)
    courant_oth = lax.ppermute(courant, "comp", swap)
    stokes_proj = jnp.transpose(stokes_proj, (0, 2, 1))
    token_type = jax.ShapeDtypeStruct((8, CHUNK), F32)
    side_rows = bins // CHUNK * cells_y + EDGE * fields
    to_e, to_w, stokes_proj = call(
        outgoing_kernel,
        "outgoing",
        (message(side_rows),) * 2 + (jax.ShapeDtypeStruct(stokes_proj.shape, BF16),),
        [HBM] * 4,
        (VMEM,) * 3,
        [
            pltpu.VMEM(currents.shape, F32),
            pltpu.VMEM(sea_mask.shape, jnp.int32),
            DMA((3,)),
            DMA((2, bins // CHUNK)),
        ],
        10**6,
        MIB,
        4,
    )(in_hbm(spectrum), in_hbm(currents), in_hbm(sea_mask), in_hbm(stokes_proj))
    west_own = lax.ppermute(to_e, "gx", east)
    east_own = lax.ppermute(to_w, "gx", west)

    edge_rows = fields + bins // CHUNK * cells_x
    s_main, s_aux, s_edge, state, to_a, to_b, token = call(
        project_kernel,
        "project",
        (
            jax.ShapeDtypeStruct((cells_x + 2, chans, cells_y), F32),
            jax.ShapeDtypeStruct((cells_x, chans, cells_y), F32),
            jax.ShapeDtypeStruct((2 * EDGE, chans, 2 * cells_y), F32),
            jax.ShapeDtypeStruct((cells_x, fields, cells_y), F32),
            message(edge_rows),
            message(edge_rows),
            token_type,
        ),
        [VMEM] * 7,
        (VMEM,) * 7,
        [
            pltpu.VMEM((cells_x, PARTS * chans, cells_y), F32),
            pltpu.VMEM((PARTS * chans, bins), BF16),
            pltpu.VMEM((PARTS * chans, bins), BF16),
        ],
        3 * 10**9,
        8 * MIB,
        8,
    )(
        spectrum, f_oth, courant, courant_oth, stokes_proj, currents, sea_mask
    )
    from_a = lax.ppermute(to_a, "gy", pairing("gy", 0))
    from_b = lax.ppermute(to_b, "gy", pairing("gy", 1))

    inner, outer = wave_groups(cells_x, cells_y, EARLY_PAIRS)
    wave_type = jax.ShapeDtypeStruct(spectrum.shape, BF16)

    def wave_scratch(groups):
        height = max(map(rows_of, groups))
        return [
            pltpu.VMEM((2 * bins, bins), BF16),
            *[pltpu.VMEM((height, 2 * bins), BF16)] * 2,
            *[pltpu.VMEM((height, CHUNK), F32)] * 2,
            pltpu.VMEM((16, cells_y + 16, CHUNK), F32),
            DMA((2,)),
        ]

    wave, token = call(
        functools.partial(inner_kernel, inner),
        "inner",
        (wave_type, token_type),
        [VMEM] * 5 + [HBM, VMEM],
        (VMEM,) * 2,
        wave_scratch(inner),
        2 * 10**9,
        5 * MIB,
        20,
    )(spectrum, f_oth, courant, courant_oth, sea_mask, in_hbm(interaction), token)

    to_e, to_w, sides_own = call(
        functools.partial(relay_kernel, cells_x),
        "relay",
        (message(EDGE * chans + fields),) * 2
        + (message(2 * bins // CHUNK * (cells_y + cells_x)),),
        [VMEM] * 6,
        (VMEM,) * 3,
        [],
        10**6,
        MIB,
        4,
    )(s_edge, from_a, from_b, west_own, east_own, token)
    sides_oth = lax.ppermute(sides_own, "comp", swap)
    from_w = lax.ppermute(to_e, "gx", east)
    from_e = lax.ppermute(to_w, "gx", west)

    wave_out, token = call(
        functools.partial(outer_kernel, outer, inner),
        "outer",
        (wave_type, token_type),
        [VMEM] * 5 + [HBM] + [VMEM] * 3,
        (HBM, VMEM),
        [
            pltpu.VMEM(spectrum.shape, BF16),
            *wave_scratch(outer),
            DMA((sum(map(len, inner + outer)),)),
        ],
        2 * 10**9,
        5 * MIB,
        20,
    )(
        spectrum, f_oth, courant, courant_oth, sea_mask, in_hbm(interaction), sides_own, sides_oth, wave
    )
    currents_out = call(
        momentum_kernel,
        "momentum",
        jax.ShapeDtypeStruct(currents.shape, F32),
        [VMEM] * 10 + [SMEM],
        HBM,
        [
            pltpu.VMEM((cells_x + 2 * SUBSTEPS, fields, 2 * cells_y), F32),
            pltpu.VMEM((cells_x + 2 * SUBSTEPS, chans, 2 * cells_y), F32),
            pltpu.VMEM((cells_x + 2 * SUBSTEPS - 2, chans, 2 * cells_y), F32),
            pltpu.VMEM(currents.shape, F32),
            DMA((cells_x // TILE,)),
        ],
        10**8,
        4 * MIB,
        10,
    )(
        s_main, s_aux, state, west_own, east_own, from_a, from_b, from_w, from_e, token,
        level_drag,
    )
    return (wave_out, currents_out)


def solution(mesh):
    in_specs = (
        P("gx", "gy", "comp"),
        P("gx", "gy"),
        P(None, "comp"),
        P(),
        P(),
        P(None, "comp", "gx", "gy"),
        P("comp"),
    )
    out_specs = (P("gx", "gy", "comp"), P(None, "comp", "gx", "gy"))
    return jax.shard_map(local, mesh=mesh, in_specs=in_specs, out_specs=out_specs, check_vma=False)
```

```python
import functools

import jax
import jax.numpy as jnp
from jax import lax
from jax.experimental import pallas as pl
from jax.experimental.pallas import tpu as pltpu
from jax.sharding import PartitionSpec as P

SUBSTEPS = 3

time_step = 0.5
viscosity = 0.4

F32 = jnp.float32
BF16 = jnp.bfloat16
MIB = 1 << 20
EDGE = 3
MASK_ROWS = 16
SLOT = 8
CHUNK = 128
TILE_ROWS = 16
EARLY_PAIRS = 4
SEAM_GROUP = 1
TILE = 8
PARTS = 5


def ring(axis):
    count = lax.axis_size(axis)
    forward = [(i, (i + 1) % count) for i in range(count)]
    return forward, [(target, source) for source, target in forward]


def pairing(axis, first):
    swaps = [(i, i + 1) for i in range(first, lax.axis_size(axis) - 1, 2)]
    return swaps + [(target, source) for source, target in swaps]


def lane_of(rows, width):
    return lax.broadcasted_iota(jnp.int32, (rows, width), 1)


def between(lane, low, high):
    return (lane >= low) & (lane < high)


def chunks_of(bins):
    return [slice(j * CHUNK, (j + 1) * CHUNK) for j in range(bins // CHUNK)]


def sea_row(mask, x, rows):
    return jnp.broadcast_to(mask[x : x + 1, :].astype(F32), (rows, mask.shape[1]))


def outgoing_kernel(
    spectrum, currents, mask_in, proj_in,
    msg_e, msg_w, proj,
    cur, mask, sem, row_sem,
):
    cells_x, width, bins = spectrum.shape
    levels = cur.shape[1]
    chans = 2 * levels
    fields = chans + MASK_ROWS
    copies = [
        pltpu.make_async_copy(currents, cur, sem.at[0]),
        pltpu.make_async_copy(mask_in, mask, sem.at[1]),
    ]
    proj_copy = pltpu.make_async_copy(proj_in, proj, sem.at[2])
    for side, (msg, x) in enumerate(((msg_e, cells_x - 1), (msg_w, 0))):
        for j, cols in enumerate(chunks_of(bins)):
            copies.append(
                pltpu.make_async_copy(
                    spectrum.at[x, :, cols], msg.at[pl.ds(j * width, width), :], row_sem.at[side, j]
                )
            )
    for copy in (*copies, proj_copy):
        copy.start()
    copies[0].wait()
    copies[1].wait()
    base = bins // CHUNK * width
    for msg, first in ((msg_e, cells_x - EDGE), (msg_w, 0)):
        for i in range(EDGE):
            x = first + i
            at = base + i * fields
            for c in range(2):
                msg[at + c * levels : at + (c + 1) * levels] = cur[c, :, x, :].astype(BF16)
            msg[at + chans : at + fields] = sea_row(mask, x, MASK_ROWS).astype(BF16)
    for copy in (*copies[2:], proj_copy):
        copy.wait()


def stokes_weights(proj, courant, core, owner, weights):
    levels = proj.shape[1] // 2
    bins = courant.shape[1]
    bins_at = pl.ds(pl.multiple_of(owner * bins, bins), bins)
    cour_x, cour_y = courant[0:1, :], courant[1:2, :]
    terms = (
        1.0 - jnp.abs(cour_x) - jnp.abs(cour_y),
        jnp.maximum(cour_x, 0.0),
        -jnp.minimum(cour_x, 0.0),
        jnp.maximum(cour_y, 0.0),
        -jnp.minimum(cour_y, 0.0),
    )
    for c in range(2):
        mine = proj[c, pl.ds(pl.multiple_of(core * levels, levels), levels), bins_at].astype(F32)
        for k, term in enumerate(terms):
            row = (2 * k + c) * levels
            weights[row : row + levels] = (mine * term).astype(BF16)


def project_kernel(
    f_own, f_oth, courant_own, courant_oth, stokes_proj, currents, mask,
    s_main, s_aux, s_edge, state, msg_a, msg_b, token,
    proj, wt_own, wt_oth,
):
    cells_x, width, bins = f_own.shape
    chans = s_main.shape[1]
    fields = chans + MASK_ROWS
    core = lax.axis_index("comp")
    token[...] = jnp.zeros_like(token)
    stokes_weights(stokes_proj, courant_own, core, core, wt_own)
    stokes_weights(stokes_proj, courant_oth, core, 1 - core, wt_oth)
    contract = (((1,), (1,)), ((), ()))
    for pair in range(cells_x // 2):
        both = 0.0
        for wt, f in ((wt_own, f_own), (wt_oth, f_oth)):
            cells = f[2 * pair : 2 * pair + 2].reshape(2 * width, bins)
            both += lax.dot_general(wt[...], cells, contract, preferred_element_type=F32)
        proj[2 * pair] = both[:, :width]
        proj[2 * pair + 1] = both[:, width:]
    lane = lane_of(chans, width)
    lane_f = lane_of(fields, width)

    def part(x, which):
        return proj[x, which * chans : (which + 1) * chans, :]

    pack_n = pack_s = jnp.zeros((chans, width), F32)
    cur_n = cur_s = jnp.zeros((fields, width), F32)
    for x in range(-1, cells_x + 1):
        start = stokes_lane(x)
        main = jnp.zeros((chans, width), F32)
        aux = jnp.zeros((chans, width), F32)
        if 0 <= x < cells_x:
            south = pltpu.roll(part(x, 3), 1, 1)
            north = pltpu.roll(part(x, 4), width - 1, 1)
            main = part(x, 0) + jnp.where(lane > 0, south, 0.0) + jnp.where(lane < width - 1, north, 0.0)
            aux = jnp.where(lane == 0, south, jnp.where(lane == width - 1, north, 0.0))
            s_aux[x] = aux
        if x >= 1:
            main += part(x - 1, 1)
        if x <= cells_x - 2:
            main += part(x + 1, 2)
        s_main[x + 1] = main
        if x < EDGE - 1 or x > cells_x - EDGE:
            at = x + 1 if x < EDGE - 1 else x - (cells_x - 2) + EDGE
            s_edge[at, :, :width] = main
            s_edge[at, :, width:] = aux
        window = between(lane, start, start + 4)
        ring_n = pltpu.roll(jnp.where(lane == 0, aux, main), (3 + start) % width, 1)
        ring_s = pltpu.roll(jnp.where(lane == width - 1, aux, main), (1 + start) % width, 1)
        pack_n = jnp.where(window, ring_n, pack_n)
        pack_s = jnp.where(window, ring_s, pack_s)
        if 0 <= x < cells_x:
            row = jnp.concatenate(
                [currents[0, :, x, :], currents[1, :, x, :], sea_row(mask, x, MASK_ROWS)], 0
            )
            state[x] = row
            start = current_lane(x, cells_x)
            window = between(lane_f, start, start + 3)
            cur_n = jnp.where(window, pltpu.roll(row, (3 + start) % width, 1), cur_n)
            cur_s = jnp.where(window, pltpu.roll(row, start, 1), cur_s)
    even = is_even("gy")
    for msg, north_first in ((msg_a, even), (msg_b, ~even)):
        pack, cur_pack = jnp.where(north_first, pack_n, pack_s), jnp.where(north_first, cur_n, cur_s)
        msg[:chans] = (pack + cur_pack[:chans]).astype(BF16)
        msg[chans:fields] = cur_pack[chans:].astype(BF16)
    for j, cols in enumerate(chunks_of(bins)):
        high = [f_own[x, width - 16 :, cols].astype(F32)[15:] for x in range(cells_x)]
        low = [f_own[x, :16, cols].astype(F32)[:1] for x in range(cells_x)]
        high, low = jnp.concatenate(high, 0), jnp.concatenate(low, 0)
        base = fields + j * cells_x
        msg_a[base : base + cells_x] = jnp.where(even, high, low).astype(BF16)
        msg_b[base : base + cells_x] = jnp.where(even, low, high).astype(BF16)


def is_even(axis):
    return lax.rem(lax.axis_index(axis), 2) == 0


def from_sides(from_a, from_b, rows):
    even = is_even("gy")
    a, b = from_a[rows].astype(F32), from_b[rows].astype(F32)
    return jnp.where(even, b, a), jnp.where(even, a, b)


def stokes_lane(x):
    return 4 * (x + 1)


def current_lane(x, cells_x):
    return 4 * (cells_x + 2) + 3 * x


def current_halo(tile_s, tile_n, x, cells_x, lane, width):
    start = current_lane(x, cells_x)
    low = pltpu.roll(tile_s, (-start - 3) % width, 1)
    return halo_lanes(lane, low, pltpu.roll(tile_n, (-start) % width, 1), width)


def southern(tile, start, width):
    return pltpu.roll(tile, (-start - 3) % width, 1)


def northern(tile, start, width):
    return pltpu.roll(tile, (-start - 1) % width, 1)


def halo_lanes(lane, low, high, width):
    return jnp.where(lane >= width - 3, low, jnp.where(lane < 3, high, 0.0))


def stokes_row(main, aux, pack_s, pack_n, start, lane, width):
    low = southern(pack_s, start, width)
    high = northern(pack_n, start, width)
    main = main + jnp.where(lane == 0, low, 0.0) + jnp.where(lane == width - 1, high, 0.0)
    return main, aux + halo_lanes(lane, low, high, width)


def relay_kernel(cells_x, s_edge, from_a, from_b, side_w, side_e, token, msg_e, msg_w, spectra):
    del token
    chans, width = s_edge.shape[1], s_edge.shape[2] // 2
    fields = chans + MASK_ROWS
    rows, edges = side_w.shape[0] - EDGE * fields, from_a.shape[0] - fields
    spectra[:rows] = side_w[:rows]
    spectra[rows : 2 * rows] = side_e[:rows]
    spectra[2 * rows : 2 * rows + edges] = from_a[fields:]
    spectra[2 * rows + edges :] = from_b[fields:]
    half = width // 2
    lane = lane_of(chans, width)
    lane_f = lane_of(fields, width)
    tile_s, tile_n = from_sides(from_a, from_b, slice(0, fields))
    for msg, first, first_cur, first_edge in (
        (msg_e, cells_x - 2, cells_x - EDGE, EDGE),
        (msg_w, -1, 0, 0),
    ):
        tile = jnp.zeros((chans, width), F32)
        cur_tile = jnp.zeros((fields, width), F32)
        for i in range(EDGE):
            edge = s_edge[first_edge + i]
            start = stokes_lane(first + i)
            main, aux = stokes_row(
                edge[:, :width], edge[:, width:], tile_s[:chans], tile_n[:chans], start, lane, width
            )
            msg[i * chans : (i + 1) * chans] = main.astype(BF16)
            at = SLOT * i
            tile = jnp.where(between(lane, at, at + 6), pltpu.roll(aux, at + 3, 1), tile)
            ring = current_halo(tile_s, tile_n, first_cur + i, cells_x, lane_f, width)
            at += half
            cur_tile = jnp.where(between(lane_f, at, at + 6), pltpu.roll(ring, at + 3, 1), cur_tile)
        base = EDGE * chans
        msg[base : base + chans] = (tile + cur_tile[:chans]).astype(BF16)
        msg[base + chans : base + fields] = cur_tile[chans:].astype(BF16)


def lat_coriolis(cells_y):
    ny_total = lax.axis_size("gy") * cells_y
    lane = lane_of(1, 2 * cells_y)
    lane = jnp.where(lane >= cells_y + cells_y // 2, lane - 2 * cells_y, lane)
    lat_index = lax.axis_index("gy") * cells_y + lane
    return jnp.sin(jnp.pi * ((lat_index.astype(F32) + 0.5) / ny_total - 0.5))


def momentum_kernel(
    s_main, s_aux, state, side_w, side_e, from_a, from_b, from_w, from_e, token, drag,
    out,
    flow_a, flow_b, stokes, result, sem,
):
    del token
    cells_x, chans, width = s_aux.shape
    fields = chans + MASK_ROWS
    levels = chans // 2
    half = width // 2
    lane = lane_of(chans, width)
    lane_f = lane_of(fields, width)
    side_base = side_w.shape[0] - EDGE * fields
    corner_w, corner_e = from_w[EDGE * chans :].astype(F32), from_e[EDGE * chans :].astype(F32)
    tile_s, tile_n = from_sides(from_a, from_b, slice(0, fields))

    def corner(tile, at, lanes):
        ring = pltpu.roll(tile, (-at - 3) % width, 1)
        return halo_lanes(lanes, ring, ring, width)

    for x in range(-SUBSTEPS, cells_x + SUBSTEPS):
        if 0 <= x < cells_x:
            flow_a[x + SUBSTEPS, :, :width] = state[x]
            aux = current_halo(tile_s, tile_n, x, cells_x, lane_f, width)
        else:
            side, tile, i = (side_w, corner_w, x + SUBSTEPS) if x < 0 else (side_e, corner_e, x - cells_x)
            at = side_base + i * fields
            flow_a[x + SUBSTEPS, :, :width] = side[at : at + fields].astype(F32)
            aux = corner(tile, half + SLOT * i, lane_f)
        flow_a[x + SUBSTEPS, :, width:] = aux

    margin = SUBSTEPS - 1
    for x in range(-margin, cells_x + margin):
        main = aux = 0.0
        if -1 <= x <= cells_x:
            own_aux = s_aux[x] if 0 <= x < cells_x else 0.0
            main, aux = stokes_row(
                s_main[x + 1], own_aux, tile_s[:chans], tile_n[:chans], stokes_lane(x), lane, width
            )
        for message, tile, first in ((from_w, corner_w, -2), (from_e, corner_e, cells_x - 1)):
            i = x - first
            if 0 <= i < EDGE:
                main += message[i * chans : (i + 1) * chans].astype(F32)
                aux += corner(tile[:chans], SLOT * i, lane)
        sea = flow_a[x + SUBSTEPS, chans : chans + 1, :]
        stokes[x + margin, :, :width] = main * sea[:, :width]
        stokes[x + margin, :, width:] = aux * sea[:, width:]

    at_level = lax.broadcasted_iota(jnp.int32, (levels, 1), 0)
    drag_col = jnp.zeros((levels, 1), F32)
    for level in range(levels):
        drag_col = jnp.where(at_level == level, drag[level], drag_col)
    def copy_out(block):
        rows = pl.ds(block * TILE, TILE)
        return pltpu.make_async_copy(
            result.at[:, :, rows, :], out.at[:, :, rows, :], sem.at[block]
        )

    half_cor = time_step * lat_coriolis(width)
    keep = 1.0 - 4.0 * time_step * viscosity - time_step * drag_col
    ring = 2 * width
    source, target = flow_a, flow_b
    for step in range(SUBSTEPS):
        margin = SUBSTEPS - 1 - step
        last = step == SUBSTEPS - 1
        for x in range(-margin, cells_x + margin):
            at = x + SUBSTEPS
            u, v = source[at, :levels], source[at, levels:chans]
            u_w, v_w = source[at - 1, :levels], source[at - 1, levels:chans]
            u_e, v_e = source[at + 1, :levels], source[at + 1, levels:chans]
            u_s, v_s = pltpu.roll(u, 1, 1), pltpu.roll(v, 1, 1)
            u_n, v_n = pltpu.roll(u, ring - 1, 1), pltpu.roll(v, ring - 1, 1)
            drift = stokes[x + SUBSTEPS - 1]
            if last:
                u, v, u_w, v_w, u_e, v_e, u_s, v_s, u_n, v_n, drift = (
                    field[:, :width] for field in (u, v, u_w, v_w, u_e, v_e, u_s, v_s, u_n, v_n, drift)
                )
            lanes = u.shape[1]
            spin = half_cor[:, :lanes] + 0.5 * time_step * ((v_e - v_w) - (u_n - u_s))
            sea = flow_a[at, chans : chans + 1, :lanes]
            u_new = keep * u + spin * (v + drift[levels:])
            v_new = keep * v - spin * (u + drift[:levels])
            u_new = sea * (u_new + time_step * viscosity * ((u_e + u_w) + (u_n + u_s)))
            v_new = sea * (v_new + time_step * viscosity * ((v_e + v_w) + (v_n + v_s)))
            if last:
                result[0, :, x, :] = u_new
                result[1, :, x, :] = v_new
                if x % TILE == TILE - 1:
                    copy_out(x // TILE).start()
            else:
                target[at, :levels] = u_new
                target[at, levels:chans] = v_new
        source, target = target, source
    for block in range(cells_x // TILE):
        copy_out(block).wait()


def wave_groups(cells_x, width, early_pairs):
    early = 1 + 2 * early_pairs
    inner = [[(x, 0, width), (x + 1, 0, width)] for x in range(1, early, 2)]
    outer = [[(0, 0, width), (cells_x - 1, 0, width)]]
    for x in range(early, cells_x - 1, 2):
        outer.append([(i, 0, width) for i in range(x, min(x + 2, cells_x - 1))])
    return inner, outer


def rows_of(group):
    return sum(last - first for _, first, last in group)


def wave_body(
    groups, sides, seam, wave, arriving,
    f_own, f_oth, courant_own, courant_oth, mask, inter,
    slots, send,
    adv, sea, moved,
):
    cells_x, width, bins = f_own.shape
    even = is_even("gy")
    per_core = bins // CHUNK
    halves = []
    for rows, side, courant in zip((f_own, f_oth), sides, (courant_own, courant_oth), strict=True):
        for j, cols in enumerate(chunks_of(bins)):
            cour_x, cour_y = courant[0:1, cols], courant[1:2, cols]
            size_x, size_y = jnp.abs(cour_x), jnp.abs(cour_y)
            south = north = None
            if side is not None:
                base = 2 * per_core * width + j * cells_x
                edge_a = side[base : base + cells_x].astype(F32)
                base += per_core * cells_x
                edge_b = side[base : base + cells_x].astype(F32)
                south, north = jnp.where(even, edge_b, edge_a), jnp.where(even, edge_a, edge_b)
            halves.append(
                (
                    rows, side, j, cols, south, north,
                    1.0 - size_x - size_y, size_x, size_y, cour_x > 0.0, cour_y > 0.0,
                )
            )

    def cell(rows, side, j, cols, x, first, last):
        if 0 <= x < cells_x:
            return rows[x, first:last, cols].astype(F32)
        base = (0 if x < 0 else per_core * width) + j * width
        return side[base + first : base + last].astype(F32)

    def advect(at, n):
        rows, side, j, cols, south, north, c_mid, c_x, c_y, up_x, up_y = halves[n]
        row = 0
        for i, (x, first, last) in enumerate(groups[at]):
            mid = cell(rows, side, j, cols, x, first, last)
            shifted = moved.at[(len(groups[at]) * n + i) % moved.shape[0]]
            shifted[8 + first : 8 + last] = mid
            none = jnp.zeros((1, CHUNK), F32)
            shifted[7:8] = none if south is None else south[x : x + 1]
            shifted[8 + width : 9 + width] = none if north is None else north[x : x + 1]
            low, high = shifted[7 + first : 7 + last], shifted[9 + first : 9 + last]
            west = cell(rows, side, j, cols, x - 1, first, last)
            east = cell(rows, side, j, cols, x + 1, first, last)
            value = c_mid * mid + c_x * jnp.where(up_x, west, east) + c_y * jnp.where(up_y, low, high)
            height = last - first
            adv[at % 2][row : row + height, n * CHUNK : (n + 1) * CHUNK] = value.astype(BF16)
            row += height

    def advect_seam(n):
        rows, _, _, cols, south, north, c_mid, c_x, c_y, up_x, up_y = halves[n]
        around = range(seam[0] - 1, seam[-1] + 2)
        own = slice(seam[0], seam[-1] + 1)
        row = rows_of(groups[SEAM_GROUP])
        for first, edge, beside in ((0, 0, 1), (width - TILE_ROWS, TILE_ROWS - 1, TILE_ROWS - 2)):
            tiles = [rows[x, first : first + TILE_ROWS, cols].astype(F32) for x in around]
            line = jnp.concatenate([tile[edge : edge + 1] for tile in tiles], 0)
            inward = jnp.concatenate([tile[beside : beside + 1] for tile in tiles[1:-1]], 0)
            low, high = (south[own], inward) if first == 0 else (inward, north[own])
            value = (
                c_mid * line[1:-1]
                + c_x * jnp.where(up_x, line[:-2], line[2:])
                + c_y * jnp.where(up_y, low, high)
            )
            value = jnp.concatenate([value, jnp.zeros((TILE_ROWS - len(seam), CHUNK), F32)], 0)
            adv[SEAM_GROUP % 2][row : row + TILE_ROWS, n * CHUNK : (n + 1) * CHUNK] = value.astype(BF16)
            row += TILE_ROWS

    def height_of(at):
        return rows_of(groups[at]) + (2 * TILE_ROWS if seam and at == SEAM_GROUP else 0)

    def put_sea(at):
        row = 0
        for x, first, last in groups[at]:
            column = jnp.transpose(sea_row(mask, x, CHUNK))
            sea[at % 2][row : row + last - first] = column[first:last]
            row += last - first
        if seam and at == SEAM_GROUP:
            for lat in (0, width - 1):
                column = mask[seam[0] : seam[-1] + 1, lat : lat + 1].astype(F32)
                column = jnp.concatenate([column, jnp.zeros((TILE_ROWS - len(seam), 1), F32)], 0)
                sea[at % 2][row : row + TILE_ROWS] = jnp.broadcast_to(column, (TILE_ROWS, CHUNK))
                row += TILE_ROWS

    def finish(at, piece):
        done, mine = adv[at % 2], sea[at % 2]
        half, block = piece // blocks, piece % blocks
        middle = height_of(at) // 2 // TILE_ROWS * TILE_ROWS
        low, high = (0, middle) if half == 0 else (middle, height_of(at))
        cols = slice(block * bins // blocks, (block + 1) * bins // blocks)
        gain = jnp.dot(done[low:high, :], inter[:, cols], preferred_element_type=F32)
        row = 0
        for x, first, last in groups[at]:
            begin, end = max(low, row), min(high, row + last - first)
            if begin < end:
                lats = slice(first + begin - row, first + end - row)
                for c in chunks_of(bins // blocks):
                    own = slice(cols.start + c.start, cols.start + c.stop)
                    total = done[begin:end, own].astype(F32) + gain[begin - low : end - low, c]
                    slots[x, lats, own] = (total * mine[begin:end]).astype(BF16)
            row += last - first
        if seam and at == SEAM_GROUP and half == 1:
            at_row = lax.broadcasted_iota(jnp.int32, (TILE_ROWS, CHUNK), 0)
            for first, edge in ((0, 0), (width - TILE_ROWS, TILE_ROWS - 1)):
                end = row + TILE_ROWS
                for c in chunks_of(bins // blocks):
                    own = slice(cols.start + c.start, cols.start + c.stop)
                    total = done[row:end, own].astype(F32) + gain[row - low : end - low, c]
                    total *= mine[row:end]
                    for i, x in enumerate(seam):
                        tile = wave[x, first : first + TILE_ROWS, own].astype(F32)
                        tile = jnp.where(at_row == edge, total[i : i + 1], tile)
                        slots[x, first : first + TILE_ROWS, own] = tile.astype(BF16)
                row = end

    blocks = 2
    pieces = 2 * blocks
    parts = len(halves)
    for n in range(parts):
        advect(0, n)
    for copy in arriving:
        copy.wait()
    for at in range(1, len(groups) + 1):
        put_sea(at - 1)
        for piece in range(pieces):
            if at < len(groups):
                for n in range(piece * parts // pieces, (piece + 1) * parts // pieces):
                    advect(at, n)
                    if seam and at == SEAM_GROUP:
                        advect_seam(n)
            finish(at - 1, piece)
        send(at - 1)


def inner_kernel(
    groups,
    f_own, f_oth, courant_own, courant_oth, mask, interaction, token_in,
    wave, inter, token,
    adv_a, adv_b, sea_a, sea_b, moved, inter_sem,
):
    token[...] = token_in[...]
    bins = f_own.shape[2]
    core = lax.axis_index("comp")
    own_at, oth_at = pl.multiple_of(core * bins, bins), pl.multiple_of((1 - core) * bins, bins)
    inter_copies = [
        pltpu.make_async_copy(
            interaction.at[pl.ds(at, bins), pl.ds(own_at, bins)],
            inter.at[pl.ds(n * bins, bins)],
            inter_sem.at[n],
        )
        for n, at in enumerate((own_at, oth_at))
    ]
    for copy in inter_copies:
        copy.start()
    wave_body(
        groups, (None, None), (), None, inter_copies,
        f_own, f_oth, courant_own, courant_oth, mask, inter,
        wave, lambda n: None,
        (adv_a, adv_b), (sea_a, sea_b), moved,
    )


def outer_kernel(
    groups, groups_before,
    f_own, f_oth, courant_own, courant_oth, mask, inter, sides_own, sides_oth, wave,
    out, token,
    slots, adv_a, adv_b, sea_a, sea_b, moved, out_sem,
):
    token[...] = jnp.zeros_like(token)
    copies = []

    def send(source, blocks):
        for x, first, last in blocks:
            lats = pl.ds(first, last - first)
            copies.append(
                pltpu.make_async_copy(source.at[x, lats], out.at[x, lats], out_sem.at[len(copies)])
            )
            copies[-1].start()

    seam = [x for group in groups_before for x, _, _ in group]
    width = wave.shape[1]
    send(wave, [(x, TILE_ROWS, width - TILE_ROWS) for x in seam])
    rims = [(0, TILE_ROWS), (width - TILE_ROWS, width)]

    def sent(n):
        send(slots, groups[n])
        if n == SEAM_GROUP:
            send(slots, [(x, first, last) for x in seam for first, last in rims])

    wave_body(
        groups, (sides_own, sides_oth), seam, wave, (),
        f_own, f_oth, courant_own, courant_oth, mask, inter,
        slots, sent,
        (adv_a, adv_b), (sea_a, sea_b), moved,
    )
    for copy in copies:
        copy.wait()


VMEM = pl.BlockSpec(memory_space=pltpu.VMEM)
SMEM = pl.BlockSpec(memory_space=pltpu.SMEM)
HBM = pl.BlockSpec(memory_space=pltpu.HBM)
DMA = pltpu.SemaphoreType.DMA


def in_hbm(array):
    return pltpu.with_memory_space_constraint(array, pltpu.HBM)


def call(kernel, name, out_shape, in_specs, out_specs, scratch, flops, traffic, limit):
    return pl.pallas_call(
        kernel,
        out_shape=out_shape,
        in_specs=in_specs,
        out_specs=out_specs,
        scratch_shapes=scratch,
        compiler_params=pltpu.CompilerParams(vmem_limit_bytes=limit * MIB),
        cost_estimate=pl.CostEstimate(flops=flops, bytes_accessed=traffic, transcendentals=0),
        name=name,
    )


def local(spectrum, sea_mask, courant, interaction, stokes_proj, currents, level_drag):
    cells_x, cells_y, bins = spectrum.shape
    levels = currents.shape[1]
    chans = 2 * levels
    fields = chans + MASK_ROWS
    swap = [(0, 1), (1, 0)]
    east, west = ring("gx")

    def message(rows):
        return jax.ShapeDtypeStruct((rows, cells_y), BF16)

    f_oth = lax.ppermute(spectrum, "comp", swap)
    courant_oth = lax.ppermute(courant, "comp", swap)
    stokes_proj = jnp.transpose(stokes_proj, (0, 2, 1))
    token_type = jax.ShapeDtypeStruct((8, CHUNK), F32)
    side_rows = bins // CHUNK * cells_y + EDGE * fields
    to_e, to_w, stokes_proj = call(
        outgoing_kernel,
        "outgoing",
        (message(side_rows),) * 2 + (jax.ShapeDtypeStruct(stokes_proj.shape, BF16),),
        [HBM] * 4,
        (VMEM,) * 3,
        [
            pltpu.VMEM(currents.shape, F32),
            pltpu.VMEM(sea_mask.shape, jnp.int32),
            DMA((3,)),
            DMA((2, bins // CHUNK)),
        ],
        10**6,
        MIB,
        4,
    )(in_hbm(spectrum), in_hbm(currents), in_hbm(sea_mask), in_hbm(stokes_proj))
    west_own = lax.ppermute(to_e, "gx", east)
    east_own = lax.ppermute(to_w, "gx", west)

    edge_rows = fields + bins // CHUNK * cells_x
    s_main, s_aux, s_edge, state, to_a, to_b, token = call(
        project_kernel,
        "project",
        (
            jax.ShapeDtypeStruct((cells_x + 2, chans, cells_y), F32),
            jax.ShapeDtypeStruct((cells_x, chans, cells_y), F32),
            jax.ShapeDtypeStruct((2 * EDGE, chans, 2 * cells_y), F32),
            jax.ShapeDtypeStruct((cells_x, fields, cells_y), F32),
            message(edge_rows),
            message(edge_rows),
            token_type,
        ),
        [VMEM] * 7,
        (VMEM,) * 7,
        [
            pltpu.VMEM((cells_x, PARTS * chans, cells_y), F32),
            pltpu.VMEM((PARTS * chans, bins), BF16),
            pltpu.VMEM((PARTS * chans, bins), BF16),
        ],
        3 * 10**9,
        8 * MIB,
        8,
    )(
        spectrum, f_oth, courant, courant_oth, stokes_proj, currents, sea_mask
    )
    from_a = lax.ppermute(to_a, "gy", pairing("gy", 0))
    from_b = lax.ppermute(to_b, "gy", pairing("gy", 1))

    inner, outer = wave_groups(cells_x, cells_y, EARLY_PAIRS)
    wave_type = jax.ShapeDtypeStruct(spectrum.shape, BF16)

    def wave_scratch(groups):
        height = max(map(rows_of, groups)) + 2 * TILE_ROWS
        return [
            *[pltpu.VMEM((height, 2 * bins), BF16)] * 2,
            *[pltpu.VMEM((height, CHUNK), F32)] * 2,
            pltpu.VMEM((16, cells_y + 16, CHUNK), F32),
        ]

    wave, inter, token = call(
        functools.partial(inner_kernel, inner),
        "inner",
        (wave_type, jax.ShapeDtypeStruct((2 * bins, bins), BF16), token_type),
        [VMEM] * 5 + [HBM, VMEM],
        (VMEM,) * 3,
        [*wave_scratch(inner), DMA((2,))],
        2 * 10**9,
        5 * MIB,
        20,
    )(spectrum, f_oth, courant, courant_oth, sea_mask, in_hbm(interaction), token)

    to_e, to_w, sides_own = call(
        functools.partial(relay_kernel, cells_x),
        "relay",
        (message(EDGE * chans + fields),) * 2
        + (message(2 * bins // CHUNK * (cells_y + cells_x)),),
        [VMEM] * 6,
        (VMEM,) * 3,
        [],
        10**6,
        MIB,
        4,
    )(s_edge, from_a, from_b, west_own, east_own, token)
    sides_oth = lax.ppermute(sides_own, "comp", swap)
    from_w = lax.ppermute(to_e, "gx", east)
    from_e = lax.ppermute(to_w, "gx", west)

    wave_out, token = call(
        functools.partial(outer_kernel, outer, inner),
        "outer",
        (wave_type, token_type),
        [VMEM] * 9,
        (HBM, VMEM),
        [
            pltpu.VMEM(spectrum.shape, BF16),
            *wave_scratch(outer),
            DMA((sum(map(len, outer)) + 3 * sum(map(len, inner)),)),
        ],
        2 * 10**9,
        5 * MIB,
        20,
    )(
        spectrum, f_oth, courant, courant_oth, sea_mask, inter, sides_own, sides_oth, wave
    )
    currents_out = call(
        momentum_kernel,
        "momentum",
        jax.ShapeDtypeStruct(currents.shape, F32),
        [VMEM] * 10 + [SMEM],
        HBM,
        [
            pltpu.VMEM((cells_x + 2 * SUBSTEPS, fields, 2 * cells_y), F32),
            pltpu.VMEM((cells_x + 2 * SUBSTEPS, chans, 2 * cells_y), F32),
            pltpu.VMEM((cells_x + 2 * SUBSTEPS - 2, chans, 2 * cells_y), F32),
            pltpu.VMEM(currents.shape, F32),
            DMA((cells_x // TILE,)),
        ],
        10**8,
        4 * MIB,
        10,
    )(
        s_main, s_aux, state, west_own, east_own, from_a, from_b, from_w, from_e, token,
        level_drag,
    )
    return (wave_out, currents_out)


def solution(mesh):
    in_specs = (
        P("gx", "gy", "comp"),
        P("gx", "gy"),
        P(None, "comp"),
        P(),
        P(),
        P(None, "comp", "gx", "gy"),
        P("comp"),
    )
    out_specs = (P("gx", "gy", "comp"), P(None, "comp", "gx", "gy"))
    return jax.shard_map(local, mesh=mesh, in_specs=in_specs, out_specs=out_specs, check_vma=False)
```

```python
import functools

import jax
import jax.numpy as jnp
from jax import lax
from jax.experimental import pallas as pl
from jax.experimental.pallas import tpu as pltpu
from jax.sharding import PartitionSpec as P

SUBSTEPS = 3

time_step = 0.5
viscosity = 0.4

F32 = jnp.float32
BF16 = jnp.bfloat16
MIB = 1 << 20
EDGE = 3
MASK_ROWS = 16
SLOT = 8
CHUNK = 128
TILE_ROWS = 16
EARLY_PAIRS = 3
SEAM_GROUP = 1
TILE = 8
PARTS = 5


def ring(axis):
    count = lax.axis_size(axis)
    forward = [(i, (i + 1) % count) for i in range(count)]
    return forward, [(target, source) for source, target in forward]


def pairing(axis, first, periodic=False):
    count = lax.axis_size(axis)
    swaps = [(i, (i + 1) % count) for i in range(first, count if periodic else count - 1, 2)]
    return swaps + [(target, source) for source, target in swaps]


def lane_of(rows, width):
    return lax.broadcasted_iota(jnp.int32, (rows, width), 1)


def between(lane, low, high):
    return (lane >= low) & (lane < high)


def chunks_of(bins):
    return [slice(j * CHUNK, (j + 1) * CHUNK) for j in range(bins // CHUNK)]


def sea_row(mask, x, rows):
    return jnp.broadcast_to(mask[x : x + 1, :].astype(F32), (rows, mask.shape[1]))


def outgoing_kernel(
    spectrum, currents, mask_in, proj_in,
    msg_e, msg_w, proj,
    cur, mask, sem, row_sem,
):
    cells_x, width, bins = spectrum.shape
    levels = cur.shape[1]
    chans = 2 * levels
    fields = chans + MASK_ROWS
    copies = [
        pltpu.make_async_copy(currents, cur, sem.at[0]),
        pltpu.make_async_copy(mask_in, mask, sem.at[1]),
    ]
    proj_copy = pltpu.make_async_copy(proj_in, proj, sem.at[2])
    for side, (msg, x) in enumerate(((msg_e, cells_x - 1), (msg_w, 0))):
        for j, cols in enumerate(chunks_of(bins)):
            copies.append(
                pltpu.make_async_copy(
                    spectrum.at[x, :, cols], msg.at[pl.ds(j * width, width), :], row_sem.at[side, j]
                )
            )
    for copy in (*copies, proj_copy):
        copy.start()
    copies[0].wait()
    copies[1].wait()
    base = bins // CHUNK * width
    for msg, first in ((msg_e, cells_x - EDGE), (msg_w, 0)):
        for i in range(EDGE):
            x = first + i
            at = base + i * fields
            for c in range(2):
                msg[at + c * levels : at + (c + 1) * levels] = cur[c, :, x, :].astype(BF16)
            msg[at + chans : at + fields] = sea_row(mask, x, MASK_ROWS).astype(BF16)
    for copy in (*copies[2:], proj_copy):
        copy.wait()


def stokes_weights(proj, courant, core, owner, weights):
    levels = proj.shape[1] // 2
    bins = courant.shape[1]
    bins_at = pl.ds(pl.multiple_of(owner * bins, bins), bins)
    cour_x, cour_y = courant[0:1, :], courant[1:2, :]
    terms = (
        1.0 - jnp.abs(cour_x) - jnp.abs(cour_y),
        jnp.maximum(cour_x, 0.0),
        -jnp.minimum(cour_x, 0.0),
        jnp.maximum(cour_y, 0.0),
        -jnp.minimum(cour_y, 0.0),
    )
    for c in range(2):
        mine = proj[c, pl.ds(pl.multiple_of(core * levels, levels), levels), bins_at].astype(F32)
        for k, term in enumerate(terms):
            row = (2 * k + c) * levels
            weights[row : row + levels] = (mine * term).astype(BF16)


def project_kernel(
    f_own, f_oth, courant_own, courant_oth, stokes_proj, currents, mask,
    s_main, s_aux, s_edge, state, msg_a, msg_b, token,
    proj, wt_own, wt_oth,
):
    cells_x, width, bins = f_own.shape
    chans = s_main.shape[1]
    fields = chans + MASK_ROWS
    core = lax.axis_index("comp")
    token[...] = jnp.zeros_like(token)
    stokes_weights(stokes_proj, courant_own, core, core, wt_own)
    stokes_weights(stokes_proj, courant_oth, core, 1 - core, wt_oth)
    contract = (((1,), (1,)), ((), ()))
    for pair in range(cells_x // 2):
        both = 0.0
        for wt, f in ((wt_own, f_own), (wt_oth, f_oth)):
            cells = f[2 * pair : 2 * pair + 2].reshape(2 * width, bins)
            both += lax.dot_general(wt[...], cells, contract, preferred_element_type=F32)
        proj[2 * pair] = both[:, :width]
        proj[2 * pair + 1] = both[:, width:]
    lane = lane_of(chans, width)
    lane_f = lane_of(fields, width)

    def part(x, which):
        return proj[x, which * chans : (which + 1) * chans, :]

    pack_n = pack_s = jnp.zeros((chans, width), F32)
    cur_n = cur_s = jnp.zeros((fields, width), F32)
    for x in range(-1, cells_x + 1):
        start = stokes_lane(x)
        main = jnp.zeros((chans, width), F32)
        aux = jnp.zeros((chans, width), F32)
        if 0 <= x < cells_x:
            south = pltpu.roll(part(x, 3), 1, 1)
            north = pltpu.roll(part(x, 4), width - 1, 1)
            main = part(x, 0) + jnp.where(lane > 0, south, 0.0) + jnp.where(lane < width - 1, north, 0.0)
            aux = jnp.where(lane == 0, south, jnp.where(lane == width - 1, north, 0.0))
            s_aux[x] = aux
        if x >= 1:
            main += part(x - 1, 1)
        if x <= cells_x - 2:
            main += part(x + 1, 2)
        s_main[x + 1] = main
        if x < EDGE - 1 or x > cells_x - EDGE:
            at = x + 1 if x < EDGE - 1 else x - (cells_x - 2) + EDGE
            s_edge[at, :, :width] = main
            s_edge[at, :, width:] = aux
        window = between(lane, start, start + 4)
        ring_n = pltpu.roll(jnp.where(lane == 0, aux, main), (3 + start) % width, 1)
        ring_s = pltpu.roll(jnp.where(lane == width - 1, aux, main), (1 + start) % width, 1)
        pack_n = jnp.where(window, ring_n, pack_n)
        pack_s = jnp.where(window, ring_s, pack_s)
        if 0 <= x < cells_x:
            row = jnp.concatenate(
                [currents[0, :, x, :], currents[1, :, x, :], sea_row(mask, x, MASK_ROWS)], 0
            )
            state[x] = row
            start = current_lane(x, cells_x)
            window = between(lane_f, start, start + 3)
            cur_n = jnp.where(window, pltpu.roll(row, (3 + start) % width, 1), cur_n)
            cur_s = jnp.where(window, pltpu.roll(row, start, 1), cur_s)
    even = is_even("gy")
    for msg, north_first in ((msg_a, even), (msg_b, ~even)):
        pack, cur_pack = jnp.where(north_first, pack_n, pack_s), jnp.where(north_first, cur_n, cur_s)
        msg[:chans] = (pack + cur_pack[:chans]).astype(BF16)
        msg[chans:fields] = cur_pack[chans:].astype(BF16)
    for j, cols in enumerate(chunks_of(bins)):
        high = [f_own[x, width - 16 :, cols].astype(F32)[15:] for x in range(cells_x)]
        low = [f_own[x, :16, cols].astype(F32)[:1] for x in range(cells_x)]
        high, low = jnp.concatenate(high, 0), jnp.concatenate(low, 0)
        base = fields + j * cells_x
        msg_a[base : base + cells_x] = jnp.where(even, high, low).astype(BF16)
        msg_b[base : base + cells_x] = jnp.where(even, low, high).astype(BF16)


def is_even(axis):
    return lax.rem(lax.axis_index(axis), 2) == 0


def from_sides(from_a, from_b, rows, axis="gy"):
    even = is_even(axis)
    a, b = from_a[rows].astype(F32), from_b[rows].astype(F32)
    return jnp.where(even, b, a), jnp.where(even, a, b)


def stokes_lane(x):
    return 4 * (x + 1)


def current_lane(x, cells_x):
    return 4 * (cells_x + 2) + 3 * x


def current_halo(tile_s, tile_n, x, cells_x, lane, width):
    start = current_lane(x, cells_x)
    low = pltpu.roll(tile_s, (-start - 3) % width, 1)
    return halo_lanes(lane, low, pltpu.roll(tile_n, (-start) % width, 1), width)


def southern(tile, start, width):
    return pltpu.roll(tile, (-start - 3) % width, 1)


def northern(tile, start, width):
    return pltpu.roll(tile, (-start - 1) % width, 1)


def halo_lanes(lane, low, high, width):
    return jnp.where(lane >= width - 3, low, jnp.where(lane < 3, high, 0.0))


def stokes_row(main, aux, pack_s, pack_n, start, lane, width):
    low = southern(pack_s, start, width)
    high = northern(pack_n, start, width)
    main = main + jnp.where(lane == 0, low, 0.0) + jnp.where(lane == width - 1, high, 0.0)
    return main, aux + halo_lanes(lane, low, high, width)


def relay_kernel(cells_x, s_edge, from_a, from_b, side_w, side_e, token, msg_b, msg_a, spectra):
    del token
    chans, width = s_edge.shape[1], s_edge.shape[2] // 2
    fields = chans + MASK_ROWS
    rows, edges = side_w.shape[0] - EDGE * fields, from_a.shape[0] - fields
    spectra[:rows] = side_w[:rows]
    spectra[rows : 2 * rows] = side_e[:rows]
    spectra[2 * rows : 2 * rows + edges] = from_a[fields:]
    spectra[2 * rows + edges :] = from_b[fields:]
    half = width // 2
    lane = lane_of(chans, width)
    lane_f = lane_of(fields, width)
    tile_s, tile_n = from_sides(from_a, from_b, slice(0, fields))
    def build(east, west):
        for msg, first, first_cur, first_edge in (
            (east, cells_x - 2, cells_x - EDGE, EDGE),
            (west, -1, 0, 0),
        ):
            tile = jnp.zeros((chans, width), F32)
            cur_tile = jnp.zeros((fields, width), F32)
            for i in range(EDGE):
                edge = s_edge[first_edge + i]
                start = stokes_lane(first + i)
                main, aux = stokes_row(
                    edge[:, :width], edge[:, width:], tile_s[:chans], tile_n[:chans], start, lane, width
                )
                msg[i * chans : (i + 1) * chans] = main.astype(BF16)
                at = SLOT * i
                tile = jnp.where(between(lane, at, at + 6), pltpu.roll(aux, at + 3, 1), tile)
                ring = current_halo(tile_s, tile_n, first_cur + i, cells_x, lane_f, width)
                at += half
                cur_tile = jnp.where(between(lane_f, at, at + 6), pltpu.roll(ring, at + 3, 1), cur_tile)
            base = EDGE * chans
            msg[base : base + chans] = (tile + cur_tile[:chans]).astype(BF16)
            msg[base + chans : base + fields] = cur_tile[chans:].astype(BF16)

    even = is_even("gx")
    pl.when(even)(functools.partial(build, msg_a, msg_b))
    pl.when(~even)(functools.partial(build, msg_b, msg_a))


def lat_coriolis(cells_y):
    ny_total = lax.axis_size("gy") * cells_y
    lane = lane_of(1, 2 * cells_y)
    lane = jnp.where(lane >= cells_y + cells_y // 2, lane - 2 * cells_y, lane)
    lat_index = lax.axis_index("gy") * cells_y + lane
    return jnp.sin(jnp.pi * ((lat_index.astype(F32) + 0.5) / ny_total - 0.5))


def momentum_kernel(
    s_main, s_aux, state, side_w, side_e, from_a, from_b, beside_b, beside_a, token, drag,
    out,
    flow_a, flow_b, stokes, result, sem,
):
    del token
    cells_x, chans, width = s_aux.shape
    fields = chans + MASK_ROWS
    levels = chans // 2
    half = width // 2
    lane = lane_of(chans, width)
    lane_f = lane_of(fields, width)
    side_base = side_w.shape[0] - EDGE * fields
    corner_w, corner_e = from_sides(beside_a, beside_b, slice(EDGE * chans, None), "gx")
    sums_w, sums_e = from_sides(beside_a, beside_b, slice(0, EDGE * chans), "gx")
    tile_s, tile_n = from_sides(from_a, from_b, slice(0, fields))

    def corner(tile, at, lanes):
        ring = pltpu.roll(tile, (-at - 3) % width, 1)
        return halo_lanes(lanes, ring, ring, width)

    for x in range(-SUBSTEPS, cells_x + SUBSTEPS):
        if 0 <= x < cells_x:
            flow_a[x + SUBSTEPS, :, :width] = state[x]
            aux = current_halo(tile_s, tile_n, x, cells_x, lane_f, width)
        else:
            side, tile, i = (side_w, corner_w, x + SUBSTEPS) if x < 0 else (side_e, corner_e, x - cells_x)
            at = side_base + i * fields
            flow_a[x + SUBSTEPS, :, :width] = side[at : at + fields].astype(F32)
            aux = corner(tile, half + SLOT * i, lane_f)
        flow_a[x + SUBSTEPS, :, width:] = aux

    margin = SUBSTEPS - 1
    for x in range(-margin, cells_x + margin):
        main = aux = 0.0
        if -1 <= x <= cells_x:
            own_aux = s_aux[x] if 0 <= x < cells_x else 0.0
            main, aux = stokes_row(
                s_main[x + 1], own_aux, tile_s[:chans], tile_n[:chans], stokes_lane(x), lane, width
            )
        for message, tile, first in ((sums_w, corner_w, -2), (sums_e, corner_e, cells_x - 1)):
            i = x - first
            if 0 <= i < EDGE:
                main += message[i * chans : (i + 1) * chans]
                aux += corner(tile[:chans], SLOT * i, lane)
        sea = flow_a[x + SUBSTEPS, chans : chans + 1, :]
        stokes[x + margin, :, :width] = main * sea[:, :width]
        stokes[x + margin, :, width:] = aux * sea[:, width:]

    at_level = lax.broadcasted_iota(jnp.int32, (levels, 1), 0)
    drag_col = jnp.zeros((levels, 1), F32)
    for level in range(levels):
        drag_col = jnp.where(at_level == level, drag[level], drag_col)
    def copy_out(block):
        rows = pl.ds(block * TILE, TILE)
        return pltpu.make_async_copy(
            result.at[:, :, rows, :], out.at[:, :, rows, :], sem.at[block]
        )

    half_cor = time_step * lat_coriolis(width)
    keep = 1.0 - 4.0 * time_step * viscosity - time_step * drag_col
    ring = 2 * width
    source, target = flow_a, flow_b
    for step in range(SUBSTEPS):
        margin = SUBSTEPS - 1 - step
        last = step == SUBSTEPS - 1
        for x in range(-margin, cells_x + margin):
            at = x + SUBSTEPS
            u, v = source[at, :levels], source[at, levels:chans]
            u_w, v_w = source[at - 1, :levels], source[at - 1, levels:chans]
            u_e, v_e = source[at + 1, :levels], source[at + 1, levels:chans]
            u_s, v_s = pltpu.roll(u, 1, 1), pltpu.roll(v, 1, 1)
            u_n, v_n = pltpu.roll(u, ring - 1, 1), pltpu.roll(v, ring - 1, 1)
            drift = stokes[x + SUBSTEPS - 1]
            if last:
                u, v, u_w, v_w, u_e, v_e, u_s, v_s, u_n, v_n, drift = (
                    field[:, :width] for field in (u, v, u_w, v_w, u_e, v_e, u_s, v_s, u_n, v_n, drift)
                )
            lanes = u.shape[1]
            spin = half_cor[:, :lanes] + 0.5 * time_step * ((v_e - v_w) - (u_n - u_s))
            sea = flow_a[at, chans : chans + 1, :lanes]
            u_new = keep * u + spin * (v + drift[levels:])
            v_new = keep * v - spin * (u + drift[:levels])
            u_new = sea * (u_new + time_step * viscosity * ((u_e + u_w) + (u_n + u_s)))
            v_new = sea * (v_new + time_step * viscosity * ((v_e + v_w) + (v_n + v_s)))
            if last:
                result[0, :, x, :] = u_new
                result[1, :, x, :] = v_new
                if x % TILE == TILE - 1:
                    copy_out(x // TILE).start()
            else:
                target[at, :levels] = u_new
                target[at, levels:chans] = v_new
        source, target = target, source
    for block in range(cells_x // TILE):
        copy_out(block).wait()


def wave_groups(cells_x, width, early_pairs):
    early = 1 + 2 * early_pairs
    inner = [[(x, 0, width), (x + 1, 0, width)] for x in range(1, early, 2)]
    outer = [[(0, 0, width), (cells_x - 1, 0, width)]]
    for x in range(early, cells_x - 1, 2):
        outer.append([(i, 0, width) for i in range(x, min(x + 2, cells_x - 1))])
    return inner, outer


def rows_of(group):
    return sum(last - first for _, first, last in group)


def wave_body(
    groups, sides, seam, wave, arriving,
    f_own, f_oth, courant_own, courant_oth, mask, inter,
    slots, send,
    adv, sea, moved,
):
    cells_x, width, bins = f_own.shape
    even = is_even("gy")
    per_core = bins // CHUNK
    halves = []
    for rows, side, courant in zip((f_own, f_oth), sides, (courant_own, courant_oth), strict=True):
        for j, cols in enumerate(chunks_of(bins)):
            cour_x, cour_y = courant[0:1, cols], courant[1:2, cols]
            size_x, size_y = jnp.abs(cour_x), jnp.abs(cour_y)
            south = north = None
            if side is not None:
                base = 2 * per_core * width + j * cells_x
                edge_a = side[base : base + cells_x].astype(F32)
                base += per_core * cells_x
                edge_b = side[base : base + cells_x].astype(F32)
                south, north = jnp.where(even, edge_b, edge_a), jnp.where(even, edge_a, edge_b)
            halves.append(
                (
                    rows, side, j, cols, south, north,
                    1.0 - size_x - size_y, size_x, size_y, cour_x > 0.0, cour_y > 0.0,
                )
            )

    def cell(rows, side, j, cols, x, first, last):
        if 0 <= x < cells_x:
            return rows[x, first:last, cols].astype(F32)
        base = (0 if x < 0 else per_core * width) + j * width
        return side[base + first : base + last].astype(F32)

    def advect(at, n):
        rows, side, j, cols, south, north, c_mid, c_x, c_y, up_x, up_y = halves[n]
        row = 0
        for i, (x, first, last) in enumerate(groups[at]):
            mid = cell(rows, side, j, cols, x, first, last)
            shifted = moved.at[(len(groups[at]) * n + i) % moved.shape[0]]
            shifted[8 + first : 8 + last] = mid
            none = jnp.zeros((1, CHUNK), F32)
            shifted[7:8] = none if south is None else south[x : x + 1]
            shifted[8 + width : 9 + width] = none if north is None else north[x : x + 1]
            low, high = shifted[7 + first : 7 + last], shifted[9 + first : 9 + last]
            west = cell(rows, side, j, cols, x - 1, first, last)
            east = cell(rows, side, j, cols, x + 1, first, last)
            value = c_mid * mid + c_x * jnp.where(up_x, west, east) + c_y * jnp.where(up_y, low, high)
            height = last - first
            adv[at % 2][row : row + height, n * CHUNK : (n + 1) * CHUNK] = value.astype(BF16)
            row += height

    def advect_seam(n):
        rows, _, _, cols, south, north, c_mid, c_x, c_y, up_x, up_y = halves[n]
        around = range(seam[0] - 1, seam[-1] + 2)
        own = slice(seam[0], seam[-1] + 1)
        row = rows_of(groups[SEAM_GROUP])
        for first, edge, beside in ((0, 0, 1), (width - TILE_ROWS, TILE_ROWS - 1, TILE_ROWS - 2)):
            tiles = [rows[x, first : first + TILE_ROWS, cols].astype(F32) for x in around]
            line = jnp.concatenate([tile[edge : edge + 1] for tile in tiles], 0)
            inward = jnp.concatenate([tile[beside : beside + 1] for tile in tiles[1:-1]], 0)
            low, high = (south[own], inward) if first == 0 else (inward, north[own])
            value = (
                c_mid * line[1:-1]
                + c_x * jnp.where(up_x, line[:-2], line[2:])
                + c_y * jnp.where(up_y, low, high)
            )
            value = jnp.concatenate([value, jnp.zeros((TILE_ROWS - len(seam), CHUNK), F32)], 0)
            adv[SEAM_GROUP % 2][row : row + TILE_ROWS, n * CHUNK : (n + 1) * CHUNK] = value.astype(BF16)
            row += TILE_ROWS

    def height_of(at):
        return rows_of(groups[at]) + (2 * TILE_ROWS if seam and at == SEAM_GROUP else 0)

    def put_sea(at):
        row = 0
        for x, first, last in groups[at]:
            column = jnp.transpose(sea_row(mask, x, CHUNK))
            sea[at % 2][row : row + last - first] = column[first:last]
            row += last - first
        if seam and at == SEAM_GROUP:
            for lat in (0, width - 1):
                column = mask[seam[0] : seam[-1] + 1, lat : lat + 1].astype(F32)
                column = jnp.concatenate([column, jnp.zeros((TILE_ROWS - len(seam), 1), F32)], 0)
                sea[at % 2][row : row + TILE_ROWS] = jnp.broadcast_to(column, (TILE_ROWS, CHUNK))
                row += TILE_ROWS

    def finish(at, piece):
        done, mine = adv[at % 2], sea[at % 2]
        half, block = piece // blocks, piece % blocks
        middle = height_of(at) // 2 // TILE_ROWS * TILE_ROWS
        low, high = (0, middle) if half == 0 else (middle, height_of(at))
        cols = slice(block * bins // blocks, (block + 1) * bins // blocks)
        gain = jnp.dot(done[low:high, :], inter[:, cols], preferred_element_type=F32)
        row = 0
        for x, first, last in groups[at]:
            begin, end = max(low, row), min(high, row + last - first)
            if begin < end:
                lats = slice(first + begin - row, first + end - row)
                for c in chunks_of(bins // blocks):
                    own = slice(cols.start + c.start, cols.start + c.stop)
                    total = done[begin:end, own].astype(F32) + gain[begin - low : end - low, c]
                    slots[x, lats, own] = (total * mine[begin:end]).astype(BF16)
            row += last - first
        if seam and at == SEAM_GROUP and half == 1:
            at_row = lax.broadcasted_iota(jnp.int32, (TILE_ROWS, CHUNK), 0)
            for first, edge in ((0, 0), (width - TILE_ROWS, TILE_ROWS - 1)):
                end = row + TILE_ROWS
                for c in chunks_of(bins // blocks):
                    own = slice(cols.start + c.start, cols.start + c.stop)
                    total = done[row:end, own].astype(F32) + gain[row - low : end - low, c]
                    total *= mine[row:end]
                    for i, x in enumerate(seam):
                        tile = wave[x, first : first + TILE_ROWS, own].astype(F32)
                        tile = jnp.where(at_row == edge, total[i : i + 1], tile)
                        slots[x, first : first + TILE_ROWS, own] = tile.astype(BF16)
                row = end

    blocks = 2
    pieces = 2 * blocks
    parts = len(halves)
    for n in range(parts):
        advect(0, n)
    for copy in arriving:
        copy.wait()
    for at in range(1, len(groups) + 1):
        put_sea(at - 1)
        for piece in range(pieces):
            if at < len(groups):
                for n in range(piece * parts // pieces, (piece + 1) * parts // pieces):
                    advect(at, n)
                    if seam and at == SEAM_GROUP:
                        advect_seam(n)
            finish(at - 1, piece)
        send(at - 1)


def inner_kernel(
    groups,
    f_own, f_oth, courant_own, courant_oth, mask, interaction, token_in,
    wave, inter, token,
    adv_a, adv_b, sea_a, sea_b, moved, inter_sem,
):
    token[...] = token_in[...]
    bins = f_own.shape[2]
    core = lax.axis_index("comp")
    own_at, oth_at = pl.multiple_of(core * bins, bins), pl.multiple_of((1 - core) * bins, bins)
    inter_copies = [
        pltpu.make_async_copy(
            interaction.at[pl.ds(at, bins), pl.ds(own_at, bins)],
            inter.at[pl.ds(n * bins, bins)],
            inter_sem.at[n],
        )
        for n, at in enumerate((own_at, oth_at))
    ]
    for copy in inter_copies:
        copy.start()
    wave_body(
        groups, (None, None), (), None, inter_copies,
        f_own, f_oth, courant_own, courant_oth, mask, inter,
        wave, lambda n: None,
        (adv_a, adv_b), (sea_a, sea_b), moved,
    )


def outer_kernel(
    groups, groups_before,
    f_own, f_oth, courant_own, courant_oth, mask, inter, sides_own, sides_oth, wave,
    out, token,
    slots, adv_a, adv_b, sea_a, sea_b, moved, out_sem,
):
    token[...] = jnp.zeros_like(token)
    copies = []

    def send(source, blocks):
        for x, first, last in blocks:
            lats = pl.ds(first, last - first)
            copies.append(
                pltpu.make_async_copy(source.at[x, lats], out.at[x, lats], out_sem.at[len(copies)])
            )
            copies[-1].start()

    seam = [x for group in groups_before for x, _, _ in group]
    width = wave.shape[1]
    send(wave, [(x, TILE_ROWS, width - TILE_ROWS) for x in seam])
    rims = [(0, TILE_ROWS), (width - TILE_ROWS, width)]

    def sent(n):
        send(slots, groups[n])
        if n == SEAM_GROUP:
            send(slots, [(x, first, last) for x in seam for first, last in rims])

    wave_body(
        groups, (sides_own, sides_oth), seam, wave, (),
        f_own, f_oth, courant_own, courant_oth, mask, inter,
        slots, sent,
        (adv_a, adv_b), (sea_a, sea_b), moved,
    )
    for copy in copies:
        copy.wait()


VMEM = pl.BlockSpec(memory_space=pltpu.VMEM)
SMEM = pl.BlockSpec(memory_space=pltpu.SMEM)
HBM = pl.BlockSpec(memory_space=pltpu.HBM)
DMA = pltpu.SemaphoreType.DMA


def in_hbm(array):
    return pltpu.with_memory_space_constraint(array, pltpu.HBM)


def call(kernel, name, out_shape, in_specs, out_specs, scratch, flops, traffic, limit):
    return pl.pallas_call(
        kernel,
        out_shape=out_shape,
        in_specs=in_specs,
        out_specs=out_specs,
        scratch_shapes=scratch,
        compiler_params=pltpu.CompilerParams(vmem_limit_bytes=limit * MIB),
        cost_estimate=pl.CostEstimate(flops=flops, bytes_accessed=traffic, transcendentals=0),
        name=name,
    )


def local(spectrum, sea_mask, courant, interaction, stokes_proj, currents, level_drag):
    cells_x, cells_y, bins = spectrum.shape
    levels = currents.shape[1]
    chans = 2 * levels
    fields = chans + MASK_ROWS
    swap = [(0, 1), (1, 0)]
    east, west = ring("gx")

    def message(rows):
        return jax.ShapeDtypeStruct((rows, cells_y), BF16)

    f_oth = lax.ppermute(spectrum, "comp", swap)
    courant_oth = lax.ppermute(courant, "comp", swap)
    stokes_proj = jnp.transpose(stokes_proj, (0, 2, 1))
    token_type = jax.ShapeDtypeStruct((8, CHUNK), F32)
    side_rows = bins // CHUNK * cells_y + EDGE * fields
    to_e, to_w, stokes_proj = call(
        outgoing_kernel,
        "outgoing",
        (message(side_rows),) * 2 + (jax.ShapeDtypeStruct(stokes_proj.shape, BF16),),
        [HBM] * 4,
        (VMEM,) * 3,
        [
            pltpu.VMEM(currents.shape, F32),
            pltpu.VMEM(sea_mask.shape, jnp.int32),
            DMA((3,)),
            DMA((2, bins // CHUNK)),
        ],
        10**6,
        MIB,
        4,
    )(in_hbm(spectrum), in_hbm(currents), in_hbm(sea_mask), in_hbm(stokes_proj))
    west_own = lax.ppermute(to_e, "gx", east)
    east_own = lax.ppermute(to_w, "gx", west)

    edge_rows = fields + bins // CHUNK * cells_x
    s_main, s_aux, s_edge, state, to_a, to_b, token = call(
        project_kernel,
        "project",
        (
            jax.ShapeDtypeStruct((cells_x + 2, chans, cells_y), F32),
            jax.ShapeDtypeStruct((cells_x, chans, cells_y), F32),
            jax.ShapeDtypeStruct((2 * EDGE, chans, 2 * cells_y), F32),
            jax.ShapeDtypeStruct((cells_x, fields, cells_y), F32),
            message(edge_rows),
            message(edge_rows),
            token_type,
        ),
        [VMEM] * 7,
        (VMEM,) * 7,
        [
            pltpu.VMEM((cells_x, PARTS * chans, cells_y), F32),
            pltpu.VMEM((PARTS * chans, bins), BF16),
            pltpu.VMEM((PARTS * chans, bins), BF16),
        ],
        3 * 10**9,
        8 * MIB,
        8,
    )(
        spectrum, f_oth, courant, courant_oth, stokes_proj, currents, sea_mask
    )
    from_a = lax.ppermute(to_a, "gy", pairing("gy", 0))
    from_b = lax.ppermute(to_b, "gy", pairing("gy", 1))

    inner, outer = wave_groups(cells_x, cells_y, EARLY_PAIRS)
    wave_type = jax.ShapeDtypeStruct(spectrum.shape, BF16)

    def wave_scratch(groups):
        height = max(map(rows_of, groups)) + 2 * TILE_ROWS
        return [
            *[pltpu.VMEM((height, 2 * bins), BF16)] * 2,
            *[pltpu.VMEM((height, CHUNK), F32)] * 2,
            pltpu.VMEM((16, cells_y + 16, CHUNK), F32),
        ]

    wave, inter, token = call(
        functools.partial(inner_kernel, inner),
        "inner",
        (wave_type, jax.ShapeDtypeStruct((2 * bins, bins), BF16), token_type),
        [VMEM] * 5 + [HBM, VMEM],
        (VMEM,) * 3,
        [*wave_scratch(inner), DMA((2,))],
        2 * 10**9,
        5 * MIB,
        20,
    )(spectrum, f_oth, courant, courant_oth, sea_mask, in_hbm(interaction), token)

    to_b, to_a, sides_own = call(
        functools.partial(relay_kernel, cells_x),
        "relay",
        (message(EDGE * chans + fields),) * 2
        + (message(2 * bins // CHUNK * (cells_y + cells_x)),),
        [VMEM] * 6,
        (VMEM,) * 3,
        [],
        10**6,
        MIB,
        4,
    )(s_edge, from_a, from_b, west_own, east_own, token)
    sides_oth = lax.ppermute(sides_own, "comp", swap)
    beside_b = lax.ppermute(to_b, "gx", pairing("gx", 1, True))
    beside_a = lax.ppermute(to_a, "gx", pairing("gx", 0, True))

    wave_out, token = call(
        functools.partial(outer_kernel, outer, inner),
        "outer",
        (wave_type, token_type),
        [VMEM] * 9,
        (HBM, VMEM),
        [
            pltpu.VMEM(spectrum.shape, BF16),
            *wave_scratch(outer),
            DMA((sum(map(len, outer)) + 3 * sum(map(len, inner)),)),
        ],
        2 * 10**9,
        5 * MIB,
        20,
    )(
        spectrum, f_oth, courant, courant_oth, sea_mask, inter, sides_own, sides_oth, wave
    )
    currents_out = call(
        momentum_kernel,
        "momentum",
        jax.ShapeDtypeStruct(currents.shape, F32),
        [VMEM] * 10 + [SMEM],
        HBM,
        [
            pltpu.VMEM((cells_x + 2 * SUBSTEPS, fields, 2 * cells_y), F32),
            pltpu.VMEM((cells_x + 2 * SUBSTEPS, chans, 2 * cells_y), F32),
            pltpu.VMEM((cells_x + 2 * SUBSTEPS - 2, chans, 2 * cells_y), F32),
            pltpu.VMEM(currents.shape, F32),
            DMA((cells_x // TILE,)),
        ],
        10**8,
        4 * MIB,
        10,
    )(
        s_main, s_aux, state, west_own, east_own, from_a, from_b, beside_b, beside_a, token,
        level_drag,
    )
    return (wave_out, currents_out)


def solution(mesh):
    in_specs = (
        P("gx", "gy", "comp"),
        P("gx", "gy"),
        P(None, "comp"),
        P(),
        P(),
        P(None, "comp", "gx", "gy"),
        P("comp"),
    )
    out_specs = (P("gx", "gy", "comp"), P(None, "comp", "gx", "gy"))
    return jax.shard_map(local, mesh=mesh, in_specs=in_specs, out_specs=out_specs, check_vma=False)
```

```python
import functools

import jax
import jax.numpy as jnp
from jax import lax
from jax.experimental import pallas as pl
from jax.experimental.pallas import tpu as pltpu
from jax.sharding import PartitionSpec as P

SUBSTEPS = 3

time_step = 0.5
viscosity = 0.4

F32 = jnp.float32
BF16 = jnp.bfloat16
MIB = 1 << 20
EDGE = 3
MASK_ROWS = 16
SLOT = 8
CHUNK = 128
TILE_ROWS = 16
EARLY_PAIRS = 3
SEAM_GROUP = 1
TILE = 8
PARTS = 5


def ring(axis):
    count = lax.axis_size(axis)
    forward = [(i, (i + 1) % count) for i in range(count)]
    return forward, [(target, source) for source, target in forward]


def pairing(axis, first, periodic=False):
    count = lax.axis_size(axis)
    swaps = [(i, (i + 1) % count) for i in range(first, count if periodic else count - 1, 2)]
    return swaps + [(target, source) for source, target in swaps]


def lane_of(rows, width):
    return lax.broadcasted_iota(jnp.int32, (rows, width), 1)


def between(lane, low, high):
    return (lane >= low) & (lane < high)


def chunks_of(bins):
    return [slice(j * CHUNK, (j + 1) * CHUNK) for j in range(bins // CHUNK)]


def sea_row(mask, x, rows):
    return jnp.broadcast_to(mask[x : x + 1, :].astype(F32), (rows, mask.shape[1]))


def outgoing_kernel(
    spectrum, currents, mask_in, proj_in,
    msg_e, msg_w, proj,
    cur, mask, sem, row_sem,
):
    cells_x, width, bins = spectrum.shape
    levels = cur.shape[1]
    chans = 2 * levels
    fields = chans + MASK_ROWS
    copies = [
        pltpu.make_async_copy(currents, cur, sem.at[0]),
        pltpu.make_async_copy(mask_in, mask, sem.at[1]),
    ]
    proj_copy = pltpu.make_async_copy(proj_in, proj, sem.at[2])
    for side, (msg, x) in enumerate(((msg_e, cells_x - 1), (msg_w, 0))):
        for j, cols in enumerate(chunks_of(bins)):
            copies.append(
                pltpu.make_async_copy(
                    spectrum.at[x, :, cols], msg.at[pl.ds(j * width, width), :], row_sem.at[side, j]
                )
            )
    for copy in (*copies, proj_copy):
        copy.start()
    copies[0].wait()
    copies[1].wait()
    base = bins // CHUNK * width
    for msg, first in ((msg_e, cells_x - EDGE), (msg_w, 0)):
        for i in range(EDGE):
            x = first + i
            at = base + i * fields
            for c in range(2):
                msg[at + c * levels : at + (c + 1) * levels] = cur[c, :, x, :].astype(BF16)
            msg[at + chans : at + fields] = sea_row(mask, x, MASK_ROWS).astype(BF16)
    for copy in (*copies[2:], proj_copy):
        copy.wait()


def stokes_weights(proj, courant, core, owner, weights):
    levels = proj.shape[1] // 2
    bins = courant.shape[1]
    bins_at = pl.ds(pl.multiple_of(owner * bins, bins), bins)
    cour_x, cour_y = courant[0:1, :], courant[1:2, :]
    terms = (
        1.0 - jnp.abs(cour_x) - jnp.abs(cour_y),
        jnp.maximum(cour_x, 0.0),
        -jnp.minimum(cour_x, 0.0),
        jnp.maximum(cour_y, 0.0),
        -jnp.minimum(cour_y, 0.0),
    )
    for c in range(2):
        mine = proj[c, pl.ds(pl.multiple_of(core * levels, levels), levels), bins_at].astype(F32)
        for k, term in enumerate(terms):
            row = (2 * k + c) * levels
            weights[row : row + levels] = (mine * term).astype(BF16)


def project_kernel(
    f_own, f_oth, courant_own, courant_oth, stokes_proj, currents, mask,
    s_main, s_aux, s_edge, state, msg_a, msg_b, token,
    proj, wt_own, wt_oth,
):
    cells_x, width, bins = f_own.shape
    chans = s_main.shape[1]
    fields = chans + MASK_ROWS
    core = lax.axis_index("comp")
    token[...] = jnp.zeros_like(token)
    stokes_weights(stokes_proj, courant_own, core, core, wt_own)
    stokes_weights(stokes_proj, courant_oth, core, 1 - core, wt_oth)
    contract = (((1,), (1,)), ((), ()))
    for pair in range(cells_x // 2):
        both = 0.0
        for wt, f in ((wt_own, f_own), (wt_oth, f_oth)):
            cells = f[2 * pair : 2 * pair + 2].reshape(2 * width, bins)
            both += lax.dot_general(wt[...], cells, contract, preferred_element_type=F32)
        proj[2 * pair] = both[:, :width]
        proj[2 * pair + 1] = both[:, width:]
    lane = lane_of(chans, width)
    lane_f = lane_of(fields, width)

    def part(x, which):
        return proj[x, which * chans : (which + 1) * chans, :]

    pack_n = pack_s = jnp.zeros((chans, width), F32)
    cur_n = cur_s = jnp.zeros((fields, width), F32)
    for x in range(-1, cells_x + 1):
        start = stokes_lane(x)
        main = jnp.zeros((chans, width), F32)
        aux = jnp.zeros((chans, width), F32)
        if 0 <= x < cells_x:
            south = pltpu.roll(part(x, 3), 1, 1)
            north = pltpu.roll(part(x, 4), width - 1, 1)
            main = part(x, 0) + jnp.where(lane > 0, south, 0.0) + jnp.where(lane < width - 1, north, 0.0)
            aux = jnp.where(lane == 0, south, jnp.where(lane == width - 1, north, 0.0))
            s_aux[x] = aux
        if x >= 1:
            main += part(x - 1, 1)
        if x <= cells_x - 2:
            main += part(x + 1, 2)
        s_main[x + 1] = main
        if x < EDGE - 1 or x > cells_x - EDGE:
            at = x + 1 if x < EDGE - 1 else x - (cells_x - 2) + EDGE
            s_edge[at, :, :width] = main
            s_edge[at, :, width:] = aux
        window = between(lane, start, start + 4)
        ring_n = pltpu.roll(jnp.where(lane == 0, aux, main), (3 + start) % width, 1)
        ring_s = pltpu.roll(jnp.where(lane == width - 1, aux, main), (1 + start) % width, 1)
        pack_n = jnp.where(window, ring_n, pack_n)
        pack_s = jnp.where(window, ring_s, pack_s)
        if 0 <= x < cells_x:
            row = jnp.concatenate(
                [currents[0, :, x, :], currents[1, :, x, :], sea_row(mask, x, MASK_ROWS)], 0
            )
            state[x] = row
            start = current_lane(x, cells_x)
            window = between(lane_f, start, start + 3)
            cur_n = jnp.where(window, pltpu.roll(row, (3 + start) % width, 1), cur_n)
            cur_s = jnp.where(window, pltpu.roll(row, start, 1), cur_s)
    even = is_even("gy")
    for msg, north_first in ((msg_a, even), (msg_b, ~even)):
        pack, cur_pack = jnp.where(north_first, pack_n, pack_s), jnp.where(north_first, cur_n, cur_s)
        msg[:chans] = (pack + cur_pack[:chans]).astype(BF16)
        msg[chans:fields] = cur_pack[chans:].astype(BF16)
    for j, cols in enumerate(chunks_of(bins)):
        high = [f_own[x, width - 16 :, cols].astype(F32)[15:] for x in range(cells_x)]
        low = [f_own[x, :16, cols].astype(F32)[:1] for x in range(cells_x)]
        high, low = jnp.concatenate(high, 0), jnp.concatenate(low, 0)
        base = fields + j * cells_x
        msg_a[base : base + cells_x] = jnp.where(even, high, low).astype(BF16)
        msg_b[base : base + cells_x] = jnp.where(even, low, high).astype(BF16)


def is_even(axis):
    return lax.rem(lax.axis_index(axis), 2) == 0


def from_sides(from_a, from_b, rows, axis="gy"):
    even = is_even(axis)
    a, b = from_a[rows].astype(F32), from_b[rows].astype(F32)
    return jnp.where(even, b, a), jnp.where(even, a, b)


def stokes_lane(x):
    return 4 * (x + 1)


def current_lane(x, cells_x):
    return 4 * (cells_x + 2) + 3 * x


def current_halo(tile_s, tile_n, x, cells_x, lane, width):
    start = current_lane(x, cells_x)
    low = pltpu.roll(tile_s, (-start - 3) % width, 1)
    return halo_lanes(lane, low, pltpu.roll(tile_n, (-start) % width, 1), width)


def southern(tile, start, width):
    return pltpu.roll(tile, (-start - 3) % width, 1)


def northern(tile, start, width):
    return pltpu.roll(tile, (-start - 1) % width, 1)


def halo_lanes(lane, low, high, width):
    return jnp.where(lane >= width - 3, low, jnp.where(lane < 3, high, 0.0))


def stokes_row(main, aux, pack_s, pack_n, start, lane, width):
    low = southern(pack_s, start, width)
    high = northern(pack_n, start, width)
    main = main + jnp.where(lane == 0, low, 0.0) + jnp.where(lane == width - 1, high, 0.0)
    return main, aux + halo_lanes(lane, low, high, width)


def relay_kernel(cells_x, s_edge, from_a, from_b, side_w, side_e, token, msg_b, msg_a, spectra):
    del token
    chans, width = s_edge.shape[1], s_edge.shape[2] // 2
    fields = chans + MASK_ROWS
    rows, edges = side_w.shape[0] - EDGE * fields, from_a.shape[0] - fields
    spectra[:rows] = side_w[:rows]
    spectra[rows : 2 * rows] = side_e[:rows]
    spectra[2 * rows : 2 * rows + edges] = from_a[fields:]
    spectra[2 * rows + edges :] = from_b[fields:]
    half = width // 2
    lane = lane_of(chans, width)
    lane_f = lane_of(fields, width)
    tile_s, tile_n = from_sides(from_a, from_b, slice(0, fields))
    def build(east, west):
        for msg, first, first_cur, first_edge in (
            (east, cells_x - 2, cells_x - EDGE, EDGE),
            (west, -1, 0, 0),
        ):
            tile = jnp.zeros((chans, width), F32)
            cur_tile = jnp.zeros((fields, width), F32)
            for i in range(EDGE):
                edge = s_edge[first_edge + i]
                start = stokes_lane(first + i)
                main, aux = stokes_row(
                    edge[:, :width], edge[:, width:], tile_s[:chans], tile_n[:chans], start, lane, width
                )
                msg[i * chans : (i + 1) * chans] = main.astype(BF16)
                at = SLOT * i
                tile = jnp.where(between(lane, at, at + 6), pltpu.roll(aux, at + 3, 1), tile)
                ring = current_halo(tile_s, tile_n, first_cur + i, cells_x, lane_f, width)
                at += half
                cur_tile = jnp.where(between(lane_f, at, at + 6), pltpu.roll(ring, at + 3, 1), cur_tile)
            base = EDGE * chans
            msg[base : base + chans] = (tile + cur_tile[:chans]).astype(BF16)
            msg[base + chans : base + fields] = cur_tile[chans:].astype(BF16)

    even = is_even("gx")
    pl.when(even)(functools.partial(build, msg_a, msg_b))
    pl.when(~even)(functools.partial(build, msg_b, msg_a))


def lat_coriolis(cells_y):
    ny_total = lax.axis_size("gy") * cells_y
    lane = lane_of(1, 2 * cells_y)
    lane = jnp.where(lane >= cells_y + cells_y // 2, lane - 2 * cells_y, lane)
    lat_index = lax.axis_index("gy") * cells_y + lane
    return jnp.sin(jnp.pi * ((lat_index.astype(F32) + 0.5) / ny_total - 0.5))


def momentum_kernel(
    s_main, s_aux, state, side_w, side_e, from_a, from_b, beside_b, beside_a, token, drag,
    out,
    flow_a, flow_b, stokes, result, sem,
):
    del token
    cells_x, chans, width = s_aux.shape
    fields = chans + MASK_ROWS
    levels = chans // 2
    half = width // 2
    lane = lane_of(chans, width)
    lane_f = lane_of(fields, width)
    side_base = side_w.shape[0] - EDGE * fields
    corner_w, corner_e = from_sides(beside_a, beside_b, slice(EDGE * chans, None), "gx")
    sums_w, sums_e = from_sides(beside_a, beside_b, slice(0, EDGE * chans), "gx")
    tile_s, tile_n = from_sides(from_a, from_b, slice(0, fields))

    def corner(tile, at, lanes):
        ring = pltpu.roll(tile, (-at - 3) % width, 1)
        return halo_lanes(lanes, ring, ring, width)

    for x in range(-SUBSTEPS, cells_x + SUBSTEPS):
        if 0 <= x < cells_x:
            flow_a[x + SUBSTEPS, :, :width] = state[x]
            aux = current_halo(tile_s, tile_n, x, cells_x, lane_f, width)
        else:
            side, tile, i = (side_w, corner_w, x + SUBSTEPS) if x < 0 else (side_e, corner_e, x - cells_x)
            at = side_base + i * fields
            flow_a[x + SUBSTEPS, :, :width] = side[at : at + fields].astype(F32)
            aux = corner(tile, half + SLOT * i, lane_f)
        flow_a[x + SUBSTEPS, :, width:] = aux

    margin = SUBSTEPS - 1
    for x in range(-margin, cells_x + margin):
        main = aux = 0.0
        if -1 <= x <= cells_x:
            own_aux = s_aux[x] if 0 <= x < cells_x else 0.0
            main, aux = stokes_row(
                s_main[x + 1], own_aux, tile_s[:chans], tile_n[:chans], stokes_lane(x), lane, width
            )
        for message, tile, first in ((sums_w, corner_w, -2), (sums_e, corner_e, cells_x - 1)):
            i = x - first
            if 0 <= i < EDGE:
                main += message[i * chans : (i + 1) * chans]
                aux += corner(tile[:chans], SLOT * i, lane)
        sea = flow_a[x + SUBSTEPS, chans : chans + 1, :]
        stokes[x + margin, :, :width] = main * sea[:, :width]
        stokes[x + margin, :, width:] = aux * sea[:, width:]

    at_level = lax.broadcasted_iota(jnp.int32, (levels, 1), 0)
    drag_col = jnp.zeros((levels, 1), F32)
    for level in range(levels):
        drag_col = jnp.where(at_level == level, drag[level], drag_col)
    def copies_out(block):
        rows = pl.ds(block * TILE, TILE)
        return [
            pltpu.make_async_copy(
                result.at[c, some, rows, :], out.at[c, some, rows, :], sem.at[block, 2 * c + half]
            )
            for c in range(2)
            for half, some in enumerate((pl.ds(0, levels // 2), pl.ds(levels // 2, levels // 2)))
        ]

    half_cor = time_step * lat_coriolis(width)
    keep = 1.0 - 4.0 * time_step * viscosity - time_step * drag_col
    ring = 2 * width
    source, target = flow_a, flow_b
    for step in range(SUBSTEPS):
        margin = SUBSTEPS - 1 - step
        last = step == SUBSTEPS - 1
        for x in range(-margin, cells_x + margin):
            at = x + SUBSTEPS
            u, v = source[at, :levels], source[at, levels:chans]
            u_w, v_w = source[at - 1, :levels], source[at - 1, levels:chans]
            u_e, v_e = source[at + 1, :levels], source[at + 1, levels:chans]
            u_s, v_s = pltpu.roll(u, 1, 1), pltpu.roll(v, 1, 1)
            u_n, v_n = pltpu.roll(u, ring - 1, 1), pltpu.roll(v, ring - 1, 1)
            drift = stokes[x + SUBSTEPS - 1]
            if last:
                u, v, u_w, v_w, u_e, v_e, u_s, v_s, u_n, v_n, drift = (
                    field[:, :width] for field in (u, v, u_w, v_w, u_e, v_e, u_s, v_s, u_n, v_n, drift)
                )
            lanes = u.shape[1]
            spin = half_cor[:, :lanes] + 0.5 * time_step * ((v_e - v_w) - (u_n - u_s))
            sea = flow_a[at, chans : chans + 1, :lanes]
            u_new = keep * u + spin * (v + drift[levels:])
            v_new = keep * v - spin * (u + drift[:levels])
            u_new = sea * (u_new + time_step * viscosity * ((u_e + u_w) + (u_n + u_s)))
            v_new = sea * (v_new + time_step * viscosity * ((v_e + v_w) + (v_n + v_s)))
            if last:
                result[0, :, x, :] = u_new
                result[1, :, x, :] = v_new
                if x % TILE == TILE - 1:
                    for copy in copies_out(x // TILE):
                        copy.start()
            else:
                target[at, :levels] = u_new
                target[at, levels:chans] = v_new
        source, target = target, source
    for block in range(cells_x // TILE):
        for copy in copies_out(block):
            copy.wait()


def wave_groups(cells_x, width, early_pairs):
    early = 1 + 2 * early_pairs
    inner = [[(x, 0, width), (x + 1, 0, width)] for x in range(1, early, 2)]
    outer = [[(0, 0, width), (cells_x - 1, 0, width)]]
    for x in range(early, cells_x - 1, 2):
        outer.append([(i, 0, width) for i in range(x, min(x + 2, cells_x - 1))])
    return inner, outer


def rows_of(group):
    return sum(last - first for _, first, last in group)


def wave_body(
    groups, sides, seam, wave, arriving,
    f_own, f_oth, courant_own, courant_oth, mask, inter,
    slots, send,
    adv, sea, moved,
):
    cells_x, width, bins = f_own.shape
    even = is_even("gy")
    per_core = bins // CHUNK
    halves = []
    for rows, side, courant in zip((f_own, f_oth), sides, (courant_own, courant_oth), strict=True):
        for j, cols in enumerate(chunks_of(bins)):
            cour_x, cour_y = courant[0:1, cols], courant[1:2, cols]
            size_x, size_y = jnp.abs(cour_x), jnp.abs(cour_y)
            south = north = None
            if side is not None:
                base = 2 * per_core * width + j * cells_x
                edge_a = side[base : base + cells_x].astype(F32)
                base += per_core * cells_x
                edge_b = side[base : base + cells_x].astype(F32)
                south, north = jnp.where(even, edge_b, edge_a), jnp.where(even, edge_a, edge_b)
            halves.append(
                (
                    rows, side, j, cols, south, north,
                    1.0 - size_x - size_y, size_x, size_y, cour_x > 0.0, cour_y > 0.0,
                )
            )

    def cell(rows, side, j, cols, x, first, last):
        if 0 <= x < cells_x:
            return rows[x, first:last, cols].astype(F32)
        base = (0 if x < 0 else per_core * width) + j * width
        return side[base + first : base + last].astype(F32)

    def advect(at, n):
        rows, side, j, cols, south, north, c_mid, c_x, c_y, up_x, up_y = halves[n]
        row = 0
        for i, (x, first, last) in enumerate(groups[at]):
            mid = cell(rows, side, j, cols, x, first, last)
            shifted = moved.at[(len(groups[at]) * n + i) % moved.shape[0]]
            shifted[8 + first : 8 + last] = mid
            none = jnp.zeros((1, CHUNK), F32)
            shifted[7:8] = none if south is None else south[x : x + 1]
            shifted[8 + width : 9 + width] = none if north is None else north[x : x + 1]
            low, high = shifted[7 + first : 7 + last], shifted[9 + first : 9 + last]
            west = cell(rows, side, j, cols, x - 1, first, last)
            east = cell(rows, side, j, cols, x + 1, first, last)
            value = c_mid * mid + c_x * jnp.where(up_x, west, east) + c_y * jnp.where(up_y, low, high)
            height = last - first
            adv[at % 2][row : row + height, n * CHUNK : (n + 1) * CHUNK] = value.astype(BF16)
            row += height

    def advect_seam(n):
        rows, _, _, cols, south, north, c_mid, c_x, c_y, up_x, up_y = halves[n]
        around = range(seam[0] - 1, seam[-1] + 2)
        own = slice(seam[0], seam[-1] + 1)
        row = rows_of(groups[SEAM_GROUP])
        for first, edge, beside in ((0, 0, 1), (width - TILE_ROWS, TILE_ROWS - 1, TILE_ROWS - 2)):
            tiles = [rows[x, first : first + TILE_ROWS, cols].astype(F32) for x in around]
            line = jnp.concatenate([tile[edge : edge + 1] for tile in tiles], 0)
            inward = jnp.concatenate([tile[beside : beside + 1] for tile in tiles[1:-1]], 0)
            low, high = (south[own], inward) if first == 0 else (inward, north[own])
            value = (
                c_mid * line[1:-1]
                + c_x * jnp.where(up_x, line[:-2], line[2:])
                + c_y * jnp.where(up_y, low, high)
            )
            value = jnp.concatenate([value, jnp.zeros((TILE_ROWS - len(seam), CHUNK), F32)], 0)
            adv[SEAM_GROUP % 2][row : row + TILE_ROWS, n * CHUNK : (n + 1) * CHUNK] = value.astype(BF16)
            row += TILE_ROWS

    def height_of(at):
        return rows_of(groups[at]) + (2 * TILE_ROWS if seam and at == SEAM_GROUP else 0)

    def put_sea(at):
        row = 0
        for x, first, last in groups[at]:
            column = jnp.transpose(sea_row(mask, x, CHUNK))
            sea[at % 2][row : row + last - first] = column[first:last]
            row += last - first
        if seam and at == SEAM_GROUP:
            for lat in (0, width - 1):
                column = mask[seam[0] : seam[-1] + 1, lat : lat + 1].astype(F32)
                column = jnp.concatenate([column, jnp.zeros((TILE_ROWS - len(seam), 1), F32)], 0)
                sea[at % 2][row : row + TILE_ROWS] = jnp.broadcast_to(column, (TILE_ROWS, CHUNK))
                row += TILE_ROWS

    def finish(at, piece):
        done, mine = adv[at % 2], sea[at % 2]
        half, block = piece // blocks, piece % blocks
        middle = height_of(at) // 2 // TILE_ROWS * TILE_ROWS
        low, high = (0, middle) if half == 0 else (middle, height_of(at))
        cols = slice(block * bins // blocks, (block + 1) * bins // blocks)
        gain = jnp.dot(done[low:high, :], inter[:, cols], preferred_element_type=F32)
        row = 0
        for x, first, last in groups[at]:
            begin, end = max(low, row), min(high, row + last - first)
            if begin < end:
                lats = slice(first + begin - row, first + end - row)
                for c in chunks_of(bins // blocks):
                    own = slice(cols.start + c.start, cols.start + c.stop)
                    total = done[begin:end, own].astype(F32) + gain[begin - low : end - low, c]
                    slots[x, lats, own] = (total * mine[begin:end]).astype(BF16)
            row += last - first
        if seam and at == SEAM_GROUP and half == 1:
            at_row = lax.broadcasted_iota(jnp.int32, (TILE_ROWS, CHUNK), 0)
            for first, edge in ((0, 0), (width - TILE_ROWS, TILE_ROWS - 1)):
                end = row + TILE_ROWS
                for c in chunks_of(bins // blocks):
                    own = slice(cols.start + c.start, cols.start + c.stop)
                    total = done[row:end, own].astype(F32) + gain[row - low : end - low, c]
                    total *= mine[row:end]
                    for i, x in enumerate(seam):
                        tile = wave[x, first : first + TILE_ROWS, own].astype(F32)
                        tile = jnp.where(at_row == edge, total[i : i + 1], tile)
                        slots[x, first : first + TILE_ROWS, own] = tile.astype(BF16)
                row = end

    blocks = 2
    pieces = 2 * blocks
    parts = len(halves)
    for n in range(parts):
        advect(0, n)
    for copy in arriving:
        copy.wait()
    for at in range(1, len(groups) + 1):
        put_sea(at - 1)
        for piece in range(pieces):
            if at < len(groups):
                for n in range(piece * parts // pieces, (piece + 1) * parts // pieces):
                    advect(at, n)
                    if seam and at == SEAM_GROUP:
                        advect_seam(n)
            finish(at - 1, piece)
            if piece == blocks - 1 and height_of(at - 1) == rows_of(groups[at - 1]) == 2 * width:
                send(at - 1, 0)
        send(at - 1, 1)


def inner_kernel(
    groups,
    f_own, f_oth, courant_own, courant_oth, mask, interaction, token_in,
    wave, inter, token,
    adv_a, adv_b, sea_a, sea_b, moved, inter_sem,
):
    token[...] = token_in[...]
    bins = f_own.shape[2]
    core = lax.axis_index("comp")
    own_at, oth_at = pl.multiple_of(core * bins, bins), pl.multiple_of((1 - core) * bins, bins)
    inter_copies = [
        pltpu.make_async_copy(
            interaction.at[pl.ds(at, bins), pl.ds(own_at, bins)],
            inter.at[pl.ds(n * bins, bins)],
            inter_sem.at[n],
        )
        for n, at in enumerate((own_at, oth_at))
    ]
    for copy in inter_copies:
        copy.start()
    wave_body(
        groups, (None, None), (), None, inter_copies,
        f_own, f_oth, courant_own, courant_oth, mask, inter,
        wave, lambda n, part: None,
        (adv_a, adv_b), (sea_a, sea_b), moved,
    )


def outer_kernel(
    groups, groups_before,
    f_own, f_oth, courant_own, courant_oth, mask, inter, sides_own, sides_oth, wave,
    out, token,
    slots, adv_a, adv_b, sea_a, sea_b, moved, out_sem,
):
    token[...] = jnp.zeros_like(token)
    copies = []

    def send(source, blocks):
        for x, first, last in blocks:
            lats = pl.ds(first, last - first)
            copies.append(
                pltpu.make_async_copy(source.at[x, lats], out.at[x, lats], out_sem.at[len(copies)])
            )
            copies[-1].start()

    seam = [x for group in groups_before for x, _, _ in group]
    width = wave.shape[1]
    send(wave, [(x, TILE_ROWS, width - TILE_ROWS) for x in seam])
    rims = [(0, TILE_ROWS), (width - TILE_ROWS, width)]

    def sent(n, part):
        whole = n == SEAM_GROUP or len(groups[n]) == 1
        send(slots, groups[n] if whole else groups[n][part : part + 1])
        if n == SEAM_GROUP:
            send(slots, [(x, first, last) for x in seam for first, last in rims])

    wave_body(
        groups, (sides_own, sides_oth), seam, wave, (),
        f_own, f_oth, courant_own, courant_oth, mask, inter,
        slots, sent,
        (adv_a, adv_b), (sea_a, sea_b), moved,
    )
    for copy in copies:
        copy.wait()


VMEM = pl.BlockSpec(memory_space=pltpu.VMEM)
SMEM = pl.BlockSpec(memory_space=pltpu.SMEM)
HBM = pl.BlockSpec(memory_space=pltpu.HBM)
DMA = pltpu.SemaphoreType.DMA


def in_hbm(array):
    return pltpu.with_memory_space_constraint(array, pltpu.HBM)


def call(kernel, name, out_shape, in_specs, out_specs, scratch, flops, traffic, limit):
    return pl.pallas_call(
        kernel,
        out_shape=out_shape,
        in_specs=in_specs,
        out_specs=out_specs,
        scratch_shapes=scratch,
        compiler_params=pltpu.CompilerParams(vmem_limit_bytes=limit * MIB),
        cost_estimate=pl.CostEstimate(flops=flops, bytes_accessed=traffic, transcendentals=0),
        name=name,
    )


def local(spectrum, sea_mask, courant, interaction, stokes_proj, currents, level_drag):
    cells_x, cells_y, bins = spectrum.shape
    levels = currents.shape[1]
    chans = 2 * levels
    fields = chans + MASK_ROWS
    swap = [(0, 1), (1, 0)]
    east, west = ring("gx")

    def message(rows):
        return jax.ShapeDtypeStruct((rows, cells_y), BF16)

    f_oth = lax.ppermute(spectrum, "comp", swap)
    courant_oth = lax.ppermute(courant, "comp", swap)
    stokes_proj = jnp.transpose(stokes_proj, (0, 2, 1))
    token_type = jax.ShapeDtypeStruct((8, CHUNK), F32)
    side_rows = bins // CHUNK * cells_y + EDGE * fields
    to_e, to_w, stokes_proj = call(
        outgoing_kernel,
        "outgoing",
        (message(side_rows),) * 2 + (jax.ShapeDtypeStruct(stokes_proj.shape, BF16),),
        [HBM] * 4,
        (VMEM,) * 3,
        [
            pltpu.VMEM(currents.shape, F32),
            pltpu.VMEM(sea_mask.shape, jnp.int32),
            DMA((3,)),
            DMA((2, bins // CHUNK)),
        ],
        10**6,
        MIB,
        4,
    )(in_hbm(spectrum), in_hbm(currents), in_hbm(sea_mask), in_hbm(stokes_proj))
    west_own = lax.ppermute(to_e, "gx", east)
    east_own = lax.ppermute(to_w, "gx", west)

    edge_rows = fields + bins // CHUNK * cells_x
    s_main, s_aux, s_edge, state, to_a, to_b, token = call(
        project_kernel,
        "project",
        (
            jax.ShapeDtypeStruct((cells_x + 2, chans, cells_y), F32),
            jax.ShapeDtypeStruct((cells_x, chans, cells_y), F32),
            jax.ShapeDtypeStruct((2 * EDGE, chans, 2 * cells_y), F32),
            jax.ShapeDtypeStruct((cells_x, fields, cells_y), F32),
            message(edge_rows),
            message(edge_rows),
            token_type,
        ),
        [VMEM] * 7,
        (VMEM,) * 7,
        [
            pltpu.VMEM((cells_x, PARTS * chans, cells_y), F32),
            pltpu.VMEM((PARTS * chans, bins), BF16),
            pltpu.VMEM((PARTS * chans, bins), BF16),
        ],
        3 * 10**9,
        8 * MIB,
        8,
    )(
        spectrum, f_oth, courant, courant_oth, stokes_proj, currents, sea_mask
    )
    from_a = lax.ppermute(to_a, "gy", pairing("gy", 0))
    from_b = lax.ppermute(to_b, "gy", pairing("gy", 1))

    inner, outer = wave_groups(cells_x, cells_y, EARLY_PAIRS)
    wave_type = jax.ShapeDtypeStruct(spectrum.shape, BF16)

    def wave_scratch(groups):
        height = max(map(rows_of, groups)) + 2 * TILE_ROWS
        return [
            *[pltpu.VMEM((height, 2 * bins), BF16)] * 2,
            *[pltpu.VMEM((height, CHUNK), F32)] * 2,
            pltpu.VMEM((16, cells_y + 16, CHUNK), F32),
        ]

    wave, inter, token = call(
        functools.partial(inner_kernel, inner),
        "inner",
        (wave_type, jax.ShapeDtypeStruct((2 * bins, bins), BF16), token_type),
        [VMEM] * 5 + [HBM, VMEM],
        (VMEM,) * 3,
        [*wave_scratch(inner), DMA((2,))],
        2 * 10**9,
        5 * MIB,
        20,
    )(spectrum, f_oth, courant, courant_oth, sea_mask, in_hbm(interaction), token)

    to_b, to_a, sides_own = call(
        functools.partial(relay_kernel, cells_x),
        "relay",
        (message(EDGE * chans + fields),) * 2
        + (message(2 * bins // CHUNK * (cells_y + cells_x)),),
        [VMEM] * 6,
        (VMEM,) * 3,
        [],
        10**6,
        MIB,
        4,
    )(s_edge, from_a, from_b, west_own, east_own, token)
    sides_oth = lax.ppermute(sides_own, "comp", swap)
    beside_b = lax.ppermute(to_b, "gx", pairing("gx", 1, True))
    beside_a = lax.ppermute(to_a, "gx", pairing("gx", 0, True))

    wave_out, token = call(
        functools.partial(outer_kernel, outer, inner),
        "outer",
        (wave_type, token_type),
        [VMEM] * 9,
        (HBM, VMEM),
        [
            pltpu.VMEM(spectrum.shape, BF16),
            *wave_scratch(outer),
            DMA((sum(map(len, outer)) + 3 * sum(map(len, inner)),)),
        ],
        2 * 10**9,
        5 * MIB,
        20,
    )(
        spectrum, f_oth, courant, courant_oth, sea_mask, inter, sides_own, sides_oth, wave
    )
    currents_out = call(
        momentum_kernel,
        "momentum",
        jax.ShapeDtypeStruct(currents.shape, F32),
        [VMEM] * 10 + [SMEM],
        HBM,
        [
            pltpu.VMEM((cells_x + 2 * SUBSTEPS, fields, 2 * cells_y), F32),
            pltpu.VMEM((cells_x + 2 * SUBSTEPS, chans, 2 * cells_y), F32),
            pltpu.VMEM((cells_x + 2 * SUBSTEPS - 2, chans, 2 * cells_y), F32),
            pltpu.VMEM(currents.shape, F32),
            DMA((cells_x // TILE, 4)),
        ],
        10**8,
        4 * MIB,
        10,
    )(
        s_main, s_aux, state, west_own, east_own, from_a, from_b, beside_b, beside_a, token,
        level_drag,
    )
    return (wave_out, currents_out)


def solution(mesh):
    in_specs = (
        P("gx", "gy", "comp"),
        P("gx", "gy"),
        P(None, "comp"),
        P(),
        P(),
        P(None, "comp", "gx", "gy"),
        P("comp"),
    )
    out_specs = (P("gx", "gy", "comp"), P(None, "comp", "gx", "gy"))
    return jax.shard_map(local, mesh=mesh, in_specs=in_specs, out_specs=out_specs, check_vma=False)
```

```python
import functools

import jax
import jax.numpy as jnp
from jax import lax
from jax.experimental import pallas as pl
from jax.experimental.pallas import tpu as pltpu
from jax.sharding import PartitionSpec as P

SUBSTEPS = 3

time_step = 0.5
viscosity = 0.4

F32 = jnp.float32
BF16 = jnp.bfloat16
MIB = 1 << 20
EDGE = 3
MASK_ROWS = 16
SLOT = 8
CHUNK = 128
TILE_ROWS = 16
EARLY_PAIRS = 3
SEAM_GROUP = 1
TILE = 8
PARTS = 5


def ring(axis):
    count = lax.axis_size(axis)
    forward = [(i, (i + 1) % count) for i in range(count)]
    return forward, [(target, source) for source, target in forward]


def pairing(axis, first, periodic=False):
    count = lax.axis_size(axis)
    swaps = [(i, (i + 1) % count) for i in range(first, count if periodic else count - 1, 2)]
    return swaps + [(target, source) for source, target in swaps]


def lane_of(rows, width):
    return lax.broadcasted_iota(jnp.int32, (rows, width), 1)


def between(lane, low, high):
    return (lane >= low) & (lane < high)


def chunks_of(bins):
    return [slice(j * CHUNK, (j + 1) * CHUNK) for j in range(bins // CHUNK)]


def sea_row(mask, x, rows):
    return jnp.broadcast_to(mask[x : x + 1, :].astype(F32), (rows, mask.shape[1]))


def outgoing_kernel(
    spectrum, currents, mask_in, proj_in,
    msg_e, msg_w, proj,
    cur, mask, sem, row_sem,
):
    cells_x, width, bins = spectrum.shape
    levels = cur.shape[1]
    chans = 2 * levels
    fields = chans + MASK_ROWS
    copies = [
        pltpu.make_async_copy(currents, cur, sem.at[0]),
        pltpu.make_async_copy(mask_in, mask, sem.at[1]),
    ]
    proj_copy = pltpu.make_async_copy(proj_in, proj, sem.at[2])
    for side, (msg, x) in enumerate(((msg_e, cells_x - 1), (msg_w, 0))):
        for j, cols in enumerate(chunks_of(bins)):
            copies.append(
                pltpu.make_async_copy(
                    spectrum.at[x, :, cols], msg.at[pl.ds(j * width, width), :], row_sem.at[side, j]
                )
            )
    for copy in (*copies, proj_copy):
        copy.start()
    copies[0].wait()
    copies[1].wait()
    base = bins // CHUNK * width
    for msg, first in ((msg_e, cells_x - EDGE), (msg_w, 0)):
        for i in range(EDGE):
            x = first + i
            at = base + i * fields
            for c in range(2):
                msg[at + c * levels : at + (c + 1) * levels] = cur[c, :, x, :].astype(BF16)
            msg[at + chans : at + fields] = sea_row(mask, x, MASK_ROWS).astype(BF16)
    for copy in (*copies[2:], proj_copy):
        copy.wait()


def stokes_weights(proj, courant, core, owner, weights):
    levels = proj.shape[1] // 2
    bins = courant.shape[1]
    bins_at = pl.ds(pl.multiple_of(owner * bins, bins), bins)
    cour_x, cour_y = courant[0:1, :], courant[1:2, :]
    terms = (
        1.0 - jnp.abs(cour_x) - jnp.abs(cour_y),
        jnp.maximum(cour_x, 0.0),
        -jnp.minimum(cour_x, 0.0),
        jnp.maximum(cour_y, 0.0),
        -jnp.minimum(cour_y, 0.0),
    )
    for c in range(2):
        mine = proj[c, pl.ds(pl.multiple_of(core * levels, levels), levels), bins_at].astype(F32)
        for k, term in enumerate(terms):
            row = (2 * k + c) * levels
            weights[row : row + levels] = (mine * term).astype(BF16)


def project_kernel(
    f_own, f_oth, courant_own, courant_oth, stokes_proj, currents, mask,
    s_main, s_aux, s_edge, state, msg_a, msg_b, token,
    proj, wt_own, wt_oth,
):
    cells_x, width, bins = f_own.shape
    chans = s_main.shape[1]
    fields = chans + MASK_ROWS
    core = lax.axis_index("comp")
    token[...] = jnp.zeros_like(token)
    stokes_weights(stokes_proj, courant_own, core, core, wt_own)
    stokes_weights(stokes_proj, courant_oth, core, 1 - core, wt_oth)
    contract = (((1,), (1,)), ((), ()))
    for pair in range(cells_x // 2):
        both = 0.0
        for wt, f in ((wt_own, f_own), (wt_oth, f_oth)):
            cells = f[2 * pair : 2 * pair + 2].reshape(2 * width, bins)
            both += lax.dot_general(wt[...], cells, contract, preferred_element_type=F32)
        proj[2 * pair] = both[:, :width]
        proj[2 * pair + 1] = both[:, width:]
    lane = lane_of(chans, width)
    lane_f = lane_of(fields, width)

    def part(x, which):
        return proj[x, which * chans : (which + 1) * chans, :]

    pack_n = pack_s = jnp.zeros((chans, width), F32)
    cur_n = cur_s = jnp.zeros((fields, width), F32)
    for x in range(-1, cells_x + 1):
        start = stokes_lane(x)
        main = jnp.zeros((chans, width), F32)
        aux = jnp.zeros((chans, width), F32)
        if 0 <= x < cells_x:
            south = pltpu.roll(part(x, 3), 1, 1)
            north = pltpu.roll(part(x, 4), width - 1, 1)
            main = part(x, 0) + jnp.where(lane > 0, south, 0.0) + jnp.where(lane < width - 1, north, 0.0)
            aux = jnp.where(lane == 0, south, jnp.where(lane == width - 1, north, 0.0))
            s_aux[x] = aux
        if x >= 1:
            main += part(x - 1, 1)
        if x <= cells_x - 2:
            main += part(x + 1, 2)
        s_main[x + 1] = main
        if x < EDGE - 1 or x > cells_x - EDGE:
            at = x + 1 if x < EDGE - 1 else x - (cells_x - 2) + EDGE
            s_edge[at, :, :width] = main
            s_edge[at, :, width:] = aux
        window = between(lane, start, start + 4)
        ring_n = pltpu.roll(jnp.where(lane == 0, aux, main), (3 + start) % width, 1)
        ring_s = pltpu.roll(jnp.where(lane == width - 1, aux, main), (1 + start) % width, 1)
        pack_n = jnp.where(window, ring_n, pack_n)
        pack_s = jnp.where(window, ring_s, pack_s)
        if 0 <= x < cells_x:
            row = jnp.concatenate(
                [currents[0, :, x, :], currents[1, :, x, :], sea_row(mask, x, MASK_ROWS)], 0
            )
            state[x] = row
            start = current_lane(x, cells_x)
            window = between(lane_f, start, start + 3)
            cur_n = jnp.where(window, pltpu.roll(row, (3 + start) % width, 1), cur_n)
            cur_s = jnp.where(window, pltpu.roll(row, start, 1), cur_s)
    even = is_even("gy")
    for msg, north_first in ((msg_a, even), (msg_b, ~even)):
        pack, cur_pack = jnp.where(north_first, pack_n, pack_s), jnp.where(north_first, cur_n, cur_s)
        msg[:chans] = (pack + cur_pack[:chans]).astype(BF16)
        msg[chans:fields] = cur_pack[chans:].astype(BF16)
    for j, cols in enumerate(chunks_of(bins)):
        high = [f_own[x, width - 16 :, cols].astype(F32)[15:] for x in range(cells_x)]
        low = [f_own[x, :16, cols].astype(F32)[:1] for x in range(cells_x)]
        high, low = jnp.concatenate(high, 0), jnp.concatenate(low, 0)
        base = fields + j * cells_x
        msg_a[base : base + cells_x] = jnp.where(even, high, low).astype(BF16)
        msg_b[base : base + cells_x] = jnp.where(even, low, high).astype(BF16)


def is_even(axis):
    return lax.rem(lax.axis_index(axis), 2) == 0


def from_sides(from_a, from_b, rows, axis="gy"):
    even = is_even(axis)
    a, b = from_a[rows].astype(F32), from_b[rows].astype(F32)
    return jnp.where(even, b, a), jnp.where(even, a, b)


def stokes_lane(x):
    return 4 * (x + 1)


def current_lane(x, cells_x):
    return 4 * (cells_x + 2) + 3 * x


def current_halo(tile_s, tile_n, x, cells_x, lane, width):
    start = current_lane(x, cells_x)
    low = pltpu.roll(tile_s, (-start - 3) % width, 1)
    return halo_lanes(lane, low, pltpu.roll(tile_n, (-start) % width, 1), width)


def southern(tile, start, width):
    return pltpu.roll(tile, (-start - 3) % width, 1)


def northern(tile, start, width):
    return pltpu.roll(tile, (-start - 1) % width, 1)


def halo_lanes(lane, low, high, width):
    return jnp.where(lane >= width - 3, low, jnp.where(lane < 3, high, 0.0))


def stokes_row(main, aux, pack_s, pack_n, start, lane, width):
    low = southern(pack_s, start, width)
    high = northern(pack_n, start, width)
    main = main + jnp.where(lane == 0, low, 0.0) + jnp.where(lane == width - 1, high, 0.0)
    return main, aux + halo_lanes(lane, low, high, width)


def relay_kernel(cells_x, s_edge, from_a, from_b, side_w, side_e, token, msg_b, msg_a, spectra):
    del token
    chans, width = s_edge.shape[1], s_edge.shape[2] // 2
    fields = chans + MASK_ROWS
    rows, edges = side_w.shape[0] - EDGE * fields, from_a.shape[0] - fields
    spectra[:rows] = side_w[:rows]
    spectra[rows : 2 * rows] = side_e[:rows]
    spectra[2 * rows : 2 * rows + edges] = from_a[fields:]
    spectra[2 * rows + edges :] = from_b[fields:]
    half = width // 2
    lane = lane_of(chans, width)
    lane_f = lane_of(fields, width)
    tile_s, tile_n = from_sides(from_a, from_b, slice(0, fields))
    def build(first, first_cur, first_edge):
        pieces = []
        tile = jnp.zeros((chans, width), F32)
        cur_tile = jnp.zeros((fields, width), F32)
        for i in range(EDGE):
            edge = s_edge[first_edge + i]
            start = stokes_lane(first + i)
            main, aux = stokes_row(
                edge[:, :width], edge[:, width:], tile_s[:chans], tile_n[:chans], start, lane, width
            )
            pieces.append((slice(i * chans, (i + 1) * chans), main))
            at = SLOT * i
            tile = jnp.where(between(lane, at, at + 6), pltpu.roll(aux, at + 3, 1), tile)
            ring = current_halo(tile_s, tile_n, first_cur + i, cells_x, lane_f, width)
            at += half
            cur_tile = jnp.where(between(lane_f, at, at + 6), pltpu.roll(ring, at + 3, 1), cur_tile)
        base = EDGE * chans
        pieces.append((slice(base, base + chans), tile + cur_tile[:chans]))
        pieces.append((slice(base + chans, base + fields), cur_tile[chans:]))
        return pieces

    even = is_even("gx")
    east = build(cells_x - 2, cells_x - EDGE, EDGE)
    west = build(-1, 0, 0)
    for (rows, to_east), (_, to_west) in zip(east, west, strict=True):
        msg_a[rows] = jnp.where(even, to_east, to_west).astype(BF16)
        msg_b[rows] = jnp.where(even, to_west, to_east).astype(BF16)


def lat_coriolis(cells_y):
    ny_total = lax.axis_size("gy") * cells_y
    lane = lane_of(1, 2 * cells_y)
    lane = jnp.where(lane >= cells_y + cells_y // 2, lane - 2 * cells_y, lane)
    lat_index = lax.axis_index("gy") * cells_y + lane
    return jnp.sin(jnp.pi * ((lat_index.astype(F32) + 0.5) / ny_total - 0.5))


def momentum_kernel(
    s_main, s_aux, state, side_w, side_e, from_a, from_b, beside_b, beside_a, token, drag,
    out,
    flow_a, flow_b, stokes, result, sem,
):
    del token
    cells_x, chans, width = s_aux.shape
    fields = chans + MASK_ROWS
    levels = chans // 2
    half = width // 2
    lane = lane_of(chans, width)
    lane_f = lane_of(fields, width)
    side_base = side_w.shape[0] - EDGE * fields
    corner_w, corner_e = from_sides(beside_a, beside_b, slice(EDGE * chans, None), "gx")
    sums_w, sums_e = from_sides(beside_a, beside_b, slice(0, EDGE * chans), "gx")
    tile_s, tile_n = from_sides(from_a, from_b, slice(0, fields))

    def corner(tile, at, lanes):
        ring = pltpu.roll(tile, (-at - 3) % width, 1)
        return halo_lanes(lanes, ring, ring, width)

    for x in range(-SUBSTEPS, cells_x + SUBSTEPS):
        if 0 <= x < cells_x:
            flow_a[x + SUBSTEPS, :, :width] = state[x]
            aux = current_halo(tile_s, tile_n, x, cells_x, lane_f, width)
        else:
            side, tile, i = (side_w, corner_w, x + SUBSTEPS) if x < 0 else (side_e, corner_e, x - cells_x)
            at = side_base + i * fields
            flow_a[x + SUBSTEPS, :, :width] = side[at : at + fields].astype(F32)
            aux = corner(tile, half + SLOT * i, lane_f)
        flow_a[x + SUBSTEPS, :, width:] = aux

    margin = SUBSTEPS - 1
    for x in range(-margin, cells_x + margin):
        main = aux = 0.0
        if -1 <= x <= cells_x:
            own_aux = s_aux[x] if 0 <= x < cells_x else 0.0
            main, aux = stokes_row(
                s_main[x + 1], own_aux, tile_s[:chans], tile_n[:chans], stokes_lane(x), lane, width
            )
        for message, tile, first in ((sums_w, corner_w, -2), (sums_e, corner_e, cells_x - 1)):
            i = x - first
            if 0 <= i < EDGE:
                main += message[i * chans : (i + 1) * chans]
                aux += corner(tile[:chans], SLOT * i, lane)
        sea = flow_a[x + SUBSTEPS, chans : chans + 1, :]
        stokes[x + margin, :, :width] = main * sea[:, :width]
        stokes[x + margin, :, width:] = aux * sea[:, width:]

    at_level = lax.broadcasted_iota(jnp.int32, (levels, 1), 0)
    drag_col = jnp.zeros((levels, 1), F32)
    for level in range(levels):
        drag_col = jnp.where(at_level == level, drag[level], drag_col)
    def copy_out(block):
        rows = pl.ds(block * TILE, TILE)
        return pltpu.make_async_copy(
            result.at[:, :, rows, :], out.at[:, :, rows, :], sem.at[block]
        )

    half_cor = time_step * lat_coriolis(width)
    keep = 1.0 - 4.0 * time_step * viscosity - time_step * drag_col
    ring = 2 * width
    source, target = flow_a, flow_b
    for step in range(SUBSTEPS):
        margin = SUBSTEPS - 1 - step
        last = step == SUBSTEPS - 1
        for x in range(-margin, cells_x + margin):
            at = x + SUBSTEPS
            u, v = source[at, :levels], source[at, levels:chans]
            u_w, v_w = source[at - 1, :levels], source[at - 1, levels:chans]
            u_e, v_e = source[at + 1, :levels], source[at + 1, levels:chans]
            u_s, v_s = pltpu.roll(u, 1, 1), pltpu.roll(v, 1, 1)
            u_n, v_n = pltpu.roll(u, ring - 1, 1), pltpu.roll(v, ring - 1, 1)
            drift = stokes[x + SUBSTEPS - 1]
            if last:
                u, v, u_w, v_w, u_e, v_e, u_s, v_s, u_n, v_n, drift = (
                    field[:, :width] for field in (u, v, u_w, v_w, u_e, v_e, u_s, v_s, u_n, v_n, drift)
                )
            lanes = u.shape[1]
            spin = half_cor[:, :lanes] + 0.5 * time_step * ((v_e - v_w) - (u_n - u_s))
            sea = flow_a[at, chans : chans + 1, :lanes]
            u_new = keep * u + spin * (v + drift[levels:])
            v_new = keep * v - spin * (u + drift[:levels])
            u_new = sea * (u_new + time_step * viscosity * ((u_e + u_w) + (u_n + u_s)))
            v_new = sea * (v_new + time_step * viscosity * ((v_e + v_w) + (v_n + v_s)))
            if last:
                result[0, :, x, :] = u_new
                result[1, :, x, :] = v_new
                if x % TILE == TILE - 1:
                    copy_out(x // TILE).start()
            else:
                target[at, :levels] = u_new
                target[at, levels:chans] = v_new
        source, target = target, source
    for block in range(cells_x // TILE):
        copy_out(block).wait()


def wave_groups(cells_x, width, early_pairs):
    early = 1 + 2 * early_pairs
    inner = [[(x, 0, width), (x + 1, 0, width)] for x in range(1, early, 2)]
    outer = [[(0, 0, width), (cells_x - 1, 0, width)]]
    for x in range(early, cells_x - 1, 2):
        outer.append([(i, 0, width) for i in range(x, min(x + 2, cells_x - 1))])
    return inner, outer


def rows_of(group):
    return sum(last - first for _, first, last in group)


def wave_body(
    groups, sides, seam, wave, arriving,
    f_own, f_oth, courant_own, courant_oth, mask, inter,
    slots, send,
    adv, sea, moved,
):
    cells_x, width, bins = f_own.shape
    even = is_even("gy")
    per_core = bins // CHUNK
    halves = []
    for rows, side, courant in zip((f_own, f_oth), sides, (courant_own, courant_oth), strict=True):
        for j, cols in enumerate(chunks_of(bins)):
            cour_x, cour_y = courant[0:1, cols], courant[1:2, cols]
            size_x, size_y = jnp.abs(cour_x), jnp.abs(cour_y)
            south = north = None
            if side is not None:
                base = 2 * per_core * width + j * cells_x
                edge_a = side[base : base + cells_x].astype(F32)
                base += per_core * cells_x
                edge_b = side[base : base + cells_x].astype(F32)
                south, north = jnp.where(even, edge_b, edge_a), jnp.where(even, edge_a, edge_b)
            halves.append(
                (
                    rows, side, j, cols, south, north,
                    1.0 - size_x - size_y, size_x, size_y, cour_x > 0.0, cour_y > 0.0,
                )
            )

    def cell(rows, side, j, cols, x, first, last):
        if 0 <= x < cells_x:
            return rows[x, first:last, cols].astype(F32)
        base = (0 if x < 0 else per_core * width) + j * width
        return side[base + first : base + last].astype(F32)

    def advect(at, n):
        rows, side, j, cols, south, north, c_mid, c_x, c_y, up_x, up_y = halves[n]
        row = 0
        for i, (x, first, last) in enumerate(groups[at]):
            mid = cell(rows, side, j, cols, x, first, last)
            shifted = moved.at[(len(groups[at]) * n + i) % moved.shape[0]]
            shifted[8 + first : 8 + last] = mid
            none = jnp.zeros((1, CHUNK), F32)
            shifted[7:8] = none if south is None else south[x : x + 1]
            shifted[8 + width : 9 + width] = none if north is None else north[x : x + 1]
            low, high = shifted[7 + first : 7 + last], shifted[9 + first : 9 + last]
            west = cell(rows, side, j, cols, x - 1, first, last)
            east = cell(rows, side, j, cols, x + 1, first, last)
            value = c_mid * mid + c_x * jnp.where(up_x, west, east) + c_y * jnp.where(up_y, low, high)
            height = last - first
            adv[at % 2][row : row + height, n * CHUNK : (n + 1) * CHUNK] = value.astype(BF16)
            row += height

    def advect_seam(n):
        rows, _, _, cols, south, north, c_mid, c_x, c_y, up_x, up_y = halves[n]
        around = range(seam[0] - 1, seam[-1] + 2)
        own = slice(seam[0], seam[-1] + 1)
        row = rows_of(groups[SEAM_GROUP])
        for first, edge, beside in ((0, 0, 1), (width - TILE_ROWS, TILE_ROWS - 1, TILE_ROWS - 2)):
            tiles = [rows[x, first : first + TILE_ROWS, cols].astype(F32) for x in around]
            line = jnp.concatenate([tile[edge : edge + 1] for tile in tiles], 0)
            inward = jnp.concatenate([tile[beside : beside + 1] for tile in tiles[1:-1]], 0)
            low, high = (south[own], inward) if first == 0 else (inward, north[own])
            value = (
                c_mid * line[1:-1]
                + c_x * jnp.where(up_x, line[:-2], line[2:])
                + c_y * jnp.where(up_y, low, high)
            )
            value = jnp.concatenate([value, jnp.zeros((TILE_ROWS - len(seam), CHUNK), F32)], 0)
            adv[SEAM_GROUP % 2][row : row + TILE_ROWS, n * CHUNK : (n + 1) * CHUNK] = value.astype(BF16)
            row += TILE_ROWS

    def height_of(at):
        return rows_of(groups[at]) + (2 * TILE_ROWS if seam and at == SEAM_GROUP else 0)

    def put_sea(at):
        row = 0
        for x, first, last in groups[at]:
            column = jnp.transpose(sea_row(mask, x, CHUNK))
            sea[at % 2][row : row + last - first] = column[first:last]
            row += last - first
        if seam and at == SEAM_GROUP:
            for lat in (0, width - 1):
                column = mask[seam[0] : seam[-1] + 1, lat : lat + 1].astype(F32)
                column = jnp.concatenate([column, jnp.zeros((TILE_ROWS - len(seam), 1), F32)], 0)
                sea[at % 2][row : row + TILE_ROWS] = jnp.broadcast_to(column, (TILE_ROWS, CHUNK))
                row += TILE_ROWS

    def finish(at, piece):
        done, mine = adv[at % 2], sea[at % 2]
        half, block = piece // blocks, piece % blocks
        middle = height_of(at) // 2 // TILE_ROWS * TILE_ROWS
        low, high = (0, middle) if half == 0 else (middle, height_of(at))
        cols = slice(block * bins // blocks, (block + 1) * bins // blocks)
        gain = jnp.dot(done[low:high, :], inter[:, cols], preferred_element_type=F32)
        row = 0
        for x, first, last in groups[at]:
            begin, end = max(low, row), min(high, row + last - first)
            if begin < end:
                lats = slice(first + begin - row, first + end - row)
                for c in chunks_of(bins // blocks):
                    own = slice(cols.start + c.start, cols.start + c.stop)
                    total = done[begin:end, own].astype(F32) + gain[begin - low : end - low, c]
                    slots[x, lats, own] = (total * mine[begin:end]).astype(BF16)
            row += last - first
        if seam and at == SEAM_GROUP and half == 1:
            at_row = lax.broadcasted_iota(jnp.int32, (TILE_ROWS, CHUNK), 0)
            for first, edge in ((0, 0), (width - TILE_ROWS, TILE_ROWS - 1)):
                end = row + TILE_ROWS
                for c in chunks_of(bins // blocks):
                    own = slice(cols.start + c.start, cols.start + c.stop)
                    total = done[row:end, own].astype(F32) + gain[row - low : end - low, c]
                    total *= mine[row:end]
                    for i, x in enumerate(seam):
                        tile = wave[x, first : first + TILE_ROWS, own].astype(F32)
                        tile = jnp.where(at_row == edge, total[i : i + 1], tile)
                        slots[x, first : first + TILE_ROWS, own] = tile.astype(BF16)
                row = end

    blocks = 2
    pieces = 2 * blocks
    parts = len(halves)
    for n in range(parts):
        advect(0, n)
    for copy in arriving:
        copy.wait()
    for at in range(1, len(groups) + 1):
        put_sea(at - 1)
        for piece in range(pieces):
            if at < len(groups):
                for n in range(piece * parts // pieces, (piece + 1) * parts // pieces):
                    advect(at, n)
                    if seam and at == SEAM_GROUP:
                        advect_seam(n)
            finish(at - 1, piece)
        send(at - 1)


def inner_kernel(
    groups,
    f_own, f_oth, courant_own, courant_oth, mask, interaction, token_in,
    wave, inter, token,
    adv_a, adv_b, sea_a, sea_b, moved, inter_sem,
):
    token[...] = token_in[...]
    bins = f_own.shape[2]
    core = lax.axis_index("comp")
    own_at, oth_at = pl.multiple_of(core * bins, bins), pl.multiple_of((1 - core) * bins, bins)
    inter_copies = [
        pltpu.make_async_copy(
            interaction.at[pl.ds(at, bins), pl.ds(own_at, bins)],
            inter.at[pl.ds(n * bins, bins)],
            inter_sem.at[n],
        )
        for n, at in enumerate((own_at, oth_at))
    ]
    for copy in inter_copies:
        copy.start()
    wave_body(
        groups, (None, None), (), None, inter_copies,
        f_own, f_oth, courant_own, courant_oth, mask, inter,
        wave, lambda n: None,
        (adv_a, adv_b), (sea_a, sea_b), moved,
    )


def outer_kernel(
    groups, groups_before,
    f_own, f_oth, courant_own, courant_oth, mask, inter, sides_own, sides_oth, wave,
    out, token,
    slots, adv_a, adv_b, sea_a, sea_b, moved, out_sem,
):
    token[...] = jnp.zeros_like(token)
    copies = []

    def send(source, blocks):
        for x, first, last in blocks:
            lats = pl.ds(first, last - first)
            copies.append(
                pltpu.make_async_copy(source.at[x, lats], out.at[x, lats], out_sem.at[len(copies)])
            )
            copies[-1].start()

    seam = [x for group in groups_before for x, _, _ in group]
    width = wave.shape[1]
    send(wave, [(x, TILE_ROWS, width - TILE_ROWS) for x in seam])
    rims = [(0, TILE_ROWS), (width - TILE_ROWS, width)]

    def sent(n):
        send(slots, groups[n])
        if n == SEAM_GROUP:
            send(slots, [(x, first, last) for x in seam for first, last in rims])

    wave_body(
        groups, (sides_own, sides_oth), seam, wave, (),
        f_own, f_oth, courant_own, courant_oth, mask, inter,
        slots, sent,
        (adv_a, adv_b), (sea_a, sea_b), moved,
    )
    for copy in copies:
        copy.wait()


VMEM = pl.BlockSpec(memory_space=pltpu.VMEM)
SMEM = pl.BlockSpec(memory_space=pltpu.SMEM)
HBM = pl.BlockSpec(memory_space=pltpu.HBM)
DMA = pltpu.SemaphoreType.DMA


def in_hbm(array):
    return pltpu.with_memory_space_constraint(array, pltpu.HBM)


def call(kernel, name, out_shape, in_specs, out_specs, scratch, flops, traffic, limit):
    return pl.pallas_call(
        kernel,
        out_shape=out_shape,
        in_specs=in_specs,
        out_specs=out_specs,
        scratch_shapes=scratch,
        compiler_params=pltpu.CompilerParams(vmem_limit_bytes=limit * MIB),
        cost_estimate=pl.CostEstimate(flops=flops, bytes_accessed=traffic, transcendentals=0),
        name=name,
    )


def local(spectrum, sea_mask, courant, interaction, stokes_proj, currents, level_drag):
    cells_x, cells_y, bins = spectrum.shape
    levels = currents.shape[1]
    chans = 2 * levels
    fields = chans + MASK_ROWS
    swap = [(0, 1), (1, 0)]
    east, west = ring("gx")

    def message(rows):
        return jax.ShapeDtypeStruct((rows, cells_y), BF16)

    f_oth = lax.ppermute(spectrum, "comp", swap)
    courant_oth = lax.ppermute(courant, "comp", swap)
    stokes_proj = jnp.transpose(stokes_proj, (0, 2, 1))
    token_type = jax.ShapeDtypeStruct((8, CHUNK), F32)
    side_rows = bins // CHUNK * cells_y + EDGE * fields
    to_e, to_w, stokes_proj = call(
        outgoing_kernel,
        "outgoing",
        (message(side_rows),) * 2 + (jax.ShapeDtypeStruct(stokes_proj.shape, BF16),),
        [HBM] * 4,
        (VMEM,) * 3,
        [
            pltpu.VMEM(currents.shape, F32),
            pltpu.VMEM(sea_mask.shape, jnp.int32),
            DMA((3,)),
            DMA((2, bins // CHUNK)),
        ],
        10**6,
        MIB,
        4,
    )(in_hbm(spectrum), in_hbm(currents), in_hbm(sea_mask), in_hbm(stokes_proj))
    west_own = lax.ppermute(to_e, "gx", east)
    east_own = lax.ppermute(to_w, "gx", west)

    edge_rows = fields + bins // CHUNK * cells_x
    s_main, s_aux, s_edge, state, to_a, to_b, token = call(
        project_kernel,
        "project",
        (
            jax.ShapeDtypeStruct((cells_x + 2, chans, cells_y), F32),
            jax.ShapeDtypeStruct((cells_x, chans, cells_y), F32),
            jax.ShapeDtypeStruct((2 * EDGE, chans, 2 * cells_y), F32),
            jax.ShapeDtypeStruct((cells_x, fields, cells_y), F32),
            message(edge_rows),
            message(edge_rows),
            token_type,
        ),
        [VMEM] * 7,
        (VMEM,) * 7,
        [
            pltpu.VMEM((cells_x, PARTS * chans, cells_y), F32),
            pltpu.VMEM((PARTS * chans, bins), BF16),
            pltpu.VMEM((PARTS * chans, bins), BF16),
        ],
        3 * 10**9,
        8 * MIB,
        8,
    )(
        spectrum, f_oth, courant, courant_oth, stokes_proj, currents, sea_mask
    )
    from_a = lax.ppermute(to_a, "gy", pairing("gy", 0))
    from_b = lax.ppermute(to_b, "gy", pairing("gy", 1))

    inner, outer = wave_groups(cells_x, cells_y, EARLY_PAIRS)
    wave_type = jax.ShapeDtypeStruct(spectrum.shape, BF16)

    def wave_scratch(groups):
        height = max(map(rows_of, groups)) + 2 * TILE_ROWS
        return [
            *[pltpu.VMEM((height, 2 * bins), BF16)] * 2,
            *[pltpu.VMEM((height, CHUNK), F32)] * 2,
            pltpu.VMEM((16, cells_y + 16, CHUNK), F32),
        ]

    wave, inter, token = call(
        functools.partial(inner_kernel, inner),
        "inner",
        (wave_type, jax.ShapeDtypeStruct((2 * bins, bins), BF16), token_type),
        [VMEM] * 5 + [HBM, VMEM],
        (VMEM,) * 3,
        [*wave_scratch(inner), DMA((2,))],
        2 * 10**9,
        5 * MIB,
        20,
    )(spectrum, f_oth, courant, courant_oth, sea_mask, in_hbm(interaction), token)

    to_b, to_a, sides_own = call(
        functools.partial(relay_kernel, cells_x),
        "relay",
        (message(EDGE * chans + fields),) * 2
        + (message(2 * bins // CHUNK * (cells_y + cells_x)),),
        [VMEM] * 6,
        (VMEM,) * 3,
        [],
        10**6,
        MIB,
        4,
    )(s_edge, from_a, from_b, west_own, east_own, token)
    sides_oth = lax.ppermute(sides_own, "comp", swap)
    beside_b = lax.ppermute(to_b, "gx", pairing("gx", 1, True))
    beside_a = lax.ppermute(to_a, "gx", pairing("gx", 0, True))

    wave_out, token = call(
        functools.partial(outer_kernel, outer, inner),
        "outer",
        (wave_type, token_type),
        [VMEM] * 9,
        (HBM, VMEM),
        [
            pltpu.VMEM(spectrum.shape, BF16),
            *wave_scratch(outer),
            DMA((sum(map(len, outer)) + 3 * sum(map(len, inner)),)),
        ],
        2 * 10**9,
        5 * MIB,
        20,
    )(
        spectrum, f_oth, courant, courant_oth, sea_mask, inter, sides_own, sides_oth, wave
    )
    currents_out = call(
        momentum_kernel,
        "momentum",
        jax.ShapeDtypeStruct(currents.shape, F32),
        [VMEM] * 10 + [SMEM],
        HBM,
        [
            pltpu.VMEM((cells_x + 2 * SUBSTEPS, fields, 2 * cells_y), F32),
            pltpu.VMEM((cells_x + 2 * SUBSTEPS, chans, 2 * cells_y), F32),
            pltpu.VMEM((cells_x + 2 * SUBSTEPS - 2, chans, 2 * cells_y), F32),
            pltpu.VMEM(currents.shape, F32),
            DMA((cells_x // TILE,)),
        ],
        10**8,
        4 * MIB,
        10,
    )(
        s_main, s_aux, state, west_own, east_own, from_a, from_b, beside_b, beside_a, token,
        level_drag,
    )
    return (wave_out, currents_out)


def solution(mesh):
    in_specs = (
        P("gx", "gy", "comp"),
        P("gx", "gy"),
        P(None, "comp"),
        P(),
        P(),
        P(None, "comp", "gx", "gy"),
        P("comp"),
    )
    out_specs = (P("gx", "gy", "comp"), P(None, "comp", "gx", "gy"))
    return jax.shard_map(local, mesh=mesh, in_specs=in_specs, out_specs=out_specs, check_vma=False)
```
